128 devices in a mesh: fsdp: 16 (over z_lo, y, core), ctx: 8 (over z_hi, x).
Axes of the slice: x: 4, y: 4, z: 4 (z_hi: 2, z_lo: 2; z = z_hi * 2 + z_lo), core: 2. Of those that a mesh axis runs over, the one named last changes fastest.
Arguments:
- inputs: bfloat16 [16, 1536, 1024], P('fsdp', 'ctx'), may hold values from -6 to 6
- doc_ids: int32 [16, 1536], P('fsdp', 'ctx'), may hold values from 0 to 2, never falling along the last dimension, each value on 1 to 1152 neighbouring positions
- query_proj: bfloat16 [1024, 2048], P('fsdp'), may hold values from -0.1875 to 0.1875
- key_projection: bfloat16 [1024, 1024], P('fsdp'), may hold values from -0.1875 to 0.1875
- value_projection: bfloat16 [1024, 1024], P('fsdp'), may hold values from -0.1875 to 0.1875
- output_proj: bfloat16 [2048, 1024], P('fsdp'), may hold values from -1 to 1
- gate_proj: bfloat16 [1024, 3072], P('fsdp'), may hold values from -0.1875 to 0.1875
- up_proj: bfloat16 [1024, 3072], P('fsdp'), may hold values from -0.1875 to 0.1875
- down_proj: bfloat16 [3072, 1024], P('fsdp'), may hold values from -0.109375 to 0.109375
- attn_gain: bfloat16 [1024], P('fsdp'), may hold values from 0.25 to 1.75
- mlp_gain: bfloat16 [1024], P('fsdp'), may hold values from 0.25 to 1.75
- query_norm_gain: bfloat16 [128], P('fsdp'), may hold values from 0.25 to 1.75
- key_gain: bfloat16 [128], P('fsdp'), may hold values from 0.25 to 1.75
- out_grad: bfloat16 [16, 1536, 1024], P('fsdp', 'ctx'), may hold values from -6 to 6
Outputs:
- outputs: bfloat16 [16, 1536, 1024], P('fsdp', 'ctx')
- input_grad: float32 [16, 1536, 1024], P('fsdp', 'ctx')
- query_proj_grad: float32 [1024, 2048], P('fsdp')
- key_proj_grad: float32 [1024, 1024], P('fsdp')
- value_proj_grad: float32 [1024, 1024], P('fsdp')
- output_proj_grad: float32 [2048, 1024], P('fsdp')
- gate_proj_grad: float32 [1024, 3072], P('fsdp')
- up_proj_grad: float32 [1024, 3072], P('fsdp')
- down_proj_grad: float32 [3072, 1024], P('fsdp')
- attn_gain_grad: float32 [1024], P('fsdp')
- mlp_gain_grad: float32 [1024], P('fsdp')
- query_gain_grad: float32 [128], P('fsdp')
- key_gain_grad: float32 [128], P('fsdp')
The draws below stay inside these ranges and needn't reach their ends.
Inputs may be any that keep to these rules, and one draw needn't show every extreme that they name: Each row of doc_ids numbers its documents 0 to 2 in order, never falling; each document has 1 to 1152 tokens, and one has exactly 1152.
All inputs are finite; a program needn't handle non-finite values.
Results may differ from the reference program's by a relative error of at most 0.025.
Values may be sent and summed in bfloat16 or wider, within the bound.
A program may use at most 192 MiB of HBM per device.

```python
import math
import jax
import jax.numpy as jnp
import numpy as np
from jax import lax

MODEL_WIDTH = 1024
QUERY_HEADS = 16
KEY_VALUE_HEADS = 8
HEAD_SIZE = 128
FF = 3072
DOCS = 3
LEN = 1536
SEQS = 16
MOST = 1152


def shard_levels(key, dims, shards, smallest, largest):
    level, own = 1.0, jax.random.fold_in(key, 6)
    for position, shards_of in shards:
        heights = jnp.exp(jax.random.uniform(jax.random.fold_in(own, position), (shards_of,), jnp.float32, smallest / len(shards), largest / len(shards)))
        level = level * jnp.repeat(heights, dims[position] // shards_of).reshape([-1 if axis == position else 1 for axis in range(len(dims))])
    return level


def profile(number_of, total, bound, lean):
    weights = [(1 << 20) // math.isqrt(standing ** lean) + 1 for standing in range(2, number_of + 1)]
    surplus, counts = total - bound - (number_of - 1), [1] * (number_of - 1)
    while surplus > 0:
        candidates = [i for i in range(number_of - 1) if counts[i] < bound]
        whole, remaining = sum([weights[i] for i in candidates]), surplus
        for i in candidates:
            extra = min(bound - counts[i], max(1, remaining * weights[i] // whole), surplus)
            counts[i] = counts[i] + extra
            surplus = surplus - extra
    return np.array([bound] + counts)


def uneven_parts(key, count, total, bound, slope):
    if count == 2:
        one = jax.random.randint(key, (), max(1, total - bound), min(bound, total - 1) + 1)
        return jnp.stack([one, total - one])
    sizes = jnp.asarray(profile(count, total, bound, slope), jnp.int32)
    twos = (count - 1) // 2
    donor, receiver = sizes[1:1 + 2 * twos:2], sizes[2:2 + 2 * twos:2]
    margin = jnp.minimum(donor - 1, bound - receiver)
    moved = jax.random.randint(jax.random.fold_in(key, 1), (twos,), 0, 1 << 20) % (margin + 1)
    sizes = sizes.at[1:1 + 2 * twos:2].set(donor - moved).at[2:2 + 2 * twos:2].set(receiver + moved)
    return sizes[jax.random.permutation(jax.random.fold_in(key, 2), count)]


def noise(stream_key, shape, scale, reach, split=(), held_as=jnp.bfloat16):
    loudness = shard_levels(stream_key, shape, split, -0.22, 0.18) if split else 1.0
    values = jax.random.normal(stream_key, shape, jnp.float32) * scale * loudness
    return jnp.minimum(jnp.maximum(values, -reach), reach).astype(held_as)


def setup_inputs(seed: int = 0) -> dict:
    splits = jax.random.split(jax.random.key(seed), 15)
    inputs = noise(splits[0], (SEQS, LEN, MODEL_WIDTH), 1.0, 6.0, ((0, 16), (1, 8)))
    doc_ids = jax.vmap(lambda own: jnp.searchsorted(jnp.cumsum(uneven_parts(own, DOCS, LEN, MOST, 1)), jnp.arange(LEN), side="right"))(jax.random.split(splits[1], SEQS)).reshape((SEQS, LEN)).astype(jnp.int32)
    query_proj = noise(splits[2], (MODEL_WIDTH, QUERY_HEADS * HEAD_SIZE), MODEL_WIDTH ** -0.5, 0.1875, ((0, 16),))
    key_projection = noise(splits[3], (MODEL_WIDTH, KEY_VALUE_HEADS * HEAD_SIZE), MODEL_WIDTH ** -0.5, 0.1875, ((0, 16),))
    value_projection = noise(splits[4], (MODEL_WIDTH, KEY_VALUE_HEADS * HEAD_SIZE), MODEL_WIDTH ** -0.5, 0.1875, ((0, 16),))
    output_proj = noise(splits[5], (QUERY_HEADS * HEAD_SIZE, MODEL_WIDTH), (max(1, QUERY_HEADS * HEAD_SIZE // 64)) ** -0.5, 1.0, ((0, 16),))
    gate_proj = noise(splits[6], (MODEL_WIDTH, FF), MODEL_WIDTH ** -0.5, 0.1875, ((0, 16),))
    up_proj = noise(splits[7], (MODEL_WIDTH, FF), MODEL_WIDTH ** -0.5, 0.1875, ((0, 16),))
    down_proj = noise(splits[8], (FF, MODEL_WIDTH), FF ** -0.5, 0.109375, ((0, 16),))
    attn_gain = jnp.clip(1.0 + 0.15 * jax.random.normal(splits[9], (MODEL_WIDTH,), jnp.float32), 0.25, 1.75).astype(jnp.bfloat16)
    mlp_gain = jnp.clip(1.0 + 0.15 * jax.random.normal(splits[10], (MODEL_WIDTH,), jnp.float32), 0.25, 1.75).astype(jnp.bfloat16)
    query_norm_gain = jnp.clip(1.0 + 0.15 * jax.random.normal(splits[11], (HEAD_SIZE,), jnp.float32), 0.25, 1.75).astype(jnp.bfloat16)
    key_gain = jnp.clip(1.0 + 0.15 * jax.random.normal(splits[12], (HEAD_SIZE,), jnp.float32), 0.25, 1.75).astype(jnp.bfloat16)
    out_grad = noise(splits[13], (SEQS, LEN, MODEL_WIDTH), 1.0, 6.0, ((0, 16), (1, 8)))
    return {"inputs": inputs, "doc_ids": doc_ids, "query_proj": query_proj, "key_projection": key_projection, "value_projection": value_projection, "output_proj": output_proj, "gate_proj": gate_proj, "up_proj": up_proj, "down_proj": down_proj, "attn_gain": attn_gain, "mlp_gain": mlp_gain, "query_norm_gain": query_norm_gain, "key_gain": key_gain, "out_grad": out_grad}


@jax.custom_vjp
def lower_precision(v):
    return lax.optimization_barrier(v.astype(jnp.bfloat16)).astype(jnp.float32)

@jax.custom_vjp
def lower_backward(v):
    return v

def low_keep(v):
    return (lower_precision(v), None)

def low_pass(kept, grad):
    return (grad,)

def back_keep(v):
    return (v, None)

def back_low(kept, grad):
    return (lower_precision(grad),)
lower_precision.defvjp(low_keep, low_pass)
lower_backward.defvjp(back_keep, back_low)
EPSILON = 1e-06
THETA = 1000000.0
NEGATIVE = -1e+30
TOP_PRECISION = lax.Precision.HIGHEST

def root_mean_norm(value_rows, scaling):
    return value_rows * lax.rsqrt(lax.optimization_barrier(jnp.mean(value_rows * value_rows, axis=-1, keepdims=True)) + EPSILON) * scaling

def rotate_halves(value_rows, cosine_table, sine_table):
    middle = value_rows.shape[-1] // 2
    former = value_rows[..., :middle]
    latter = value_rows[..., middle:]
    return jnp.concatenate([former * cosine_table - latter * sine_table, latter * cosine_table + former * sine_table], axis=-1)

def doc_positions(row_document_index):
    position_table = jnp.arange(row_document_index.shape[0], dtype=jnp.int32)
    numbers = jnp.arange(DOCS, dtype=jnp.int32)
    starts = lax.optimization_barrier(jnp.sum((row_document_index[:, None] < numbers[None, :]).astype(jnp.int32), axis=0))
    own_start = lax.optimization_barrier(jnp.sum(jnp.where(row_document_index[:, None] == numbers[None, :], starts[None, :], 0), axis=1))
    return (position_table - own_start).astype(jnp.int32)

def rope_tables(positions):
    freqs = THETA ** (-jnp.arange(HEAD_SIZE // 2, dtype=jnp.float32) * 2.0 / HEAD_SIZE)
    angles = positions.astype(jnp.float32)[:, None] * freqs[None, :]
    return (jnp.cos(angles)[:, None, :], jnp.sin(angles)[:, None, :])

def block_forward(inputs, row_document_index, query_proj, key_projection, value_projection, output_proj, gate_proj, up_proj, down_proj, attn_gain, mlp_gain, query_norm_gain, key_gain):
    length_total = inputs.shape[0]
    cosine_table, sine_table = rope_tables(doc_positions(row_document_index))
    position_table = jnp.arange(length_total, dtype=jnp.int32)
    factor = 1.0 / math.sqrt(HEAD_SIZE)
    normalized_rows = lower_precision(root_mean_norm(inputs, attn_gain))
    query_linear = lower_backward(jnp.dot(normalized_rows, query_proj, precision=TOP_PRECISION)).reshape(length_total, QUERY_HEADS, HEAD_SIZE)
    key_linear = lower_backward(jnp.dot(normalized_rows, key_projection, precision=TOP_PRECISION)).reshape(length_total, KEY_VALUE_HEADS, HEAD_SIZE)
    value_rows = lower_precision(lower_backward(jnp.dot(normalized_rows, value_projection, precision=TOP_PRECISION))).reshape(length_total, KEY_VALUE_HEADS, HEAD_SIZE)
    query_rows = lower_precision(rotate_halves(root_mean_norm(query_linear, query_norm_gain), cosine_table, sine_table)).reshape(length_total, KEY_VALUE_HEADS, QUERY_HEADS // KEY_VALUE_HEADS, HEAD_SIZE)
    keys = lower_precision(rotate_halves(root_mean_norm(key_linear, key_gain), cosine_table, sine_table))
    block_of_rows = 512 if length_total % 512 == 0 else length_total
    block_list = length_total // block_of_rows

    def attend_heads(block_in):
        query_block, query_places, query_ids = block_in
        scores = lower_backward(jnp.einsum('tgrd,sgd->tgrs', query_block, keys, precision=TOP_PRECISION) * factor)
        allowed = (query_ids[:, None] == row_document_index[None, :]) & (position_table[None, :] <= query_places[:, None])
        scores = jnp.where(allowed[:, None, None, :], scores, NEGATIVE)
        probs = jax.nn.softmax(scores, axis=-1)
        return jnp.einsum('tgrs,sgd->tgrd', lower_precision(probs), value_rows, precision=TOP_PRECISION)
    attended_rows = lax.map(jax.checkpoint(attend_heads), (query_rows.reshape(block_list, block_of_rows, KEY_VALUE_HEADS, QUERY_HEADS // KEY_VALUE_HEADS, HEAD_SIZE), position_table.reshape(block_list, block_of_rows), row_document_index.reshape(block_list, block_of_rows)))
    heads = lower_precision(lower_backward(attended_rows.reshape(length_total, QUERY_HEADS * HEAD_SIZE)))
    hidden = inputs + lower_backward(jnp.dot(heads, output_proj, precision=TOP_PRECISION))
    mixed = lower_precision(root_mean_norm(hidden, mlp_gain))
    gate = lower_backward(jnp.dot(mixed, gate_proj, precision=TOP_PRECISION))
    upward = lower_backward(jnp.dot(mixed, up_proj, precision=TOP_PRECISION))
    active = lower_precision(jax.nn.silu(gate) * upward)
    return hidden + lower_backward(jnp.dot(active, down_proj, precision=TOP_PRECISION))

def reference(inputs, doc_ids, query_proj, key_projection, value_projection, output_proj, gate_proj, up_proj, down_proj, attn_gain, mlp_gain, query_norm_gain, key_gain, out_grad):
    params = tuple((weight.astype(jnp.float32) for weight in (query_proj, key_projection, value_projection, output_proj, gate_proj, up_proj, down_proj, attn_gain, mlp_gain, query_norm_gain, key_gain)))

    def sequence_step(totals, sequence):
        seq_inputs, row_document_index, seq_grad = sequence

        def forward_only(seq_values, *weights):
            return block_forward(seq_values, row_document_index, *weights)
        result, pullback = jax.vjp(forward_only, seq_inputs.astype(jnp.float32), *params)
        grads = pullback(seq_grad.astype(jnp.float32))
        totals = tuple((total_grad + grad_part for total_grad, grad_part in zip(totals, grads[1:])))
        return (totals, (result.astype(jnp.bfloat16), grads[0]))
    zeros = tuple((jnp.zeros_like(weight) for weight in params))
    totals, (outputs, input_grad) = lax.scan(sequence_step, zeros, (inputs, doc_ids, out_grad))
    return (outputs, input_grad) + totals
```

```python
import functools
import math

import jax
import jax.numpy as jnp
import numpy as np
from jax import lax
from jax.experimental import pallas as pl
from jax.experimental.pallas import tpu as pltpu
from jax.sharding import PartitionSpec as P

MESH = pl.DeviceIdType.MESH
HEAD = 128
EPSILON = 1e-06
THETA = 1000000.0
BF16, F32 = jnp.bfloat16, jnp.float32
FACTOR = 1.0 / math.sqrt(HEAD)
ANY = pl.BlockSpec(memory_space=pl.ANY)
VM = pl.BlockSpec(memory_space=pltpu.VMEM)
DMA = pltpu.SemaphoreType.DMA


def fid(zl, y, k):
    return zl * 8 + y * 2 + k


class Net:
    def __init__(self):
        f, c = lax.axis_index("fsdp"), lax.axis_index("ctx")
        zl, y, k, zh, x = f // 8, (f // 2) % 4, f % 2, c // 4, c % 4
        self.zl, self.y, self.k, self.zh, self.x = zl, y, k, zh, x
        self.z = zh * 2 + zl
        self.f, self.c = f, c
        self.yp, self.ym = self.along("y", 1), self.along("y", 3)
        self.zp, self.zm = self.along("z", 1), self.along("z", 3)
        self.xp, self.xm = self.along("x", 1), self.along("x", 3)
        self.pair = (fid(1 - zl, y, k), c)
        self.sib = (fid(zl, y, 1 - k), c)
        self.peer_c = (1 - zh) * 4 + x
        self.peer = (f, self.peer_c)

    def at(self, dim):
        return {"y": self.y, "x": self.x, "z": self.z}[dim]

    def along(self, dim, off):
        there = (self.at(dim) + off) % 4
        if dim == "y":
            return (fid(self.zl, there, self.k), self.c)
        if dim == "x":
            return (self.f, self.zh * 4 + there)
        return (fid(there % 2, self.y, self.k), (there // 2) * 4 + self.x)

    def ctx(self, off):
        return (self.c + off) % 8


def barrier(devices):
    sem = pltpu.get_barrier_semaphore()
    for d in devices:
        pl.semaphore_signal(sem, inc=1, device_id=d, device_id_type=MESH)
    pl.semaphore_wait(sem, len(devices))


class Wire:
    def __init__(self, send, recv):
        self.send, self.recv, self.n, self.all = send, recv, 0, []

    def __call__(self, src, dst, device):
        i = self.n
        self.n += 1
        copy = pltpu.make_async_remote_copy(
            src_ref=src, dst_ref=dst, send_sem=self.send.at[i], recv_sem=self.recv.at[i],
            device_id=device, device_id_type=MESH)
        copy.start()
        self.all.append(copy)
        return copy

    def finish(self):
        for copy in self.all:
            copy.wait_send()


class Local:
    def __init__(self, sems):
        self.sems, self.n = sems, 0

    def __call__(self, src, dst):
        copy = pltpu.make_async_copy(src, dst, self.sems.at[self.n])
        self.n += 1
        copy.start()
        return copy


def sems(wires, local):
    return [DMA((wires,)), DMA((wires,)), DMA((local,))]


def talking(number, name, **more):
    return dict(
        compiler_params=pltpu.CompilerParams(
            collective_id=number, has_side_effects=True, vmem_limit_bytes=60 << 20),
        name=name, **more)
def quarters(rows):
    if rows % 64 == 0:
        q = rows // 4
        return (0, q, 2 * q, 3 * q, rows)
    return (0, 16, 32, 48, rows)


class WeightFlow:
    def __init__(self, net, wire, src, out, paired=False):
        self.net, self.wire, self.src, self.out = net, wire, src, out
        self.zp, self.zm = (net.pair, net.pair) if paired else (net.zp, net.zm)
        self.rows = src.shape[0]
        self.q = quarters(self.rows)
        self.c = {}

    def place(self, dz, dy, a=0, b=4):
        n = self.net
        zl = n.zl if dz == 0 else 1 - n.zl
        at = fid(zl, (n.y + dy + 4) % 4, n.k) * self.rows + self.q[a]
        return self.out.at[pl.ds(pl.multiple_of(at, 16), self.q[b] - self.q[a])]

    def own(self, a=0, b=4):
        return self.src.at[pl.ds(self.q[a], self.q[b] - self.q[a])]

    def pass_on(self, name, device, dz, dy, a=0, b=4):
        ref = self.place(dz, dy, a, b)
        self.c[name] = self.wire(ref, ref, device)

    def got(self, name):
        self.c[name].wait_recv()

    def stage(self, s):
        n, w, c = self.net, self.wire, self.c
        if s == 0:
            c["yp"] = w(self.own(), self.place(0, 0), n.yp)
            c["ym"] = w(self.own(), self.place(0, 0), n.ym)
            c["zp"] = w(self.own(0, 2), self.place(0, 0, 0, 2), self.zp)
            c["zm"] = w(self.own(2, 4), self.place(0, 0, 2, 4), self.zm)
            c["d"] = w(self.own(), self.place(0, 0), n.sib)
        elif s == 1:
            self.got("yp")
            self.pass_on("yp2", n.yp, 0, -1, 0, 2)
            self.pass_on("zp_m", self.zp, 0, -1, 0, 2)
            self.pass_on("zm_m", self.zm, 0, -1, 2, 4)
            self.pass_on("d_m", n.sib, 0, -1)
            self.got("ym")
            self.pass_on("ym2", n.ym, 0, 1, 2, 4)
            self.pass_on("zp_p", self.zp, 0, 1, 0, 2)
            self.pass_on("zm_p", self.zm, 0, 1, 2, 4)
            self.pass_on("d_p", n.sib, 0, 1)
            self.got("zp")
            self.pass_on("dz0", n.sib, 1, 0, 0, 2)
            self.got("zm")
            self.pass_on("dz1", n.sib, 1, 0, 2, 4)
        elif s == 2:
            self.got("yp2")
            self.pass_on("zp_2", self.zp, 0, 2, 0, 1)
            self.pass_on("d2a", n.sib, 0, 2, 0, 2)
            self.got("ym2")
            self.pass_on("zm_2", self.zm, 0, 2, 2, 3)
            self.pass_on("d2b", n.sib, 0, 2, 2, 4)
            self.got("zp_m")
            self.pass_on("yq", n.yp, 1, -1, 1, 2)
            self.pass_on("dzm0", n.sib, 1, -1, 0, 2)
            self.got("zm_p")
            self.pass_on("yr", n.ym, 1, 1, 3, 4)
            self.pass_on("dzp1", n.sib, 1, 1, 2, 4)
            self.got("zm_m")
            self.pass_on("dzm1", n.sib, 1, -1, 2, 4)
            self.got("zp_p")
            self.pass_on("dzp0", n.sib, 1, 1, 0, 2)
        elif s == 3:
            self.got("zp_2")
            self.got("yq")
            self.pass_on("dz20", n.sib, 1, 2, 0, 2)
            self.got("zm_2")
            self.got("yr")
            self.pass_on("dz21", n.sib, 1, 2, 2, 4)
        elif s == 4:
            for name in ("d", "d_m", "d_p", "dz0", "dz1", "d2a", "d2b", "dzm0", "dzp1", "dzm1", "dzp0", "dz20", "dz21"):
                self.got(name)


class RowFlow:
    def __init__(self, net, wire, src, out):
        self.net, self.wire, self.src, self.out = net, wire, src, out
        self.rows = src.shape[0]
        self.c = {}

    def place(self, ctx, a=0, b=2):
        lo, hi = a * self.rows // 2, b * self.rows // 2
        return self.out.at[pl.ds(pl.multiple_of(ctx * self.rows + lo, 16), hi - lo)]

    def pass_on(self, name, device, ctx, a=0, b=2):
        ref = self.place(ctx, a, b)
        self.c[name] = self.wire(ref, ref, device)

    def got(self, name):
        self.c[name].wait_recv()

    def stage(self, s):
        n, w, c = self.net, self.wire, self.c
        left, right = n.zh * 4 + (n.x + 3) % 4, n.zh * 4 + (n.x + 1) % 4
        left2, right2 = (1 - n.zh) * 4 + (n.x + 3) % 4, (1 - n.zh) * 4 + (n.x + 1) % 4
        if s == 0:
            c["pz"] = w(self.src, self.place(n.c), n.peer)
            c["xp"] = w(self.src, self.place(n.c), n.xp)
            c["xm"] = w(self.src, self.place(n.c), n.xm)
        elif s == 1:
            self.got("pz")
            self.pass_on("px", n.xp, n.peer_c)
            self.pass_on("pxm", n.xm, n.peer_c)
            self.got("xp")
            self.pass_on("xp2", n.xp, left, 0, 1)
            self.got("xm")
            self.pass_on("xm2", n.xm, right, 1, 2)
        elif s == 2:
            self.got("px")
            self.pass_on("px2", n.xp, left2, 0, 1)
            self.got("pxm")
            self.pass_on("pxm2", n.xm, right2, 1, 2)
        elif s == 3:
            for name in ("xp2", "xm2", "px2", "pxm2"):
                self.got(name)


def gather_kernel(nw, *refs):
    srcs, rows = refs[:nw], refs[nw]
    outs, rows_out = refs[nw + 1:2 * nw + 1], refs[2 * nw + 1]
    send, recv, local = refs[2 * nw + 2:]
    net, wire, here = Net(), Wire(send, recv), Local(local)
    barrier([net.yp, net.ym, net.zp, net.zm, net.sib, net.xp, net.xm, net.peer])
    flows = [WeightFlow(net, wire, s, o, i == 0) for i, (s, o) in enumerate(zip(srcs, outs))]
    seq = RowFlow(net, wire, rows, rows_out)
    flows[0].stage(0)
    seq.stage(0)
    flows[1].stage(0)
    kept = [here(fl.src, fl.place(0, 0)) for fl in flows]
    kept.append(here(rows, seq.place(net.c)))
    flows[0].stage(1)
    flows[2].stage(0)
    seq.stage(1)
    flows[0].stage(2)
    flows[1].stage(1)
    seq.stage(2)
    flows[0].stage(3)
    flows[0].stage(4)
    for s in range(2, nw + 3):
        if s + 1 < nw:
            flows[s + 1].stage(0)
        if s < nw:
            flows[s].stage(1)
        if s == 2:
            seq.stage(3)
        if s - 1 < nw:
            flows[s - 1].stage(2)
        if 1 <= s - 2 < nw:
            flows[s - 2].stage(3)
            flows[s - 2].stage(4)
    for h in kept:
        h.wait()
    wire.finish()


def gather(weights, rows):
    nw = len(weights)
    outs = [jax.ShapeDtypeStruct((16 * w.shape[0], w.shape[1]), w.dtype) for w in weights]
    outs.append(jax.ShapeDtypeStruct((8 * rows.shape[0], rows.shape[1]), rows.dtype))
    res = pl.pallas_call(
        functools.partial(gather_kernel, nw),
        out_shape=outs, in_specs=[ANY] * (nw + 1), out_specs=[ANY] * len(outs),
        scratch_shapes=sems(27 * nw + 9, nw + 1), **talking(0, "gather"),
    )(*weights, rows)
    return res[:nw], res[nw]


def spread_kernel(forward, src, dst, send, recv, local):
    net, wire, here = Net(), Wire(send, recv), Local(local)
    barrier([(net.f, net.ctx(o)) for o in range(1, 8)])
    rows, cols = (dst.shape[0], src.shape[1]) if forward else (src.shape[0], dst.shape[1])

    def by_row(ref, c):
        return ref.at[pl.ds(pl.multiple_of(c * rows, 16), rows)]

    def by_col(ref, c):
        return ref.at[:, pl.ds(pl.multiple_of(c * cols, 128), cols)]

    pick, put = (by_row, by_col) if forward else (by_col, by_row)
    copies = []
    for o in (4, 6, 2, 5, 7, 1, 3):
        there = net.ctx(o)
        copies.append(wire(pick(src, there), put(dst, net.c), (net.f, there)))
    own = here(pick(src, net.c), put(dst, net.c))
    for copy in copies:
        copy.wait_recv()
    own.wait()
    wire.finish()


def spread(forward, src, number):
    a, b = src.shape
    shape = (a // 8, b * 8) if forward else (a * 8, b // 8)
    return pl.pallas_call(
        functools.partial(spread_kernel, forward),
        out_shape=jax.ShapeDtypeStruct(shape, src.dtype), in_specs=[ANY], out_specs=ANY,
        scratch_shapes=sems(7, 1), **talking(number, "spread%d" % number),
    )(src)
def block(i, size):
    return pl.ds(pl.multiple_of(i * size, size), size)


def dot_t(left, right):
    return lax.dot_general(left, right, (((1,), (1,)), ((), ())), preferred_element_type=F32)


def t_dot(left, right):
    return lax.dot_general(left, right, (((0,), (0,)), ((), ())), preferred_element_type=F32)


def plain_dot(left, right):
    return jnp.dot(left, right, preferred_element_type=F32)


def unit(v):
    r = lax.rsqrt(jnp.mean(v * v, axis=-1, keepdims=True) + EPSILON)
    return v * r, r


ROWS = 256


def attn_forward(x, t, cos_in, sin_in, w, gains, q, k, v, lin, cs, sn, start, hf, heads, inv):
    length, width = x.shape[0], x.shape[1] - HEAD
    per = t.shape[0] // 16
    depth = per - 16
    total = jnp.zeros((16, t.shape[1]), F32)
    for f in range(16):
        w[f * depth:(f + 1) * depth, :] = t[f * per:f * per + depth, :]
        total = total + t[f * per + depth:(f + 1) * per, :].astype(F32)
    gains[...] = total
    attn_gain = jnp.concatenate([total[0:1], total[1:2]], axis=1)
    query_gain, key_gain = total[4:5, 0:HEAD], total[4:5, HEAD:2 * HEAD]

    def count(i, carry):
        doc = x[block(i, ROWS), width:].astype(F32)
        return (carry[0] + jnp.sum((doc < 0.5).astype(F32), axis=0, keepdims=True),
                carry[1] + jnp.sum((doc < 1.5).astype(F32), axis=0, keepdims=True))

    zero = jnp.zeros((1, HEAD), F32)
    first, second = lax.fori_loop(0, length // ROWS, count, (zero, zero))
    lanes = lax.broadcasted_iota(jnp.int32, (1, HEAD), 1) % (HEAD // 2)
    freqs = jnp.exp(lanes.astype(F32) * (-2.0 * math.log(THETA) / HEAD))
    c1, s1 = jnp.cos(first * freqs), jnp.sin(first * freqs)
    c2, s2 = jnp.cos(second * freqs), jnp.sin(second * freqs)
    sign = jnp.where(lax.broadcasted_iota(jnp.int32, (1, HEAD), 1) < HEAD // 2, -1.0, 1.0)

    def prepare(i, carry):
        rows = block(i, ROWS)
        doc = x[rows, width:].astype(F32)
        start[rows, :] = jnp.where(doc < 0.5, 0.0, jnp.where(doc < 1.5, first, second))
        cd = jnp.where(doc < 0.5, 1.0, jnp.where(doc < 1.5, c1, c2))
        sd = jnp.where(doc < 0.5, 0.0, jnp.where(doc < 1.5, s1, s2))
        ci, si = cos_in[rows, :], sin_in[rows, :]
        cosine = ci * cd + si * sd
        sine = (si * cd - ci * sd) * sign
        cs[rows, :] = cosine
        sn[rows, :] = sine
        normed = (unit(x[rows, :width].astype(F32))[0] * attn_gain).astype(BF16)
        out = plain_dot(normed, w[...])
        lin[rows, :] = out[:, :3 * HEAD]
        v[rows, :] = out[:, 3 * HEAD:].astype(BF16)
        for h in range(3):
            e = unit(out[:, h * HEAD:(h + 1) * HEAD])[0] * (query_gain if h < 2 else key_gain)
            e = (e * cosine + pltpu.roll(e, HEAD // 2, 1) * sine).astype(BF16)
            if h < 2:
                q[h, rows, :] = e
            else:
                k[rows, :] = e
        return carry

    lax.fori_loop(0, length // ROWS, prepare, 0)

    def queries(i, carry):
        rows = block(i, ROWS)
        here = q[:, rows, :].reshape(2 * ROWS, HEAD)
        begin = start[rows, :]

        def keys(j, state):
            acc, norm = state
            these = block(j, ROWS)
            p = jnp.exp(dot_t(here, k[these, :]) * FACTOR)
            p = jnp.where(allowed_at(i, j, begin), p.reshape(2, ROWS, ROWS), 0.0).reshape(2 * ROWS, ROWS)
            norm = norm + p[:, :HEAD] + p[:, HEAD:]
            return acc + plain_dot(p.astype(BF16), v[these, :]), norm

        zeros = jnp.zeros((2 * ROWS, HEAD), F32)
        acc, norm = lax.fori_loop(0, i + 1, keys, (zeros, zeros))
        over = jnp.broadcast_to(1.0 / jnp.sum(norm, axis=1, keepdims=True), (2 * ROWS, HEAD))
        acc = acc * over
        inv[:, rows, :] = over.reshape(2, ROWS, HEAD)
        for h in range(2):
            part = acc[h * ROWS:(h + 1) * ROWS]
            hf[rows, h * HEAD:(h + 1) * HEAD] = part
            heads[rows, h * HEAD:(h + 1) * HEAD] = part.astype(BF16)
        return carry

    lax.fori_loop(0, length // ROWS, queries, 0)


def allowed_at(i, j, begin):
    own = lax.broadcasted_iota(jnp.int32, (ROWS, ROWS), 0) + i * ROWS
    other = lax.broadcasted_iota(jnp.int32, (ROWS, ROWS), 1) + j * ROWS
    begin = jnp.concatenate([begin, begin], axis=1)
    return ((other.astype(F32) >= begin) & (other <= own))[None]


def attn_backward(x, w, gains, q, k, v, lin, cs, sn, start, hf, inv, dh, dw, dn, dg, dq, dk, dv, delta, dlin):
    length, width = x.shape[0], x.shape[1] - HEAD
    blocks = length // ROWS
    g = gains[...]
    attn_gain = jnp.concatenate([g[0:1], g[1:2]], axis=1)
    query_gain, key_gain = g[4:5, 0:HEAD], g[4:5, HEAD:2 * HEAD]

    def before(i, carry):
        rows = block(i, ROWS)
        for h in range(2):
            cols = slice(h * HEAD, (h + 1) * HEAD)
            s = jnp.sum(dh[rows, cols].astype(F32) * hf[rows, cols], axis=1, keepdims=True)
            delta[h, rows, :] = jnp.broadcast_to(s, (ROWS, HEAD))
            dq[h, rows, :] = jnp.zeros((ROWS, HEAD), F32)
        return carry

    lax.fori_loop(0, blocks, before, 0)

    def keys(j, carry):
        these = block(j, ROWS)
        kt, vt = k[these, :], v[these, :]

        def queries(i, state):
            d_key, d_value = state
            rows = block(i, ROWS)
            here = q[:, rows, :].reshape(2 * ROWS, HEAD)
            grad = jnp.concatenate([dh[rows, :HEAD], dh[rows, HEAD:]], axis=0)
            over = inv[:, rows, :].reshape(2 * ROWS, HEAD)
            off = delta[:, rows, :].reshape(2 * ROWS, HEAD)
            over = jnp.concatenate([over, over], axis=1)
            off = jnp.concatenate([off, off], axis=1)
            p = jnp.exp(dot_t(here, kt) * FACTOR) * over
            p = jnp.where(allowed_at(i, j, start[rows, :]), p.reshape(2, ROWS, ROWS), 0.0).reshape(2 * ROWS, ROWS)
            ds = (p * (dot_t(grad, vt) - off)).astype(BF16)
            dq[:, rows, :] = dq[:, rows, :] + plain_dot(ds, kt).reshape(2, ROWS, HEAD)
            return d_key + t_dot(ds, here), d_value + t_dot(p.astype(BF16), grad)

        zeros = jnp.zeros((ROWS, HEAD), F32)
        d_key, d_value = lax.fori_loop(j, blocks, queries, (zeros, zeros))
        dk[these, :] = d_key
        dv[these, :] = d_value
        return carry

    lax.fori_loop(0, blocks, keys, 0)

    def after(i, carry):
        d_attn, d_query, d_key = carry
        rows = block(i, ROWS)
        cosine, sine = cs[rows, :], sn[rows, :]
        for h in range(3):
            cols = slice(h * HEAD, (h + 1) * HEAD)
            d = (dq[h, rows, :] if h < 2 else dk[rows, :]) * FACTOR
            d = d * cosine - pltpu.roll(d, HEAD // 2, 1) * sine
            e, r = unit(lin[rows, cols])
            s = jnp.sum(d * e, axis=0, keepdims=True)
            d_query, d_key = (d_query + s, d_key) if h < 2 else (d_query, d_key + s)
            d = d * (query_gain if h < 2 else key_gain)
            d = r * (d - e * jnp.mean(d * e, axis=-1, keepdims=True))
            dlin[rows, cols] = d.astype(BF16)
        dlin[rows, 3 * HEAD:] = dv[rows, :].astype(BF16)
        part = dot_t(dlin[rows, :], w[...])
        e = unit(x[rows, :width].astype(F32))[0]
        d_attn = d_attn + jnp.sum(part * e, axis=0, keepdims=True)
        dn[rows, :] = part.astype(BF16)
        normed = (e * attn_gain).astype(BF16)

        part = t_dot(normed, dlin[rows, :])
        dw[...] = jnp.where(i == 0, part, dw[...] + part)
        return d_attn, d_query, d_key

    zero = jnp.zeros((1, HEAD), F32)
    dw[...] = jnp.zeros_like(dw)
    d_attn, d_query, d_key = lax.fori_loop(0, blocks, after, (jnp.zeros((1, width), F32), zero, zero))
    dg[0:1, :] = d_attn
    dg[1:2, :] = jnp.concatenate([d_query, d_key, jnp.zeros((1, width - 2 * HEAD), F32)], axis=1)


def shapes(*items):
    return [jax.ShapeDtypeStruct(s, d) for s, d in items]


def attend(x, t, cos_in, sin_in):
    length = x.shape[0]
    out = shapes(
        ((16 * (t.shape[0] // 16 - 16), t.shape[1]), BF16), ((16, t.shape[1]), F32),
        ((2, length, HEAD), BF16), ((length, HEAD), BF16), ((length, HEAD), BF16), ((length, 3 * HEAD), F32),
        ((length, HEAD), F32), ((length, HEAD), F32), ((length, HEAD), F32), ((length, 2 * HEAD), F32),
        ((length, 2 * HEAD), BF16), ((2, length, HEAD), F32))
    return pl.pallas_call(
        attn_forward, out_shape=out, in_specs=[VM] * 4, out_specs=[VM] * len(out),
        compiler_params=pltpu.CompilerParams(vmem_limit_bytes=56 << 20), name="attend")(x, t, cos_in, sin_in)


def attend_back(x, kept, dh):
    w, gains, q, k, v, lin, cs, sn, start, hf, _, inv = kept
    length, width = x.shape[0], x.shape[1] - HEAD
    out = shapes((w.shape, F32), ((length, width), BF16), ((8, width), F32))
    args = (x, w, gains, q, k, v, lin, cs, sn, start, hf, inv, dh)
    return pl.pallas_call(
        attn_backward, out_shape=out, in_specs=[VM] * len(args), out_specs=[VM] * len(out),
        scratch_shapes=[
            pltpu.VMEM((2, length, HEAD), F32), pltpu.VMEM((length, HEAD), F32), pltpu.VMEM((length, HEAD), F32),
            pltpu.VMEM((2, length, HEAD), F32), pltpu.VMEM((length, 4 * HEAD), BF16)],
        compiler_params=pltpu.CompilerParams(vmem_limit_bytes=60 << 20), name="attend_back")(*args)
def add_rows(out, parts, rows, step):
    def some(r, carry):
        here = pl.ds(pl.multiple_of(r * step, 16), step)
        total = parts[0](here).astype(F32)
        for part in parts[1:]:
            total = total + part(here).astype(F32)
        out(here, total.astype(BF16))
        return carry

    lax.fori_loop(0, rows // step, some, 0)


class SumFlow:
    def __init__(self, net, wire, here, src, first, order, mine, other, got, part, fin, out):
        self.net, self.wire, self.here, self.src, self.first, self.order = net, wire, here, src, first, order
        self.mine, self.other, self.got, self.part, self.fin, self.out = mine, other, got, part, fin, out
        self.rows, self.cols = mine.shape[2], mine.shape[3]
        self.w = self.cols // 8
        self.far = {}

    def cut(self, ref, dim, d, k=None):
        tail = ref.shape[-1]
        a = (slice(None), slice(None))
        cols = pl.ds(0, tail)
        if dim == "y":
            a = (slice(None), pl.ds(d, 1))
        elif dim == "x":
            cols = pl.ds(pl.multiple_of(d * (tail // 4), 128), tail // 4)
        else:
            a = (pl.ds(d % 2, 1), slice(None))
            cols = pl.ds(pl.multiple_of((d // 2) * (tail // 2), 128), tail // 2)
        if k is None:
            return ref.at[a[0], a[1], :, cols]
        return ref.at[a[0], a[1], k, pl.ds(self.first, self.rows), cols]

    def begin(self):
        n, dim = self.net, self.order[0]
        self.near, self.own = {}, {}
        for o in (2, 1, 3, 0):
            d = (n.at(dim) + o) % 4
            self.near[o] = self.wire(self.cut(self.src, dim, d, 1 - n.k), self.cut(self.other, dim, d), n.sib)
            self.own[o] = self.here(self.cut(self.src, dim, d, n.k), self.cut(self.mine, dim, d))

    def add(self, out, parts):
        a, b = out.shape[0], out.shape[1]
        step = 16
        for i in range(a):
            for j in range(b):
                def take(ref):
                    return lambda here: ref[i, j, here, :]

                def put(here, value):
                    out[i, j, here, :] = value
                add_rows(put, [take(p) for p in parts], self.rows, step)

    def chip(self, o):
        n, dim = self.net, self.order[0]
        d = (n.at(dim) + o) % 4
        self.near[o].wait_recv()
        self.own[o].wait()
        piece = self.cut(self.mine, dim, d)
        self.add(piece, [piece, self.cut(self.other, dim, d)])
        if o:
            self.far[o] = self.wire(piece, self.got[0].at[o - 1], n.along(dim, o))

    def phase(self, p):
        n, dim = self.net, self.order[p]
        held = self.mine if p == 0 else self.part[p - 1]
        for o in (1, 3, 2):
            self.far[o].wait_recv()
        result = self.part[p] if p < 2 else self.fin
        self.add(result, [self.cut(held, dim, n.at(dim))] + [self.got[p].at[o - 1] for o in (1, 2, 3)])
        if p < 2:
            after = self.order[p + 1]
            for o in (2, 1, 3):
                d = (n.at(after) + o) % 4
                self.far[o] = self.wire(self.cut(result, after, d), self.got[p + 1].at[o - 1], n.along(after, o))
        else:
            s = n.c if self.order == "zyx" else n.x * 2 + n.zh
            to = self.out.at[pl.ds(self.first, self.rows), pl.ds(pl.multiple_of(s * self.w, 128), self.w)]
            fin = self.fin.at[0, 0]
            self.last = [self.wire(fin, to, (n.f, n.ctx(o))) for o in (4, 6, 2, 5, 7, 1, 3)]
            self.kept = self.here(fin, to)

    def end(self):
        for copy in self.last:
            copy.wait_recv()
        self.kept.wait()


def sum_shapes(rows, cols, order):
    shape, out = [2, 4, rows, cols], []
    for dim in order:
        if dim == "y":
            shape[1] = 1
        elif dim == "x":
            shape[3] //= 4
        else:
            shape[0], shape[3] = 1, shape[3] // 2
        out.append(tuple(shape))
    return out


PLAN = ((0, 0, 64, "yxz"), (1, 0, 64, "xzy"), (2, 0, 192, "zyx"),
        (3, 0, 48, "yxz"), (3, 48, 48, "xzy"), (3, 96, 32, "zyx"))


def everyone(net):
    return ([net.sib] + [net.along(d, o) for d in "yxz" for o in (1, 2, 3)]
            + [(net.f, (1 - net.zh) * 4 + (net.x + o) % 4) for o in (1, 2, 3)])


def sum_scratch(plan, shapes_in):
    held = []
    for which, first, rows, order in plan:
        cols = shapes_in[which][-1]
        a, b, c = sum_shapes(rows, cols, order)
        full = (2, 4, rows, cols)
        held += [pltpu.VMEM(s, BF16) for s in (full, full, (3, *a), (3, *b), (3, *c), a, b, c)]
    return held


def make_flows(net, wire, here, plan, srcs, outs, held):
    flows = []
    for n, (which, first, rows, order) in enumerate(plan):
        mine, other, g0, g1, g2, p0, p1, fin = held[8 * n:8 * n + 8]
        flows.append(SumFlow(net, wire, here, srcs[which], first, order, mine, other, (g0, g1, g2), (p0, p1), fin, outs[which]))
    return flows


def sum_kernel(plan, count, *refs):
    srcs, outs = refs[:count], refs[count:2 * count]
    held, (send, recv, local) = refs[2 * count:-3], refs[-3:]
    net, wire, here = Net(), Wire(send, recv), Local(local)
    barrier(everyone(net))
    flows = make_flows(net, wire, here, plan, srcs, outs, held)
    for fl in flows:
        fl.begin()
    for o in (2, 1, 3, 0):
        for fl in flows:
            fl.chip(o)
    for p in range(3):
        for fl in flows:
            fl.phase(p)
    for fl in flows:
        fl.end()
    wire.finish()


def sum_all(grads, number):
    srcs = [g.reshape(2, 4, 2, g.shape[0] // 16, g.shape[1]) for g in grads]
    out = [jax.ShapeDtypeStruct((g.shape[0] // 16, g.shape[1]), BF16) for g in grads]
    wires, locals_ = 20 * len(PLAN), 5 * len(PLAN)
    return pl.pallas_call(
        functools.partial(sum_kernel, PLAN, len(grads)), out_shape=out,
        in_specs=[ANY] * len(grads), out_specs=[ANY] * len(grads),
        scratch_shapes=sum_scratch(PLAN, [g.shape for g in grads]) + sems(wires, locals_), **talking(number, "sum_all"))(*srcs)


def last_kernel(dw, dn, rows_out, dn_out, mine, other, got, fin, blocks, own, send, recv, local):
    net, wire, here = Net(), Wire(send, recv), Local(local)
    others = [(o, (net.f, net.ctx(o))) for o in (4, 6, 2, 5, 7, 1, 3)]
    cores = [(dz, dy, (fid((net.zl + dz) % 2, (net.y + dy) % 4, net.k), net.c)) for dz in (1, 0) for dy in (2, 1, 3, 0) if dz or dy]
    barrier([net.sib] + [d for _, d in others] + [d for _, _, d in cores])
    rows = own.shape[0]
    near = wire(dw.at[:, :, 1 - net.k], other, net.sib)
    kept = here(dw.at[:, :, net.k], mine)
    home = here(dn.at[pl.ds(pl.multiple_of(net.c * rows, 16), rows)], own)
    moved = [wire(dn.at[pl.ds(pl.multiple_of(net.ctx(o) * rows, 16), rows)], blocks.at[o - 1], d) for o, d in others]
    near.wait_recv()
    kept.wait()
    for a in range(2):
        for b in range(4):
            mine[a, b] = (mine[a, b].astype(F32) + other[a, b].astype(F32)).astype(BF16)
    far = [wire(mine.at[(net.zl + dz) % 2, (net.y + dy) % 4], got.at[dz * 4 + dy - 1], d) for dz, dy, d in cores]
    for copy in far:
        copy.wait_recv()
    total = mine[net.zl, net.y].astype(F32)
    for i in range(7):
        total = total + got[i].astype(F32)
    fin[...] = total.astype(BF16)
    spreads = [wire(fin, rows_out.at[net.c], d) for _, d in others]
    placed = here(fin, rows_out.at[net.c])
    for copy in moved:
        copy.wait_recv()
    home.wait()

    def some(r, carry):
        at = pl.ds(pl.multiple_of(r * 16, 16), 16)
        s = own[at, :].astype(F32)
        for i in range(7):
            s = s + blocks[i, at, :].astype(F32)
        dn_out[at, :] = s
        return carry

    lax.fori_loop(0, rows // 16, some, 0)
    for copy in spreads:
        copy.wait_recv()
    placed.wait()
    wire.finish()


def last_sums(dw, dn, number):
    rows, width = dn.shape[0] // 8, dn.shape[1]
    a, b = dw.shape[-2:]
    return pl.pallas_call(
        last_kernel, out_shape=shapes(((8, a, b), BF16), ((rows, width), F32)),
        in_specs=[ANY, ANY], out_specs=[ANY, VM],
        scratch_shapes=[
            pltpu.VMEM((2, 4, a, b), BF16), pltpu.VMEM((2, 4, a, b), BF16), pltpu.VMEM((7, a, b), BF16), pltpu.VMEM((a, b), BF16),
            pltpu.VMEM((7, rows, width), BF16), pltpu.VMEM((rows, width), BF16)] + sems(22, 3), **talking(number, "last_sums"))(dw, dn)
def root_mean_norm(rows, scaling):
    return rows * lax.rsqrt(jnp.mean(rows * rows, axis=-1, keepdims=True) + EPSILON) * scaling


def silu_product(gate, upward):
    return jax.nn.silu(gate) * upward


def mlp(residual, heads, grad_rows, full_output, full_gate, full_up, full_down, mlp_scale):
    hidden = residual + plain_dot(heads, full_output)
    mixed_f, mix_pull = jax.vjp(root_mean_norm, hidden, mlp_scale)
    mixed = mixed_f.astype(BF16)
    gate, upward = plain_dot(mixed, full_gate), plain_dot(mixed, full_up)
    active_f, active_pull = jax.vjp(silu_product, gate, upward)
    active = active_f.astype(BF16)
    outputs = (hidden + plain_dot(active, full_down)).astype(BF16)
    d_down = t_dot(active, grad_rows)
    d_gate, d_upward = active_pull(dot_t(grad_rows, full_down))
    gate_low, up_low = d_gate.astype(BF16), d_upward.astype(BF16)
    d_gate_w, d_up_w = t_dot(mixed, gate_low), t_dot(mixed, up_low)
    d_mixed = dot_t(gate_low, full_gate) + dot_t(up_low, full_up)
    d_hidden_norm, d_mlp_scale = mix_pull(d_mixed)
    d_hidden = grad_rows.astype(F32) + d_hidden_norm
    hidden_low = d_hidden.astype(BF16)
    d_output = t_dot(heads, hidden_low)
    d_heads = dot_t(hidden_low, full_output).astype(BF16)
    grads = [g.astype(BF16) for g in (d_gate_w, d_up_w, d_down, d_output)]
    return outputs, d_hidden, d_heads, grads, d_mlp_scale


def tables(length):
    freqs = THETA ** (-np.arange(HEAD // 2, dtype=np.float64) * 2.0 / HEAD)
    angles = np.arange(length, dtype=np.float64)[:, None] * np.concatenate([freqs, freqs])[None, :]
    return jnp.asarray(np.cos(angles), F32), jnp.asarray(np.sin(angles), F32)


def placed(values, f, size):
    return lax.dynamic_update_slice_in_dim(jnp.zeros((size,), BF16), values, f * values.shape[0], 0)


def body(inputs, doc_ids, query_proj, key_projection, value_projection, output_proj, gate_proj, up_proj, down_proj,
         attn_gain, mlp_gain, query_norm_gain, key_gain, out_grad):
    f, c = lax.axis_index("fsdp"), lax.axis_index("ctx")
    rows, width = inputs.shape[1:]
    depth = query_proj.shape[0]
    cols = 4 * HEAD
    own = jnp.concatenate([
        lax.dynamic_slice_in_dim(query_proj, c * 2 * HEAD, 2 * HEAD, 1),
        lax.dynamic_slice_in_dim(key_projection, c * HEAD, HEAD, 1),
        lax.dynamic_slice_in_dim(value_projection, c * HEAD, HEAD, 1)], axis=1)
    small = jnp.concatenate([
        placed(attn_gain, f, width), placed(mlp_gain, f, width), placed(query_norm_gain, f, HEAD), placed(key_gain, f, HEAD),
        jnp.zeros((16 * cols - 2 * width - 2 * HEAD,), BF16)]).reshape(16, cols)
    pack = jnp.concatenate([own, small], axis=0)
    sequence = jnp.concatenate([inputs[0], jnp.broadcast_to(doc_ids[0].astype(BF16)[:, None], (rows, HEAD))], axis=1)
    (t, full_output, full_gate, full_up, full_down), x = gather([pack, output_proj, gate_proj, up_proj, down_proj], sequence)
    kept = attend(x, t, *tables(x.shape[0]))
    gains, heads = kept[1], kept[10]
    own_heads = spread(True, heads, 1)
    residual = inputs[0].astype(F32)
    mlp_scale = gains[2:4].reshape(width)
    outputs, d_hidden, d_heads, grads, d_mlp_scale = mlp(
        residual, own_heads, out_grad[0], full_output, full_gate, full_up, full_down, mlp_scale)
    dh = spread(False, d_heads, 2)
    gate_g, up_g, down_g, output_g = sum_all(grads, 3)
    dw, dn, dg = attend_back(x, kept, dh)
    gain_rows = jnp.concatenate([
        dg[0].reshape(16, depth), d_mlp_scale.reshape(16, depth),
        dg[1, :HEAD].reshape(16, 8), dg[1, HEAD:2 * HEAD].reshape(16, 8)], axis=1)
    gain_rows = jnp.pad(gain_rows[:, None, :], ((0, 0), (0, 15), (0, cols - gain_rows.shape[1])))
    dw = jnp.concatenate([dw.reshape(16, depth, cols), gain_rows], axis=1).astype(BF16)
    back, d_normed = last_sums(dw.reshape(2, 4, 2, depth + 16, cols), dn, 4)
    _, norm_pull = jax.vjp(lambda r: root_mean_norm(r, gains[0:2].reshape(width)), residual)
    input_grad = d_hidden + norm_pull(d_normed)[0]
    back = back.astype(F32)
    query_g = jnp.moveaxis(back[:, :depth, :2 * HEAD], 0, 1).reshape(depth, -1)
    key_g = jnp.moveaxis(back[:, :depth, 2 * HEAD:3 * HEAD], 0, 1).reshape(depth, -1)
    value_g = jnp.moveaxis(back[:, :depth, 3 * HEAD:], 0, 1).reshape(depth, -1)
    small_g = jnp.sum(back[:, depth, :], axis=0)
    return (outputs[None], input_grad[None], query_g, key_g, value_g, output_g.astype(F32), gate_g.astype(F32),
            up_g.astype(F32), down_g.astype(F32), small_g[:depth], small_g[depth:2 * depth],
            small_g[2 * depth:2 * depth + 8], small_g[2 * depth + 8:2 * depth + 16])


def solution(mesh):
    seq, weight, gain = P("fsdp", "ctx", None), P("fsdp", None), P("fsdp")
    in_specs = (seq, P("fsdp", "ctx")) + (weight,) * 7 + (gain,) * 4 + (seq,)
    out_specs = (seq, seq) + (weight,) * 7 + (gain,) * 4
    return jax.shard_map(body, mesh=mesh, in_specs=in_specs, out_specs=out_specs, check_vma=False)
```

```python
import functools
import math

import jax
import jax.numpy as jnp
import numpy as np
from jax import lax
from jax.experimental import pallas as pl
from jax.experimental.pallas import tpu as pltpu
from jax.sharding import PartitionSpec as P

MESH = pl.DeviceIdType.MESH
HEAD = 128
EPSILON = 1e-06
THETA = 1000000.0
BF16, F32 = jnp.bfloat16, jnp.float32
FACTOR = 1.0 / math.sqrt(HEAD)
ANY = pl.BlockSpec(memory_space=pl.ANY)
VM = pl.BlockSpec(memory_space=pltpu.VMEM)
DMA = pltpu.SemaphoreType.DMA


def fid(zl, y, k):
    return zl * 8 + y * 2 + k


class Net:
    def __init__(self):
        f, c = lax.axis_index("fsdp"), lax.axis_index("ctx")
        zl, y, k, zh, x = f // 8, (f // 2) % 4, f % 2, c // 4, c % 4
        self.zl, self.y, self.k, self.zh, self.x = zl, y, k, zh, x
        self.z = zh * 2 + zl
        self.f, self.c = f, c
        self.yp, self.ym = self.along("y", 1), self.along("y", 3)
        self.zp, self.zm = self.along("z", 1), self.along("z", 3)
        self.xp, self.xm = self.along("x", 1), self.along("x", 3)
        self.pair = (fid(1 - zl, y, k), c)
        self.sib = (fid(zl, y, 1 - k), c)
        self.peer_c = (1 - zh) * 4 + x
        self.peer = (f, self.peer_c)

    def at(self, dim):
        return {"y": self.y, "x": self.x, "z": self.z}[dim]

    def along(self, dim, off):
        there = (self.at(dim) + off) % 4
        if dim == "y":
            return (fid(self.zl, there, self.k), self.c)
        if dim == "x":
            return (self.f, self.zh * 4 + there)
        return (fid(there % 2, self.y, self.k), (there // 2) * 4 + self.x)

    def ctx(self, off):
        return (self.c + off) % 8


def barrier(devices):
    sem = pltpu.get_barrier_semaphore()
    for d in devices:
        pl.semaphore_signal(sem, inc=1, device_id=d, device_id_type=MESH)
    pl.semaphore_wait(sem, len(devices))


class Copy:
    def __init__(self, copy, made_by):
        self.copy, self.made_by = copy, made_by
        if not made_by.again:
            copy.start()

    def wait_recv(self):
        if not self.made_by.again:
            self.copy.wait_recv()

    def wait(self):
        if not self.made_by.again:
            self.copy.wait()


class Wire:
    def __init__(self, send, recv, again=False):
        self.send, self.recv, self.n, self.all, self.again = send, recv, 0, [], again

    def __call__(self, src, dst, device):
        i = self.n
        self.n += 1
        copy = pltpu.make_async_remote_copy(
            src_ref=src, dst_ref=dst, send_sem=self.send.at[i], recv_sem=self.recv.at[i],
            device_id=device, device_id_type=MESH)
        self.all.append(copy)
        return Copy(copy, self)

    def finish(self):
        for copy in self.all:
            copy.wait_send()


class Local:
    def __init__(self, sems, again=False):
        self.sems, self.n, self.again = sems, 0, again

    def __call__(self, src, dst):
        i = self.n
        self.n += 1
        return Copy(None if self.again else pltpu.make_async_copy(src, dst, self.sems.at[i]), self)


def sems(wires, local):
    return [DMA((wires,)), DMA((wires,)), DMA((local,))]


def talking(number, name, **more):
    return dict(
        compiler_params=pltpu.CompilerParams(
            collective_id=number, has_side_effects=True, vmem_limit_bytes=63 << 20),
        name=name, **more)
def quarters(rows):
    if rows % 64 == 0:
        q = rows // 4
        return (0, q, 2 * q, 3 * q, rows)
    return (0, 16, 32, 48, rows)


class WeightFlow:
    def __init__(self, net, wire, src, out, paired=False):
        self.net, self.wire, self.src, self.out = net, wire, src, out
        self.zp, self.zm = (net.pair, net.pair) if paired else (net.zp, net.zm)
        self.rows = src.shape[0]
        self.q = quarters(self.rows)
        self.c = {}

    def place(self, dz, dy, a=0, b=4):
        n = self.net
        zl = n.zl if dz == 0 else 1 - n.zl
        at = fid(zl, (n.y + dy + 4) % 4, n.k) * self.rows + self.q[a]
        return self.out.at[pl.ds(pl.multiple_of(at, 16), self.q[b] - self.q[a])]

    def own(self, a=0, b=4):
        return self.src.at[pl.ds(self.q[a], self.q[b] - self.q[a])]

    def pass_on(self, name, device, dz, dy, a=0, b=4):
        ref = self.place(dz, dy, a, b)
        self.c[name] = self.wire(ref, ref, device)

    def got(self, name):
        self.c[name].wait_recv()

    def stage(self, s):
        n, w, c = self.net, self.wire, self.c
        if s == 0:
            c["yp"] = w(self.own(), self.place(0, 0), n.yp)
            c["ym"] = w(self.own(), self.place(0, 0), n.ym)
            c["zp"] = w(self.own(0, 2), self.place(0, 0, 0, 2), self.zp)
            c["zm"] = w(self.own(2, 4), self.place(0, 0, 2, 4), self.zm)
            c["d"] = w(self.own(), self.place(0, 0), n.sib)
        elif s == 1:
            self.got("yp")
            self.pass_on("yp2", n.yp, 0, -1, 0, 2)
            self.pass_on("zp_m", self.zp, 0, -1, 0, 2)
            self.pass_on("zm_m", self.zm, 0, -1, 2, 4)
            self.pass_on("d_m", n.sib, 0, -1)
            self.got("ym")
            self.pass_on("ym2", n.ym, 0, 1, 2, 4)
            self.pass_on("zp_p", self.zp, 0, 1, 0, 2)
            self.pass_on("zm_p", self.zm, 0, 1, 2, 4)
            self.pass_on("d_p", n.sib, 0, 1)
            self.got("zp")
            self.pass_on("dz0", n.sib, 1, 0, 0, 2)
            self.got("zm")
            self.pass_on("dz1", n.sib, 1, 0, 2, 4)
        elif s == 2:
            self.got("yp2")
            self.pass_on("zp_2", self.zp, 0, 2, 0, 1)
            self.pass_on("d2a", n.sib, 0, 2, 0, 2)
            self.got("ym2")
            self.pass_on("zm_2", self.zm, 0, 2, 2, 3)
            self.pass_on("d2b", n.sib, 0, 2, 2, 4)
            self.got("zp_m")
            self.pass_on("yq", n.yp, 1, -1, 1, 2)
            self.pass_on("dzm0", n.sib, 1, -1, 0, 2)
            self.got("zm_p")
            self.pass_on("yr", n.ym, 1, 1, 3, 4)
            self.pass_on("dzp1", n.sib, 1, 1, 2, 4)
            self.got("zm_m")
            self.pass_on("dzm1", n.sib, 1, -1, 2, 4)
            self.got("zp_p")
            self.pass_on("dzp0", n.sib, 1, 1, 0, 2)
        elif s == 3:
            self.got("zp_2")
            self.got("yq")
            self.pass_on("dz20", n.sib, 1, 2, 0, 2)
            self.got("zm_2")
            self.got("yr")
            self.pass_on("dz21", n.sib, 1, 2, 2, 4)
        elif s == 4:
            for name in ("d", "d_m", "d_p", "dz0", "dz1", "d2a", "d2b", "dzm0", "dzp1", "dzm1", "dzp0", "dz20", "dz21"):
                self.got(name)


class RowFlow:
    def __init__(self, net, wire, src, out):
        self.net, self.wire, self.src, self.out = net, wire, src, out
        self.rows = src.shape[0]
        self.c = {}

    def place(self, ctx, a=0, b=2):
        lo, hi = a * self.rows // 2, b * self.rows // 2
        return self.out.at[pl.ds(pl.multiple_of(ctx * self.rows + lo, 16), hi - lo)]

    def pass_on(self, name, device, ctx, a=0, b=2):
        ref = self.place(ctx, a, b)
        self.c[name] = self.wire(ref, ref, device)

    def got(self, name):
        self.c[name].wait_recv()

    def stage(self, s):
        n, w, c = self.net, self.wire, self.c
        left, right = n.zh * 4 + (n.x + 3) % 4, n.zh * 4 + (n.x + 1) % 4
        left2, right2 = (1 - n.zh) * 4 + (n.x + 3) % 4, (1 - n.zh) * 4 + (n.x + 1) % 4
        if s == 0:
            c["pz"] = w(self.src, self.place(n.c), n.peer)
            c["xp"] = w(self.src, self.place(n.c), n.xp)
            c["xm"] = w(self.src, self.place(n.c), n.xm)
        elif s == 1:
            self.got("pz")
            self.pass_on("px", n.xp, n.peer_c)
            self.pass_on("pxm", n.xm, n.peer_c)
            self.got("xp")
            self.pass_on("xp2", n.xp, left, 0, 1)
            self.got("xm")
            self.pass_on("xm2", n.xm, right, 1, 2)
        elif s == 2:
            self.got("px")
            self.pass_on("px2", n.xp, left2, 0, 1)
            self.got("pxm")
            self.pass_on("pxm2", n.xm, right2, 1, 2)
        elif s == 3:
            for name in ("xp2", "xm2", "px2", "pxm2"):
                self.got(name)


class Later:
    def __init__(self, steps):
        self.steps = list(steps)

    def __call__(self):
        if self.steps:
            self.steps.pop(0)()

    def rest(self):
        while self.steps:
            self()


def stage(flow, *numbers):
    def go():
        for s in numbers:
            flow.stage(s)
    return go


def together(*steps):
    def go():
        for s in steps:
            s()
    return go


class Spread:
    def __init__(self, net, wire, here, forward, src, dst):
        rows, cols = (dst.shape[0], src.shape[1]) if forward else (src.shape[0], dst.shape[1])

        def by_row(ref, c):
            return ref.at[pl.ds(pl.multiple_of(c * rows, 16), rows)]

        def by_col(ref, c):
            return ref.at[:, pl.ds(pl.multiple_of(c * cols, 128), cols)]

        pick, put = (by_row, by_col) if forward else (by_col, by_row)
        self.copies = []
        for o in (6, 2, 4, 5, 7, 1, 3):
            there = net.ctx(o)
            self.copies.append(wire(pick(src, there), put(dst, net.c), (net.f, there)))
        self.own = here(pick(src, net.c), put(dst, net.c))

    def end(self):
        for copy in self.copies:
            copy.wait_recv()
        self.own.wait()


def neighbours(net):
    return ([net.sib] + [net.along(d, o) for d in "yz" for o in (1, 2, 3)] + [(net.f, net.ctx(o)) for o in (1, 2, 3, 5, 6, 7)])


KEPT = 11


def forward_kernel(nw, *refs):
    srcs, rows, cos_in, sin_in = refs[:nw], refs[nw], refs[nw + 1], refs[nw + 2]
    refs = refs[nw + 3:]
    outs, rows_out, own_heads, kept_out = refs[:nw - 1], refs[nw - 1], refs[nw], refs[nw + 1:nw + 1 + KEPT]
    refs = refs[nw + 1 + KEPT:]
    x, t, cos_at, sin_at, heads = refs[:5]
    kept = refs[5:5 + KEPT]
    send, recv, local = refs[5 + KEPT:]
    w, gains, q, k, v, lin, cs, sn, start, hf, inv = kept
    net, wire, here = Net(), Wire(send, recv), Local(local)
    barrier(neighbours(net))
    flows = [WeightFlow(net, wire, s, o, i == 0) for i, (s, o) in enumerate(zip(srcs, (t, *outs)))]
    first, seq = flows[0], RowFlow(net, wire, rows, x)
    first.stage(0)
    seq.stage(0)
    flows[1].stage(0)
    tables_in = [here(cos_in, cos_at), here(sin_in, sin_at)]
    placed_here = [here(fl.src, fl.place(0, 0)) for fl in flows]
    placed_here.append(here(rows, seq.place(net.c)))
    first.stage(1)
    flows[2].stage(0)
    seq.stage(1)
    first.stage(2)
    flows[1].stage(1)
    seq.stage(2)
    first.stage(3)
    flows[3].stage(0)
    first.stage(4)
    flows[2].stage(1)
    flows[1].stage(2)
    seq.stage(3)
    for c in tables_in + placed_here:
        c.wait()
    saved = [here(x, rows_out)]
    tick = Later([
        together(stage(flows[4], 0), stage(flows[1], 3)),
        together(stage(flows[3], 1), stage(flows[2], 2)),
        stage(flows[2], 3),
        together(stage(flows[4], 1), stage(flows[3], 2)),
        stage(flows[3], 3),
        stage(flows[4], 2),
    ])
    attn_forward(tick, x, t, cos_at, sin_at, w, gains, q, k, v, lin, cs, sn, start, hf, heads, inv)
    spread = Spread(net, wire, here, True, heads, own_heads)
    saved += [here(a, b) for a, b in zip(kept, kept_out)]
    tick.rest()
    flows[4].stage(3)
    for fl in flows[1:]:
        fl.stage(4)
    spread.end()
    for c in saved:
        c.wait()
    wire.finish()


def shapes(*items):
    return [jax.ShapeDtypeStruct(s, d) for s, d in items]


def forward(weights, rows, cos_in, sin_in):
    nw = len(weights)
    per, cols = weights[0].shape
    length = 8 * rows.shape[0]
    kept = shapes(
        ((16 * (per - 16), cols), BF16), ((16, cols), F32), ((2, length, HEAD), BF16), ((length, HEAD), BF16),
        ((length, HEAD), BF16), ((length, 3 * HEAD), F32), ((length, HEAD), F32), ((length, HEAD), F32),
        ((length, HEAD), F32), ((length, 2 * HEAD), F32), ((2, length, HEAD), F32))
    outs = [jax.ShapeDtypeStruct((16 * w.shape[0], w.shape[1]), w.dtype) for w in weights[1:]]
    outs += shapes(((length, rows.shape[1]), BF16), ((rows.shape[0], 16 * HEAD), BF16)) + kept
    scratch = [((length, rows.shape[1]), BF16), ((16 * per, cols), BF16), ((length, HEAD), F32), ((length, HEAD), F32), ((length, 2 * HEAD), BF16)]
    res = pl.pallas_call(
        functools.partial(forward_kernel, nw),
        out_shape=outs, in_specs=[ANY] * (nw + 3), out_specs=[ANY] * len(outs),
        scratch_shapes=[pltpu.VMEM(s, d) for s, d in scratch] + [pltpu.VMEM(a.shape, a.dtype) for a in kept]
        + sems(27 * nw + 9 + 7, nw + 3 + 1 + 1 + KEPT), **talking(0, "layer_forward"),
    )(*weights, rows, cos_in, sin_in)
    return res[:nw - 1], res[nw - 1], res[nw], res[nw + 1:]
def block(i, size):
    return pl.ds(pl.multiple_of(i * size, size), size)


def dot_t(left, right):
    return lax.dot_general(left, right, (((1,), (1,)), ((), ())), preferred_element_type=F32)


def t_dot(left, right):
    return lax.dot_general(left, right, (((0,), (0,)), ((), ())), preferred_element_type=F32)


def plain_dot(left, right):
    return jnp.dot(left, right, preferred_element_type=F32)


def unit(v):
    r = lax.rsqrt(jnp.mean(v * v, axis=-1, keepdims=True) + EPSILON)
    return v * r, r


ROWS = 256


def attn_forward(tick, x, t, cos_in, sin_in, w, gains, q, k, v, lin, cs, sn, start, hf, heads, inv):
    length, width = x.shape[0], x.shape[1] - HEAD
    per = t.shape[0] // 16
    depth = per - 16
    total = jnp.zeros((16, t.shape[1]), F32)
    for f in range(16):
        w[f * depth:(f + 1) * depth, :] = t[f * per:f * per + depth, :]
        total = total + t[f * per + depth:(f + 1) * per, :].astype(F32)
    gains[...] = total
    attn_gain = jnp.concatenate([total[0:1], total[1:2]], axis=1)
    query_gain, key_gain = total[4:5, 0:HEAD], total[4:5, HEAD:2 * HEAD]

    def count(i, carry):
        doc = x[block(i, ROWS), width:].astype(F32)
        return (carry[0] + jnp.sum((doc < 0.5).astype(F32), axis=0, keepdims=True),
                carry[1] + jnp.sum((doc < 1.5).astype(F32), axis=0, keepdims=True))

    zero = jnp.zeros((1, HEAD), F32)
    first, second = lax.fori_loop(0, length // ROWS, count, (zero, zero))
    lanes = lax.broadcasted_iota(jnp.int32, (1, HEAD), 1) % (HEAD // 2)
    freqs = jnp.exp(lanes.astype(F32) * (-2.0 * math.log(THETA) / HEAD))
    c1, s1 = jnp.cos(first * freqs), jnp.sin(first * freqs)
    c2, s2 = jnp.cos(second * freqs), jnp.sin(second * freqs)
    sign = jnp.where(lax.broadcasted_iota(jnp.int32, (1, HEAD), 1) < HEAD // 2, -1.0, 1.0)

    def prepare(i, carry):
        rows = block(i, ROWS)
        doc = x[rows, width:].astype(F32)
        start[rows, :] = jnp.where(doc < 0.5, 0.0, jnp.where(doc < 1.5, first, second))
        cd = jnp.where(doc < 0.5, 1.0, jnp.where(doc < 1.5, c1, c2))
        sd = jnp.where(doc < 0.5, 0.0, jnp.where(doc < 1.5, s1, s2))
        ci, si = cos_in[rows, :], sin_in[rows, :]
        cosine = ci * cd + si * sd
        sine = (si * cd - ci * sd) * sign
        cs[rows, :] = cosine
        sn[rows, :] = sine
        normed = (unit(x[rows, :width].astype(F32))[0] * attn_gain).astype(BF16)
        out = plain_dot(normed, w[...])
        lin[rows, :] = out[:, :3 * HEAD]
        v[rows, :] = out[:, 3 * HEAD:].astype(BF16)
        for h in range(3):
            e = unit(out[:, h * HEAD:(h + 1) * HEAD])[0] * (query_gain if h < 2 else key_gain)
            e = (e * cosine + pltpu.roll(e, HEAD // 2, 1) * sine).astype(BF16)
            if h < 2:
                q[h, rows, :] = e
            else:
                k[rows, :] = e
        return carry

    for i in range(0, length // ROWS, 2):
        lax.fori_loop(i, i + 2, prepare, 0)
        tick()

    def queries(i, carry):
        rows = block(i, ROWS)
        here = q[:, rows, :].reshape(2 * ROWS, HEAD)
        begin = start[rows, :]

        def keys(j, state):
            acc, norm = state
            these = block(j, ROWS)
            p = jnp.exp(dot_t(here, k[these, :]) * FACTOR)
            p = jnp.where(allowed_at(i, j, begin), p.reshape(2, ROWS, ROWS), 0.0).reshape(2 * ROWS, ROWS)
            norm = norm + p[:, :HEAD] + p[:, HEAD:]
            return acc + plain_dot(p.astype(BF16), v[these, :]), norm

        zeros = jnp.zeros((2 * ROWS, HEAD), F32)
        acc, norm = lax.fori_loop(0, i + 1, keys, (zeros, zeros))
        over = jnp.broadcast_to(1.0 / jnp.sum(norm, axis=1, keepdims=True), (2 * ROWS, HEAD))
        acc = acc * over
        inv[:, rows, :] = over.reshape(2, ROWS, HEAD)
        for h in range(2):
            part = acc[h * ROWS:(h + 1) * ROWS]
            hf[rows, h * HEAD:(h + 1) * HEAD] = part
            heads[rows, h * HEAD:(h + 1) * HEAD] = part.astype(BF16)
        return carry

    for i, j in ((0, 3), (3, 4), (4, 5), (5, 6)):
        lax.fori_loop(i, j, queries, 0)
        tick()


def allowed_at(i, j, begin):
    own = lax.broadcasted_iota(jnp.int32, (ROWS, ROWS), 0) + i * ROWS
    other = lax.broadcasted_iota(jnp.int32, (ROWS, ROWS), 1) + j * ROWS
    begin = jnp.concatenate([begin, begin], axis=1)
    return ((other.astype(F32) >= begin) & (other <= own))[None]


def attn_backward(tick, gains, q, k, v, start, hf, inv, dh, dq, dk, dv, delta):
    length = dh.shape[0]
    blocks = length // ROWS

    def before(i, carry):
        rows = block(i, ROWS)
        for h in range(2):
            cols = slice(h * HEAD, (h + 1) * HEAD)
            s = jnp.sum(dh[rows, cols].astype(F32) * hf[rows, cols], axis=1, keepdims=True)
            delta[h, rows, :] = jnp.broadcast_to(s, (ROWS, HEAD))
            dq[h, rows, :] = jnp.zeros((ROWS, HEAD), F32)
        return carry

    lax.fori_loop(0, blocks, before, 0)

    def keys(j, carry):
        these = block(j, ROWS)
        kt, vt = k[these, :], v[these, :]

        def queries(i, state):
            d_key, d_value = state
            rows = block(i, ROWS)
            here = q[:, rows, :].reshape(2 * ROWS, HEAD)
            grad = jnp.concatenate([dh[rows, :HEAD], dh[rows, HEAD:]], axis=0)
            over = inv[:, rows, :].reshape(2 * ROWS, HEAD)
            off = delta[:, rows, :].reshape(2 * ROWS, HEAD)
            over = jnp.concatenate([over, over], axis=1)
            off = jnp.concatenate([off, off], axis=1)
            p = jnp.exp(dot_t(here, kt) * FACTOR) * over
            p = jnp.where(allowed_at(i, j, start[rows, :]), p.reshape(2, ROWS, ROWS), 0.0).reshape(2 * ROWS, ROWS)
            ds = (p * (dot_t(grad, vt) - off)).astype(BF16)
            dq[:, rows, :] = dq[:, rows, :] + plain_dot(ds, kt).reshape(2, ROWS, HEAD)
            return d_key + t_dot(ds, here), d_value + t_dot(p.astype(BF16), grad)

        zeros = jnp.zeros((ROWS, HEAD), F32)
        d_key, d_value = lax.fori_loop(j, blocks, queries, (zeros, zeros))
        dk[these, :] = d_key
        dv[these, :] = d_value
        return carry

    for i, j in ((0, 1), (1, 2), (2, 4), (4, 6)):
        lax.fori_loop(i, j, keys, 0)
        tick()


WIDE = 384


def attn_backward_end(x, w, gains, lin, cs, sn, dq, dk, dv, dlin, dw, dn):
    length, width = x.shape[0], x.shape[1] - HEAD
    g = gains[...]
    attn_gain = jnp.concatenate([g[0:1], g[1:2]], axis=1)
    query_gain, key_gain = g[4:5, 0:HEAD], g[4:5, HEAD:2 * HEAD]

    def after(i, carry):
        d_attn, d_query, d_key = carry
        rows = block(i, WIDE)
        cosine, sine = cs[rows, :], sn[rows, :]
        for h in range(3):
            cols = slice(h * HEAD, (h + 1) * HEAD)
            d = (dq[h, rows, :] if h < 2 else dk[rows, :]) * FACTOR
            d = d * cosine - pltpu.roll(d, HEAD // 2, 1) * sine
            e, r = unit(lin[rows, cols])
            s = jnp.sum(d * e, axis=0, keepdims=True)
            d_query, d_key = (d_query + s, d_key) if h < 2 else (d_query, d_key + s)
            d = d * (query_gain if h < 2 else key_gain)
            d = r * (d - e * jnp.mean(d * e, axis=-1, keepdims=True))
            dlin[rows, cols] = d.astype(BF16)
        dlin[rows, 3 * HEAD:] = dv[rows, :].astype(BF16)
        part = dot_t(dlin[rows, :], w[...])
        e = unit(x[rows, :width].astype(F32))[0]
        d_attn = d_attn + jnp.sum(part * e, axis=0, keepdims=True)
        dn[i // 2, pl.ds((i % 2) * 2, 2)] = part.astype(BF16).reshape(2, WIDE // 2, width)
        normed = (e * attn_gain).astype(BF16)

        part = t_dot(normed, dlin[rows, :])
        dw[...] = jnp.where(i == 0, part, dw[...] + part)
        return d_attn, d_query, d_key

    zero = jnp.zeros((1, HEAD), F32)
    dw[...] = jnp.zeros_like(dw)
    return lax.fori_loop(0, length // WIDE, after, (jnp.zeros((1, width), F32), zero, zero))


def shapes(*items):
    return [jax.ShapeDtypeStruct(s, d) for s, d in items]


def add_rows(out, parts, rows, step):
    def some(r, carry):
        here = pl.ds(pl.multiple_of(r * step, 16), step)
        if len(parts) == 2:
            out(here, parts[0](here) + parts[1](here))
            return carry
        total = parts[0](here).astype(F32)
        for part in parts[1:]:
            total = total + part(here).astype(F32)
        out(here, total.astype(BF16))
        return carry

    lax.fori_loop(0, rows // step, some, 0)


FIRST = (2, 1, 3, 0)


class SumFlow:
    def __init__(self, net, wire, here, src, first, order, slots, other, got, part, fin, out):
        self.net, self.wire, self.here, self.src, self.first, self.order = net, wire, here, src, first, order
        self.slots, self.other, self.got, self.part, self.fin, self.out = slots, other, got, part, fin, out
        self.rows, self.cols = other.shape[2], other.shape[3]
        self.w = self.cols // 8
        self.far = {}

    def cut(self, ref, dim, d, k=None):
        tail = ref.shape[-1]
        a = (slice(None), slice(None))
        cols = pl.ds(0, tail)
        if dim == "y":
            a = (slice(None), pl.ds(d, 1))
        elif dim == "x":
            cols = pl.ds(pl.multiple_of(d * (tail // 4), 128), tail // 4)
        else:
            a = (pl.ds(d % 2, 1), slice(None))
            cols = pl.ds(pl.multiple_of((d // 2) * (tail // 2), 128), tail // 2)
        if k is None:
            return ref.at[a[0], a[1], :, cols]
        return ref.at[a[0], a[1], k, pl.ds(self.first, self.rows), cols]

    def begin(self):
        n, dim = self.net, self.order[0]
        self.near, self.own = {}, {}
        for o in FIRST:
            d = (n.at(dim) + o) % 4
            self.near[o] = self.wire(self.cut(self.src, dim, d, 1 - n.k), self.cut(self.other, dim, d), n.sib)
        self.bring(0)
        self.bring(1)

    def bring(self, i):
        n, dim = self.net, self.order[0]
        d = (n.at(dim) + FIRST[i]) % 4
        self.own[FIRST[i]] = self.here(self.cut(self.src, dim, d, n.k), self.slots.at[i % 2])

    def add(self, out, parts):
        if self.wire.again:
            return
        a, b = out.shape[0], out.shape[1]
        step = 16
        for i in range(a):
            for j in range(b):
                def take(ref):
                    return lambda here: ref[i, j, here, :]

                def put(here, value):
                    out[i, j, here, :] = value
                add_rows(put, [take(p) for p in parts], self.rows, step)

    def chip(self, o):
        n, dim = self.net, self.order[0]
        d = (n.at(dim) + o) % 4
        self.near[o].wait_recv()
        self.own[o].wait()
        i = FIRST.index(o)
        piece = self.cut(self.other, dim, d)
        self.add(piece, [piece, self.slots.at[i % 2]])
        if i + 2 < 4:
            self.bring(i + 2)
        if o:
            self.far[o] = self.wire(piece, self.got[0].at[o - 1], n.along(dim, o))

    def phase(self, p):
        n, dim = self.net, self.order[p]
        held = self.other if p == 0 else self.part[p - 1]
        for o in (1, 3, 2):
            self.far[o].wait_recv()
        result = self.part[p] if p < 2 else self.fin
        self.add(result, [self.cut(held, dim, n.at(dim))] + [self.got[p].at[o - 1] for o in (1, 2, 3)])
        if p < 2:
            after = self.order[p + 1]
            for o in (2, 1, 3):
                d = (n.at(after) + o) % 4
                self.far[o] = self.wire(self.cut(result, after, d), self.got[p + 1].at[o - 1], n.along(after, o))
        else:
            fin, to = self.fin.at[0, 0], self.place(n.zh)
            self.across = self.wire(fin, to, n.peer)
            self.last = [self.wire(fin, to, n.along("x", o)) for o in (2, 1, 3)]
            self.kept = self.here(fin, to)

    def place(self, zh):
        n = self.net
        s = zh * 4 + n.x if self.order == "zyx" else n.x * 2 + zh
        return self.out.at[pl.ds(self.first, self.rows), pl.ds(pl.multiple_of(s * self.w, 128), self.w)]

    def share(self):
        n = self.net
        self.across.wait_recv()
        to = self.place(1 - n.zh)
        self.last += [self.wire(to, to, n.along("x", o)) for o in (2, 1, 3)]

    def end(self):
        for copy in self.last:
            copy.wait_recv()
        self.kept.wait()


def sum_shapes(rows, cols, order):
    shape, out = [2, 4, rows, cols], []
    for dim in order:
        if dim == "y":
            shape[1] = 1
        elif dim == "x":
            shape[3] //= 4
        else:
            shape[0], shape[3] = 1, shape[3] // 2
        out.append(tuple(shape))
    return out


PLAN = ((0, 0, 64, "yxz"), (1, 0, 64, "yxz"), (2, 0, 192, "zyx"), (3, 0, 64, "xzy"), (3, 64, 64, "zyx"))


def first_shapes(plan, shapes_in):
    return [sum_shapes(rows, shapes_in[which][-1], order)[0] for which, _, rows, order in plan]


def sum_scratch(plan, shapes_in):
    held = []
    for which, first, rows, order in plan:
        cols = shapes_in[which][-1]
        a, b, c = sum_shapes(rows, cols, order)
        held += [pltpu.VMEM(s, BF16) for s in ((2, 4, rows, cols), (3, *a), (3, *b), (3, *c), a, b, c)]
    return held


def make_flows(net, wire, here, plan, srcs, outs, held, slots):
    flows = []
    for n, (which, first, rows, order) in enumerate(plan):
        other, g0, g1, g2, p0, p1, fin = held[7 * n:7 * n + 7]
        flows.append(SumFlow(net, wire, here, srcs[which], first, order, slots[n], other, (g0, g1, g2), (p0, p1), fin, outs[which]))
    return flows


class Ends:
    def __init__(self, net, wire, here, dwx, dn, rows_out, dn_out, other, got, fin, got_x, part, got_z):
        self.net, self.wire, self.here, self.dwx, self.dn, self.rows_out, self.dn_out = net, wire, here, dwx, dn, rows_out, dn_out
        self.other, self.got, self.fin, self.got_x, self.part, self.got_z = other, got, fin, got_x, part, got_z

    def begin(self):
        n = self.net
        self.moved = {o: self.wire(self.dn.at[:, (n.x + o) % 4], self.got_x.at[o - 1], n.along("x", o)) for o in (2, 1, 3)}
        self.near = self.wire(self.dwx.at[:, :, 1 - n.k], self.other, n.sib)

    def chip(self):
        n = self.net
        self.near.wait_recv()
        for a in range(2):
            for b in range(4):
                self.other[a, b] = self.other[a, b] + self.dwx[a, b, n.k]
        self.far = []
        for dz in (1, 0):
            for dy in (2, 1, 3, 0):
                if dz or dy:
                    there = ((n.zl + dz) % 2, (n.y + dy) % 4)
                    self.far.append(self.wire(self.other.at[there[0], there[1]], self.got.at[dz * 4 + dy - 1], (fid(there[0], there[1], n.k), n.c)))

    def along_x(self):
        n = self.net
        for copy in self.moved.values():
            copy.wait_recv()

        for zh in range(2):
            def take(o):
                return (lambda here: self.dn[zh, n.x, here, :]) if o == 0 else (lambda here: self.got_x[o - 1, zh, here, :])

            def put(here, value):
                self.part[zh, here, :] = value
            add_rows(put, [take(o) for o in range(4)], self.part.shape[1], 16)
        self.over = self.wire(self.part.at[1 - n.zh], self.got_z, n.peer)

    def share(self):
        n = self.net
        for copy in self.far:
            copy.wait_recv()
        total = self.other[n.zl, n.y].astype(F32)
        for i in range(7):
            total = total + self.got[i].astype(F32)
        self.fin[...] = total.astype(BF16)
        self.copies = [self.wire(self.fin, self.rows_out.at[n.c], (n.f, n.ctx(o))) for o in (6, 2, 4, 5, 7, 1, 3)]
        self.kept = self.here(self.fin, self.rows_out.at[n.c])

    def end(self):
        n = self.net
        self.over.wait_recv()

        def some(r, carry):
            at = pl.ds(pl.multiple_of(r * 16, 16), 16)
            self.dn_out[at, :] = self.part[n.zh, at, :].astype(F32) + self.got_z[at, :].astype(F32)
            return carry

        lax.fori_loop(0, self.got_z.shape[0] // 16, some, 0)
        for copy in self.copies:
            copy.wait_recv()
        self.kept.wait()


def backward_kernel(ng, *refs):
    srcs, x_in, d_heads, mlp_rows, kept_in = refs[:ng], refs[ng], refs[ng + 1], refs[ng + 2], refs[ng + 3:ng + 3 + KEPT]
    refs = refs[ng + 3 + KEPT:]
    outs, rows_out, dn_out = refs[:ng], refs[ng], refs[ng + 1]
    refs = refs[ng + 2:]
    kept, refs = refs[:KEPT], refs[KEPT:]
    w, gains, q, k, v, lin, cs, sn, start, hf, inv = kept
    dh, dq, dk, dv, delta, mlp_at, dwx, dn = refs[:8]
    end_held, refs = refs[8:14], refs[14:]
    held, (send, recv, local) = refs[:-3], refs[-3:]
    net = Net()
    length, width = x_in.shape[0], x_in.shape[1] - HEAD
    depth = w.shape[0] // 16

    def slotted(*slots):
        wire, here = Wire(send, recv), Local(local)
        barrier(neighbours(net))
        spread = Spread(net, wire, here, False, d_heads, dh)
        flows = make_flows(net, wire, here, PLAN, srcs, outs, held, slots)
        for fl in flows:
            fl.begin()
        loads = [here(a, b) for a, b in zip(kept_in, kept)] + [here(mlp_rows, mlp_at)]
        for fl in flows:
            fl.chip(2)
        for c in loads:
            c.wait()
        spread.end()

        def chips(o):
            def go():
                for fl in flows:
                    fl.chip(o)
            return go

        tick = Later([chips(1), chips(3), chips(0)])
        attn_backward(tick, gains, q, k, v, start, hf, inv, dh, dq, dk, dv, delta)
        tick.rest()

    pl.run_scoped(slotted, *[pltpu.VMEM((2, *a), BF16) for a in first_shapes(PLAN, [s.shape for s in srcs])])
    wire, here = Wire(send, recv, True), Local(local, True)
    Spread(net, wire, here, False, d_heads, dh)
    flows = make_flows(net, wire, here, PLAN, srcs, outs, held, held[1::7])
    for fl in flows:
        fl.begin()
    for a, b in list(zip(kept_in, kept)) + [(mlp_rows, mlp_at)]:
        here(a, b)
    for o in (2, 1, 3, 0):
        for fl in flows:
            fl.chip(o)
    wire.again = here.again = False
    ends = Ends(net, wire, here, dwx, dn, rows_out, dn_out, *end_held)

    def ending(x, dlin, dw):
        fetch = pltpu.make_async_copy(x_in, x, local.at[local.shape[0] - 1])
        fetch.start()
        fetch.wait()
        d_attn, d_query, d_key = attn_backward_end(x, w, gains, lin, cs, sn, dq, dk, dv, dlin, dw, dn)
        cols = dw.shape[1]
        lanes = jnp.concatenate([d_query, d_key, jnp.zeros((1, cols - 2 * HEAD), F32)], axis=1)
        small = jnp.concatenate([d_attn[:, :cols], d_attn[:, cols:], jnp.zeros((2, cols), F32), lanes, jnp.zeros((11, cols), F32)], axis=0)
        small = (small + mlp_at[...]).astype(BF16)
        for f in range(16):
            at = (f // 8, (f // 2) % 4, f % 2)
            dwx[at[0], at[1], at[2], :depth, :] = dw[f * depth:(f + 1) * depth, :].astype(BF16)
            dwx[at[0], at[1], at[2], depth:, :] = small

    pl.run_scoped(ending, pltpu.VMEM((length, width + HEAD), BF16), pltpu.VMEM((length, 4 * HEAD), BF16), pltpu.VMEM((16 * depth, 4 * HEAD), F32))
    ends.begin()
    for fl in flows:
        fl.phase(0)
    ends.chip()
    ends.along_x()
    for fl in flows:
        fl.phase(1)
    ends.share()
    for fl in flows:
        fl.phase(2)
    for fl in flows:
        fl.share()
    ends.end()
    for fl in flows:
        fl.end()
    wire.finish()


def backward(grads, x, d_heads, mlp_rows, kept):
    srcs = [g.reshape(2, 4, 2, g.shape[0] // 16, g.shape[1]) for g in grads]
    length, width = x.shape[0], x.shape[1] - HEAD
    rows, cols = length // 8, 4 * HEAD
    depth = width // 16
    out = [jax.ShapeDtypeStruct((g.shape[0] // 16, g.shape[1]), BF16) for g in grads]
    out += shapes(((8, depth + 16, cols), BF16), ((rows, width), F32))
    scratch = [(a.shape, a.dtype) for a in kept]
    scratch += [((length, 2 * HEAD), BF16), ((2, length, HEAD), F32), ((length, HEAD), F32), ((length, HEAD), F32),
                ((2, length, HEAD), F32), (mlp_rows.shape, F32), ((2, 4, 2, depth + 16, cols), BF16), ((2, 4, rows, width), BF16)]
    scratch += [((2, 4, depth + 16, cols), BF16), ((7, depth + 16, cols), BF16), ((depth + 16, cols), BF16),
                ((3, 2, rows, width), BF16), ((2, rows, width), BF16), ((rows, width), BF16)]
    ng = len(grads)
    wires = 20 * len(PLAN) + 7 + 3 + 1 + 7 + 1 + 7
    local = 5 * len(PLAN) + 1 + KEPT + 1 + 1 + 1
    res = pl.pallas_call(
        functools.partial(backward_kernel, ng), out_shape=out,
        in_specs=[ANY] * (ng + 3 + KEPT), out_specs=[ANY] * (ng + 1) + [VM],
        scratch_shapes=[pltpu.VMEM(s, d) for s, d in scratch] + sum_scratch(PLAN, [s.shape for s in srcs]) + sems(wires, local),
        **talking(1, "layer_backward"))(*srcs, x, d_heads, mlp_rows, *kept)
    return res[:ng], res[ng], res[ng + 1]
def root_mean_norm(rows, scaling):
    return rows * lax.rsqrt(jnp.mean(rows * rows, axis=-1, keepdims=True) + EPSILON) * scaling


def silu_product(gate, upward):
    return jax.nn.silu(gate) * upward


def mlp(residual, heads, grad_rows, full_output, full_gate, full_up, full_down, mlp_scale):
    hidden = residual + plain_dot(heads, full_output)
    mixed_f, mix_pull = jax.vjp(root_mean_norm, hidden, mlp_scale)
    mixed = mixed_f.astype(BF16)
    gate, upward = plain_dot(mixed, full_gate), plain_dot(mixed, full_up)
    active_f, active_pull = jax.vjp(silu_product, gate, upward)
    active = active_f.astype(BF16)
    outputs = (hidden + plain_dot(active, full_down)).astype(BF16)
    d_down = t_dot(active, grad_rows)
    d_gate, d_upward = active_pull(dot_t(grad_rows, full_down))
    gate_low, up_low = d_gate.astype(BF16), d_upward.astype(BF16)
    d_gate_w, d_up_w = t_dot(mixed, gate_low), t_dot(mixed, up_low)
    d_mixed = dot_t(gate_low, full_gate) + dot_t(up_low, full_up)
    d_hidden_norm, d_mlp_scale = mix_pull(d_mixed)
    d_hidden = grad_rows.astype(F32) + d_hidden_norm
    hidden_low = d_hidden.astype(BF16)
    d_output = t_dot(heads, hidden_low)
    d_heads = dot_t(hidden_low, full_output).astype(BF16)
    grads = [g.astype(BF16) for g in (d_gate_w, d_up_w, d_down, d_output)]
    return outputs, d_hidden, d_heads, grads, d_mlp_scale


def tables(length):
    freqs = THETA ** (-np.arange(HEAD // 2, dtype=np.float64) * 2.0 / HEAD)
    angles = np.arange(length, dtype=np.float64)[:, None] * np.concatenate([freqs, freqs])[None, :]
    return jnp.asarray(np.cos(angles), F32), jnp.asarray(np.sin(angles), F32)


def placed(values, f, size):
    return lax.dynamic_update_slice_in_dim(jnp.zeros((size,), BF16), values, f * values.shape[0], 0)


def body(inputs, doc_ids, query_proj, key_projection, value_projection, output_proj, gate_proj, up_proj, down_proj,
         attn_gain, mlp_gain, query_norm_gain, key_gain, out_grad):
    f, c = lax.axis_index("fsdp"), lax.axis_index("ctx")
    rows, width = inputs.shape[1:]
    depth = query_proj.shape[0]
    cols = 4 * HEAD
    own = jnp.concatenate([
        lax.dynamic_slice_in_dim(query_proj, c * 2 * HEAD, 2 * HEAD, 1),
        lax.dynamic_slice_in_dim(key_projection, c * HEAD, HEAD, 1),
        lax.dynamic_slice_in_dim(value_projection, c * HEAD, HEAD, 1)], axis=1)
    small = jnp.concatenate([
        placed(attn_gain, f, width), placed(mlp_gain, f, width), placed(query_norm_gain, f, HEAD), placed(key_gain, f, HEAD),
        jnp.zeros((16 * cols - 2 * width - 2 * HEAD,), BF16)]).reshape(16, cols)
    pack = jnp.concatenate([own, small], axis=0)
    sequence = jnp.concatenate([inputs[0], jnp.broadcast_to(doc_ids[0].astype(BF16)[:, None], (rows, HEAD))], axis=1)
    (full_output, full_gate, full_up, full_down), x, own_heads, kept = forward(
        [pack, output_proj, gate_proj, up_proj, down_proj], sequence, *tables(8 * rows))
    gains = kept[1]
    residual = inputs[0].astype(F32)
    mlp_scale = gains[2:4].reshape(width)
    outputs, d_hidden, d_heads, grads, d_mlp_scale = mlp(
        residual, own_heads, out_grad[0], full_output, full_gate, full_up, full_down, mlp_scale)
    mlp_rows = jnp.pad(d_mlp_scale.reshape(2, cols), ((2, 12), (0, 0)))
    (gate_g, up_g, down_g, output_g), back, d_normed = backward(grads, x, d_heads, mlp_rows, kept)
    _, norm_pull = jax.vjp(lambda r: root_mean_norm(r, gains[0:2].reshape(width)), residual)
    input_grad = d_hidden + norm_pull(d_normed)[0]
    back = back.astype(F32)
    query_g = jnp.moveaxis(back[:, :depth, :2 * HEAD], 0, 1).reshape(depth, -1)
    key_g = jnp.moveaxis(back[:, :depth, 2 * HEAD:3 * HEAD], 0, 1).reshape(depth, -1)
    value_g = jnp.moveaxis(back[:, :depth, 3 * HEAD:], 0, 1).reshape(depth, -1)
    small_g = jnp.sum(back[:, depth:, :], axis=0)

    def mine(values, size):
        return lax.dynamic_slice_in_dim(values, f * size, size)

    return (outputs[None], input_grad[None], query_g, key_g, value_g, output_g.astype(F32), gate_g.astype(F32),
            up_g.astype(F32), down_g.astype(F32), mine(small_g[0:2].reshape(width), depth), mine(small_g[2:4].reshape(width), depth),
            mine(small_g[4, :HEAD], HEAD // 16), mine(small_g[4, HEAD:2 * HEAD], HEAD // 16))


def solution(mesh):
    seq, weight, gain = P("fsdp", "ctx", None), P("fsdp", None), P("fsdp")
    in_specs = (seq, P("fsdp", "ctx")) + (weight,) * 7 + (gain,) * 4 + (seq,)
    out_specs = (seq, seq) + (weight,) * 7 + (gain,) * 4
    return jax.shard_map(body, mesh=mesh, in_specs=in_specs, out_specs=out_specs, check_vma=False)
```

```python
import functools
import math

import jax
import jax.numpy as jnp
import numpy as np
from jax import lax
from jax.experimental import pallas as pl
from jax.experimental.pallas import tpu as pltpu
from jax.sharding import PartitionSpec as P

MESH = pl.DeviceIdType.MESH
HEAD = 128
EPSILON = 1e-06
THETA = 1000000.0
BF16, F32 = jnp.bfloat16, jnp.float32
FACTOR = 1.0 / math.sqrt(HEAD)
ANY = pl.BlockSpec(memory_space=pl.ANY)
VM = pl.BlockSpec(memory_space=pltpu.VMEM)
DMA = pltpu.SemaphoreType.DMA


def fid(zl, y, k):
    return zl * 8 + y * 2 + k


class Net:
    def __init__(self):
        f, c = lax.axis_index("fsdp"), lax.axis_index("ctx")
        zl, y, k, zh, x = f // 8, (f // 2) % 4, f % 2, c // 4, c % 4
        self.zl, self.y, self.k, self.zh, self.x = zl, y, k, zh, x
        self.z = zh * 2 + zl
        self.f, self.c = f, c
        self.yp, self.ym = self.along("y", 1), self.along("y", 3)
        self.zp, self.zm = self.along("z", 1), self.along("z", 3)
        self.xp, self.xm = self.along("x", 1), self.along("x", 3)
        self.pair = (fid(1 - zl, y, k), c)
        self.sib = (fid(zl, y, 1 - k), c)
        self.peer_c = (1 - zh) * 4 + x
        self.peer = (f, self.peer_c)

    def at(self, dim):
        return {"y": self.y, "x": self.x, "z": self.z}[dim]

    def along(self, dim, off):
        there = (self.at(dim) + off) % 4
        if dim == "y":
            return (fid(self.zl, there, self.k), self.c)
        if dim == "x":
            return (self.f, self.zh * 4 + there)
        return (fid(there % 2, self.y, self.k), (there // 2) * 4 + self.x)

    def ctx(self, off):
        return (self.c + off) % 8


def barrier(devices):
    sem = pltpu.get_barrier_semaphore()
    for d in devices:
        pl.semaphore_signal(sem, inc=1, device_id=d, device_id_type=MESH)
    pl.semaphore_wait(sem, len(devices))


class Copy:
    def __init__(self, copy, made_by):
        self.copy, self.made_by = copy, made_by
        if not made_by.again:
            copy.start()

    def wait_recv(self):
        if not self.made_by.again:
            self.copy.wait_recv()

    def wait(self):
        if not self.made_by.again:
            self.copy.wait()


class Wire:
    def __init__(self, send, recv, again=False):
        self.send, self.recv, self.n, self.all, self.again = send, recv, 0, [], again

    def __call__(self, src, dst, device):
        i = self.n
        self.n += 1
        copy = pltpu.make_async_remote_copy(
            src_ref=src, dst_ref=dst, send_sem=self.send.at[i], recv_sem=self.recv.at[i],
            device_id=device, device_id_type=MESH)
        self.all.append(copy)
        return Copy(copy, self)

    def finish(self):
        for copy in self.all:
            copy.wait_send()


class Local:
    def __init__(self, sems, again=False):
        self.sems, self.n, self.again = sems, 0, again

    def __call__(self, src, dst):
        i = self.n
        self.n += 1
        return Copy(None if self.again else pltpu.make_async_copy(src, dst, self.sems.at[i]), self)


def sems(wires, local):
    return [DMA((wires,)), DMA((wires,)), DMA((local,))]


def talking(number, name, **more):
    return dict(
        compiler_params=pltpu.CompilerParams(
            collective_id=number, has_side_effects=True, vmem_limit_bytes=63 << 20),
        name=name, **more)
def quarters(rows):
    if rows % 64 == 0:
        q = rows // 4
        return (0, q, 2 * q, 3 * q, rows)
    return (0, 16, 32, 48, rows)


class WeightFlow:
    def __init__(self, net, wire, src, out, paired=False):
        self.net, self.wire, self.src, self.out = net, wire, src, out
        self.zp, self.zm = (net.pair, net.pair) if paired else (net.zp, net.zm)
        self.rows = src.shape[0]
        self.q = quarters(self.rows)
        self.c = {}

    def place(self, dz, dy, a=0, b=4):
        n = self.net
        zl = n.zl if dz == 0 else 1 - n.zl
        at = fid(zl, (n.y + dy + 4) % 4, n.k) * self.rows + self.q[a]
        return self.out.at[pl.ds(pl.multiple_of(at, 16), self.q[b] - self.q[a])]

    def own(self, a=0, b=4):
        return self.src.at[pl.ds(self.q[a], self.q[b] - self.q[a])]

    def pass_on(self, name, device, dz, dy, a=0, b=4):
        ref = self.place(dz, dy, a, b)
        self.c[name] = self.wire(ref, ref, device)

    def got(self, name):
        self.c[name].wait_recv()

    def stage(self, s):
        n, w, c = self.net, self.wire, self.c
        if s == 0:
            c["yp"] = w(self.own(), self.place(0, 0), n.yp)
            c["ym"] = w(self.own(), self.place(0, 0), n.ym)
            c["zp"] = w(self.own(0, 2), self.place(0, 0, 0, 2), self.zp)
            c["zm"] = w(self.own(2, 4), self.place(0, 0, 2, 4), self.zm)
            c["d"] = w(self.own(), self.place(0, 0), n.sib)
        elif s == 1:
            self.got("yp")
            self.pass_on("yp2", n.yp, 0, -1, 0, 2)
            self.pass_on("zp_m", self.zp, 0, -1, 0, 2)
            self.pass_on("zm_m", self.zm, 0, -1, 2, 4)
            self.pass_on("d_m", n.sib, 0, -1)
            self.got("ym")
            self.pass_on("ym2", n.ym, 0, 1, 2, 4)
            self.pass_on("zp_p", self.zp, 0, 1, 0, 2)
            self.pass_on("zm_p", self.zm, 0, 1, 2, 4)
            self.pass_on("d_p", n.sib, 0, 1)
            self.got("zp")
            self.pass_on("dz0", n.sib, 1, 0, 0, 2)
            self.got("zm")
            self.pass_on("dz1", n.sib, 1, 0, 2, 4)
        elif s == 2:
            self.got("yp2")
            self.pass_on("zp_2", self.zp, 0, 2, 0, 1)
            self.pass_on("d2a", n.sib, 0, 2, 0, 2)
            self.got("ym2")
            self.pass_on("zm_2", self.zm, 0, 2, 2, 3)
            self.pass_on("d2b", n.sib, 0, 2, 2, 4)
            self.got("zp_m")
            self.pass_on("yq", n.yp, 1, -1, 1, 2)
            self.pass_on("dzm0", n.sib, 1, -1, 0, 2)
            self.got("zm_p")
            self.pass_on("yr", n.ym, 1, 1, 3, 4)
            self.pass_on("dzp1", n.sib, 1, 1, 2, 4)
            self.got("zm_m")
            self.pass_on("dzm1", n.sib, 1, -1, 2, 4)
            self.got("zp_p")
            self.pass_on("dzp0", n.sib, 1, 1, 0, 2)
        elif s == 3:
            self.got("zp_2")
            self.got("yq")
            self.pass_on("dz20", n.sib, 1, 2, 0, 2)
            self.got("zm_2")
            self.got("yr")
            self.pass_on("dz21", n.sib, 1, 2, 2, 4)
        elif s == 4:
            for name in ("d", "d_m", "d_p", "dz0", "dz1", "d2a", "d2b", "dzm0", "dzp1", "dzm1", "dzp0", "dz20", "dz21"):
                self.got(name)


class SharedFlow(WeightFlow):
    def quarter(self, dz, dy, hi, own=False):
        n, q = self.net, self.rows // 4
        zl = n.zl if dz == 0 else 1 - n.zl
        at = (2 * hi + n.x % 2) * q
        if own:
            return self.src.at[pl.ds(pl.multiple_of(at, 16), q)]
        return self.out.at[pl.ds(pl.multiple_of(fid(zl, (n.y + dy + 4) % 4, n.k) * self.rows + at, 16), q)]

    def hand(self, name, device, dz, dy, hi):
        ref = self.quarter(dz, dy, hi)
        self.c[name] = self.wire(ref, ref, device)

    def along_z(self, tag, dy):
        self.hand("zp" + tag, self.zp, 0, dy, 0)
        self.hand("zm" + tag, self.zm, 0, dy, 1)

    def along_x(self, tag, dy):
        self.got("zp" + tag)
        self.hand("xp" + tag, self.net.xp, 1, dy, 0)
        self.got("zm" + tag)
        self.hand("xm" + tag, self.net.xm, 1, dy, 1)

    def to_sibling(self, tag, dy):
        self.got("xp" + tag)
        self.got("xm" + tag)
        self.pass_on("dz" + tag, self.net.sib, 1, dy)

    def stage(self, s):
        n, w, c = self.net, self.wire, self.c
        if s == 0:
            c["yp"] = w(self.own(), self.place(0, 0), n.yp)
            c["ym"] = w(self.own(), self.place(0, 0), n.ym)
            c["zp0"] = w(self.quarter(0, 0, 0, True), self.quarter(0, 0, 0), self.zp)
            c["zm0"] = w(self.quarter(0, 0, 1, True), self.quarter(0, 0, 1), self.zm)
            c["d"] = w(self.own(), self.place(0, 0), n.sib)
        elif s == 1:
            self.got("yp")
            self.pass_on("yp2", n.yp, 0, -1, 0, 2)
            self.along_z("m", -1)
            self.pass_on("d_m", n.sib, 0, -1)
            self.got("ym")
            self.pass_on("ym2", n.ym, 0, 1, 2, 4)
            self.along_z("p", 1)
            self.pass_on("d_p", n.sib, 0, 1)
            self.along_x("0", 0)
        elif s == 2:
            self.got("yp2")
            self.hand("zp2", self.zp, 0, 2, 0)
            self.pass_on("d2a", n.sib, 0, 2, 0, 2)
            self.got("ym2")
            self.hand("zm2", self.zm, 0, 2, 1)
            self.pass_on("d2b", n.sib, 0, 2, 2, 4)
            self.along_x("m", -1)
            self.along_x("p", 1)
            self.to_sibling("0", 0)
        elif s == 3:
            self.along_x("2", 2)
            self.to_sibling("m", -1)
            self.to_sibling("p", 1)
        elif s == 4:
            self.to_sibling("2", 2)
            for name in ("d", "d_m", "d_p", "d2a", "d2b", "dz0", "dzm", "dzp", "dz2"):
                self.got(name)


class RowFlow:
    def __init__(self, net, wire, src, out):
        self.net, self.wire, self.src, self.out = net, wire, src, out
        self.rows = src.shape[0]
        self.c = {}

    def place(self, ctx, a=0, b=2):
        lo, hi = a * self.rows // 2, b * self.rows // 2
        return self.out.at[pl.ds(pl.multiple_of(ctx * self.rows + lo, 16), hi - lo)]

    def pass_on(self, name, device, ctx, a=0, b=2):
        ref = self.place(ctx, a, b)
        self.c[name] = self.wire(ref, ref, device)

    def got(self, name):
        self.c[name].wait_recv()

    def stage(self, s):
        n, w, c = self.net, self.wire, self.c
        left, right = n.zh * 4 + (n.x + 3) % 4, n.zh * 4 + (n.x + 1) % 4
        left2, right2 = (1 - n.zh) * 4 + (n.x + 3) % 4, (1 - n.zh) * 4 + (n.x + 1) % 4
        if s == 0:
            c["pz"] = w(self.src, self.place(n.c), n.peer)
            c["xp"] = w(self.src, self.place(n.c), n.xp)
            c["xm"] = w(self.src, self.place(n.c), n.xm)
        elif s == 1:
            self.got("pz")
            self.pass_on("px", n.xp, n.peer_c)
            self.pass_on("pxm", n.xm, n.peer_c)
            self.got("xp")
            self.pass_on("xp2", n.xp, left, 0, 1)
            self.got("xm")
            self.pass_on("xm2", n.xm, right, 1, 2)
        elif s == 2:
            self.got("px")
            self.pass_on("px2", n.xp, left2, 0, 1)
            self.got("pxm")
            self.pass_on("pxm2", n.xm, right2, 1, 2)
        elif s == 3:
            for name in ("xp2", "xm2", "px2", "pxm2"):
                self.got(name)


class Later:
    def __init__(self, steps):
        self.steps = list(steps)

    def __call__(self):
        if self.steps:
            self.steps.pop(0)()

    def rest(self):
        while self.steps:
            self()


def stage(flow, *numbers):
    def go():
        for s in numbers:
            flow.stage(s)
    return go


def together(*steps):
    def go():
        for s in steps:
            s()
    return go


class Spread:
    def __init__(self, net, wire, here, forward, src, dst):
        rows, cols = (dst.shape[0], src.shape[1]) if forward else (src.shape[0], dst.shape[1])

        def by_row(ref, c):
            return ref.at[pl.ds(pl.multiple_of(c * rows, 16), rows)]

        def by_col(ref, c):
            return ref.at[:, pl.ds(pl.multiple_of(c * cols, 128), cols)]

        pick, put = (by_row, by_col) if forward else (by_col, by_row)
        self.copies = []
        for o in (6, 2, 4, 5, 7, 1, 3):
            there = net.ctx(o)
            self.copies.append(wire(pick(src, there), put(dst, net.c), (net.f, there)))
        self.own = here(pick(src, net.c), put(dst, net.c))

    def end(self):
        for copy in self.copies:
            copy.wait_recv()
        self.own.wait()


def neighbours(net):
    return ([net.sib] + [net.along(d, o) for d in "yz" for o in (1, 2, 3)] + [(net.f, net.ctx(o)) for o in (1, 2, 3, 5, 6, 7)])


KEPT = 11


def forward_kernel(nw, *refs):
    srcs, rows, cos_in, sin_in = refs[:nw], refs[nw], refs[nw + 1], refs[nw + 2]
    refs = refs[nw + 3:]
    outs, rows_out, own_heads, kept_out = refs[:nw - 1], refs[nw - 1], refs[nw], refs[nw + 1:nw + 1 + KEPT]
    refs = refs[nw + 1 + KEPT:]
    x, t, cos_at, sin_at, heads = refs[:5]
    kept = refs[5:5 + KEPT]
    send, recv, local = refs[5 + KEPT:]
    w, gains, q, k, v, lin, cs, sn, start, hf, inv = kept
    net, wire, here = Net(), Wire(send, recv), Local(local)
    barrier(neighbours(net))
    first, out_f, gate_f, up_f, down_f = [
        kind(net, wire, s, o, i == 0)
        for i, (kind, s, o) in enumerate(zip((WeightFlow, WeightFlow, WeightFlow, SharedFlow, SharedFlow), srcs, (t, *outs)))]
    flows = (first, out_f, gate_f, up_f, down_f)
    seq = RowFlow(net, wire, rows, x)
    first.stage(0)
    seq.stage(0)
    out_f.stage(0)
    gate_f.stage(0)
    tables_in = [here(cos_in, cos_at), here(sin_in, sin_at)]
    placed_here = [here(fl.src, fl.place(0, 0)) for fl in flows]
    placed_here.append(here(rows, seq.place(net.c)))
    first.stage(1)
    out_f.stage(1)
    up_f.stage(0)
    first.stage(2)
    seq.stage(1)
    gate_f.stage(1)
    down_f.stage(0)
    first.stage(3)
    out_f.stage(2)
    seq.stage(2)
    up_f.stage(1)
    first.stage(4)
    gate_f.stage(2)
    seq.stage(3)
    for c in tables_in + placed_here:
        c.wait()
    saved = [here(x, rows_out)]
    tick = Later([
        together(stage(down_f, 1), stage(out_f, 3)),
        stage(up_f, 2),
        stage(gate_f, 3),
        stage(down_f, 2),
        stage(up_f, 3),
        stage(down_f, 3),
    ])
    attn_forward(tick, x, t, cos_at, sin_at, w, gains, q, k, v, lin, cs, sn, start, hf, heads, inv)
    spread = Spread(net, wire, here, True, heads, own_heads)
    saved += [here(a, b) for a, b in zip(kept, kept_out)]
    tick.rest()
    for fl in flows[1:]:
        fl.stage(4)
    spread.end()
    for c in saved:
        c.wait()
    wire.finish()


def shapes(*items):
    return [jax.ShapeDtypeStruct(s, d) for s, d in items]


def forward(weights, rows, cos_in, sin_in):
    nw = len(weights)
    per, cols = weights[0].shape
    length = 8 * rows.shape[0]
    kept = shapes(
        ((16 * (per - 16), cols), BF16), ((16, cols), F32), ((2, length, HEAD), BF16), ((length, HEAD), BF16),
        ((length, HEAD), BF16), ((length, 3 * HEAD), F32), ((length, HEAD), F32), ((length, HEAD), F32),
        ((length, HEAD), F32), ((length, 2 * HEAD), F32), ((2, length, HEAD), F32))
    outs = [jax.ShapeDtypeStruct((16 * w.shape[0], w.shape[1]), w.dtype) for w in weights[1:]]
    outs += shapes(((length, rows.shape[1]), BF16), ((rows.shape[0], 16 * HEAD), BF16)) + kept
    scratch = [((length, rows.shape[1]), BF16), ((16 * per, cols), BF16), ((length, HEAD), F32), ((length, HEAD), F32), ((length, 2 * HEAD), BF16)]
    res = pl.pallas_call(
        functools.partial(forward_kernel, nw),
        out_shape=outs, in_specs=[ANY] * (nw + 3), out_specs=[ANY] * len(outs),
        scratch_shapes=[pltpu.VMEM(s, d) for s, d in scratch] + [pltpu.VMEM(a.shape, a.dtype) for a in kept]
        + sems(29 * nw + 9 + 7, nw + 3 + 1 + 1 + KEPT), **talking(0, "layer_forward"),
    )(*weights, rows, cos_in, sin_in)
    return res[:nw - 1], res[nw - 1], res[nw], res[nw + 1:]
def block(i, size):
    return pl.ds(pl.multiple_of(i * size, size), size)


def dot_t(left, right):
    return lax.dot_general(left, right, (((1,), (1,)), ((), ())), preferred_element_type=F32)


def t_dot(left, right):
    return lax.dot_general(left, right, (((0,), (0,)), ((), ())), preferred_element_type=F32)


def plain_dot(left, right):
    return jnp.dot(left, right, preferred_element_type=F32)


def unit(v):
    r = lax.rsqrt(jnp.mean(v * v, axis=-1, keepdims=True) + EPSILON)
    return v * r, r


ROWS = 256


def attn_forward(tick, x, t, cos_in, sin_in, w, gains, q, k, v, lin, cs, sn, start, hf, heads, inv):
    length, width = x.shape[0], x.shape[1] - HEAD
    per = t.shape[0] // 16
    depth = per - 16
    total = jnp.zeros((16, t.shape[1]), F32)
    for f in range(16):
        w[f * depth:(f + 1) * depth, :] = t[f * per:f * per + depth, :]
        total = total + t[f * per + depth:(f + 1) * per, :].astype(F32)
    gains[...] = total
    attn_gain = jnp.concatenate([total[0:1], total[1:2]], axis=1)
    query_gain, key_gain = total[4:5, 0:HEAD], total[4:5, HEAD:2 * HEAD]

    def count(i, carry):
        doc = x[block(i, ROWS), width:].astype(F32)
        return (carry[0] + jnp.sum((doc < 0.5).astype(F32), axis=0, keepdims=True),
                carry[1] + jnp.sum((doc < 1.5).astype(F32), axis=0, keepdims=True))

    zero = jnp.zeros((1, HEAD), F32)
    first, second = lax.fori_loop(0, length // ROWS, count, (zero, zero))
    lanes = lax.broadcasted_iota(jnp.int32, (1, HEAD), 1) % (HEAD // 2)
    freqs = jnp.exp(lanes.astype(F32) * (-2.0 * math.log(THETA) / HEAD))
    c1, s1 = jnp.cos(first * freqs), jnp.sin(first * freqs)
    c2, s2 = jnp.cos(second * freqs), jnp.sin(second * freqs)
    sign = jnp.where(lax.broadcasted_iota(jnp.int32, (1, HEAD), 1) < HEAD // 2, -1.0, 1.0)

    def prepare(i, carry):
        rows = block(i, ROWS)
        doc = x[rows, width:].astype(F32)
        start[rows, :] = jnp.where(doc < 0.5, 0.0, jnp.where(doc < 1.5, first, second))
        cd = jnp.where(doc < 0.5, 1.0, jnp.where(doc < 1.5, c1, c2))
        sd = jnp.where(doc < 0.5, 0.0, jnp.where(doc < 1.5, s1, s2))
        ci, si = cos_in[rows, :], sin_in[rows, :]
        cosine = ci * cd + si * sd
        sine = (si * cd - ci * sd) * sign
        cs[rows, :] = cosine
        sn[rows, :] = sine
        normed = (unit(x[rows, :width].astype(F32))[0] * attn_gain).astype(BF16)
        out = plain_dot(normed, w[...])
        lin[rows, :] = out[:, :3 * HEAD]
        v[rows, :] = out[:, 3 * HEAD:].astype(BF16)
        for h in range(3):
            e = unit(out[:, h * HEAD:(h + 1) * HEAD])[0] * (query_gain if h < 2 else key_gain)
            e = (e * cosine + pltpu.roll(e, HEAD // 2, 1) * sine).astype(BF16)
            if h < 2:
                q[h, rows, :] = e
            else:
                k[rows, :] = e
        return carry

    for i in range(0, length // ROWS, 2):
        lax.fori_loop(i, i + 2, prepare, 0)
        tick()

    def queries(i, carry):
        rows = block(i, ROWS)
        here = q[:, rows, :].reshape(2 * ROWS, HEAD)
        begin = start[rows, :]

        def keys(j, state):
            acc, norm = state
            these = block(j, ROWS)
            p = jnp.exp(dot_t(here, k[these, :]) * FACTOR)
            p = jnp.where(allowed_at(i, j, begin), p.reshape(2, ROWS, ROWS), 0.0).reshape(2 * ROWS, ROWS)
            norm = norm + p[:, :HEAD] + p[:, HEAD:]
            return acc + plain_dot(p.astype(BF16), v[these, :]), norm

        zeros = jnp.zeros((2 * ROWS, HEAD), F32)
        acc, norm = lax.fori_loop(0, i + 1, keys, (zeros, zeros))
        over = jnp.broadcast_to(1.0 / jnp.sum(norm, axis=1, keepdims=True), (2 * ROWS, HEAD))
        acc = acc * over
        inv[:, rows, :] = over.reshape(2, ROWS, HEAD)
        for h in range(2):
            part = acc[h * ROWS:(h + 1) * ROWS]
            hf[rows, h * HEAD:(h + 1) * HEAD] = part
            heads[rows, h * HEAD:(h + 1) * HEAD] = part.astype(BF16)
        return carry

    for i, j in ((0, 3), (3, 4), (4, 5), (5, 6)):
        lax.fori_loop(i, j, queries, 0)
        tick()


def allowed_at(i, j, begin):
    own = lax.broadcasted_iota(jnp.int32, (ROWS, ROWS), 0) + i * ROWS
    other = lax.broadcasted_iota(jnp.int32, (ROWS, ROWS), 1) + j * ROWS
    begin = jnp.concatenate([begin, begin], axis=1)
    return ((other.astype(F32) >= begin) & (other <= own))[None]


def attn_backward(tick, gains, q, k, v, start, hf, inv, dh, dq, dk, dv, delta):
    length = dh.shape[0]
    blocks = length // ROWS

    def before(i, carry):
        rows = block(i, ROWS)
        for h in range(2):
            cols = slice(h * HEAD, (h + 1) * HEAD)
            s = jnp.sum(dh[rows, cols].astype(F32) * hf[rows, cols], axis=1, keepdims=True)
            delta[h, rows, :] = jnp.broadcast_to(s, (ROWS, HEAD))
            dq[h, rows, :] = jnp.zeros((ROWS, HEAD), F32)
        return carry

    lax.fori_loop(0, blocks, before, 0)

    def keys(j, carry):
        these = block(j, ROWS)
        kt, vt = k[these, :], v[these, :]

        def queries(i, state):
            d_key, d_value = state
            rows = block(i, ROWS)
            here = q[:, rows, :].reshape(2 * ROWS, HEAD)
            grad = jnp.concatenate([dh[rows, :HEAD], dh[rows, HEAD:]], axis=0)
            over = inv[:, rows, :].reshape(2 * ROWS, HEAD)
            off = delta[:, rows, :].reshape(2 * ROWS, HEAD)
            over = jnp.concatenate([over, over], axis=1)
            off = jnp.concatenate([off, off], axis=1)
            p = jnp.exp(dot_t(here, kt) * FACTOR) * over
            p = jnp.where(allowed_at(i, j, start[rows, :]), p.reshape(2, ROWS, ROWS), 0.0).reshape(2 * ROWS, ROWS)
            ds = (p * (dot_t(grad, vt) - off)).astype(BF16)
            dq[:, rows, :] = dq[:, rows, :] + plain_dot(ds, kt).reshape(2, ROWS, HEAD)
            return d_key + t_dot(ds, here), d_value + t_dot(p.astype(BF16), grad)

        zeros = jnp.zeros((ROWS, HEAD), F32)
        d_key, d_value = lax.fori_loop(j, blocks, queries, (zeros, zeros))
        dk[these, :] = d_key
        dv[these, :] = d_value
        return carry

    for i, j in ((0, 1), (1, 2), (2, 4), (4, 6)):
        lax.fori_loop(i, j, keys, 0)
        tick()


WIDE = 384


def attn_backward_end(x, w, gains, lin, cs, sn, dq, dk, dv, dlin, dw, dn):
    length, width = x.shape[0], x.shape[1] - HEAD
    g = gains[...]
    attn_gain = jnp.concatenate([g[0:1], g[1:2]], axis=1)
    query_gain, key_gain = g[4:5, 0:HEAD], g[4:5, HEAD:2 * HEAD]

    def after(i, carry):
        d_attn, d_query, d_key = carry
        rows = block(i, WIDE)
        cosine, sine = cs[rows, :], sn[rows, :]
        for h in range(3):
            cols = slice(h * HEAD, (h + 1) * HEAD)
            d = (dq[h, rows, :] if h < 2 else dk[rows, :]) * FACTOR
            d = d * cosine - pltpu.roll(d, HEAD // 2, 1) * sine
            e, r = unit(lin[rows, cols])
            s = jnp.sum(d * e, axis=0, keepdims=True)
            d_query, d_key = (d_query + s, d_key) if h < 2 else (d_query, d_key + s)
            d = d * (query_gain if h < 2 else key_gain)
            d = r * (d - e * jnp.mean(d * e, axis=-1, keepdims=True))
            dlin[rows, cols] = d.astype(BF16)
        dlin[rows, 3 * HEAD:] = dv[rows, :].astype(BF16)
        part = dot_t(dlin[rows, :], w[...])
        e = unit(x[rows, :width].astype(F32))[0]
        d_attn = d_attn + jnp.sum(part * e, axis=0, keepdims=True)
        dn[i // 2, pl.ds((i % 2) * 2, 2)] = part.astype(BF16).reshape(2, WIDE // 2, width)
        normed = (e * attn_gain).astype(BF16)

        part = t_dot(normed, dlin[rows, :])
        dw[...] = jnp.where(i == 0, part, dw[...] + part)
        return d_attn, d_query, d_key

    zero = jnp.zeros((1, HEAD), F32)
    dw[...] = jnp.zeros_like(dw)
    return lax.fori_loop(0, length // WIDE, after, (jnp.zeros((1, width), F32), zero, zero))


def shapes(*items):
    return [jax.ShapeDtypeStruct(s, d) for s, d in items]


def add_rows(out, parts, rows, step):
    def some(r, carry):
        here = pl.ds(pl.multiple_of(r * step, 16), step)
        if len(parts) == 2:
            out(here, parts[0](here) + parts[1](here))
            return carry
        total = parts[0](here).astype(F32)
        for part in parts[1:]:
            total = total + part(here).astype(F32)
        out(here, total.astype(BF16))
        return carry

    lax.fori_loop(0, rows // step, some, 0)


FIRST = (2, 1, 3, 0)


class SumFlow:
    def __init__(self, net, wire, here, src, first, order, slots, other, relay, got, part, fin, out):
        self.net, self.wire, self.here, self.src, self.first, self.order = net, wire, here, src, first, order
        self.slots, self.other, self.relay, self.got, self.part, self.fin, self.out = slots, other, relay, got, part, fin, out
        self.rows, self.cols = other.shape[2], other.shape[3]
        self.w = self.cols // 8
        self.far, self.via = {}, {}

    def cut(self, ref, dim, d, k=None):
        tail = ref.shape[-1]
        a = (slice(None), slice(None))
        cols = pl.ds(0, tail)
        if dim == "y":
            a = (slice(None), pl.ds(d, 1))
        elif dim == "x":
            cols = pl.ds(pl.multiple_of(d * (tail // 4), 128), tail // 4)
        else:
            a = (pl.ds(d % 2, 1), slice(None))
            cols = pl.ds(pl.multiple_of((d // 2) * (tail // 2), 128), tail // 2)
        if k is None:
            return ref.at[a[0], a[1], :, cols]
        return ref.at[a[0], a[1], k, pl.ds(self.first, self.rows), cols]

    def begin(self):
        self.near, self.own = {}, {}
        self.bring(0)
        self.bring(1)

    def bring(self, i):
        n, dim = self.net, self.order[0]
        o = FIRST[i]
        d = (n.at(dim) + o) % 4
        self.near[o] = self.wire(self.cut(self.src, dim, d, 1 - n.k), self.cut(self.other, dim, d), n.sib)
        self.own[o] = self.here(self.cut(self.src, dim, d, n.k), self.slots.at[i % 2])

    def add(self, out, parts):
        if self.wire.again:
            return
        a, b = out.shape[0], out.shape[1]
        step = 16
        for i in range(a):
            for j in range(b):
                def take(ref):
                    return lambda here: ref[i, j, here, :]

                def put(here, value):
                    out[i, j, here, :] = value
                add_rows(put, [take(p) for p in parts], out.shape[2], step)

    def chip(self, o):
        n, dim = self.net, self.order[0]
        d = (n.at(dim) + o) % 4
        self.near[o].wait_recv()
        self.own[o].wait()
        i = FIRST.index(o)
        piece = self.cut(self.other, dim, d)
        self.add(piece, [piece, self.slots.at[i % 2]])
        if i + 2 < 4:
            self.bring(i + 2)
        half = self.rows // 2
        if o == 2:
            for which, to in ((0, 1), (1, 3)):
                self.via[to] = self.wire(piece.at[:, :, pl.ds(which * half, half)], self.relay.at[which], n.along(dim, to))
        elif o:
            which = 0 if o == 1 else 1
            self.via[o].wait_recv()
            part = piece.at[:, :, pl.ds(which * half, half)]
            self.add(part, [part, self.relay.at[which]])
            self.far[o] = self.wire(piece, self.got[0].at[which], n.along(dim, o))

    def phase(self, p):
        n, dim = self.net, self.order[p]
        held = self.other if p == 0 else self.part[p - 1]
        for o in (1, 3, 2) if p else (1, 3):
            self.far[o].wait_recv()
        result = self.part[p] if p < 2 else self.fin
        self.add(result, [self.cut(held, dim, n.at(dim))] + [self.got[p].at[i] for i in range(3 if p else 2)])
        if p < 2:
            after = self.order[p + 1]
            for o in (2, 1, 3):
                d = (n.at(after) + o) % 4
                self.far[o] = self.wire(self.cut(result, after, d), self.got[p + 1].at[o - 1], n.along(after, o))
        else:
            fin, to = self.fin.at[0, 0], self.place(n.zh)
            self.across = self.wire(fin, to, n.peer)
            self.last = [self.wire(fin, to, n.along("x", o)) for o in (2, 1, 3)]
            self.kept = self.here(fin, to)

    def place(self, zh):
        n = self.net
        s = zh * 4 + n.x if self.order.index("z") < self.order.index("x") else n.x * 2 + zh
        return self.out.at[pl.ds(self.first, self.rows), pl.ds(pl.multiple_of(s * self.w, 128), self.w)]

    def share(self):
        n = self.net
        self.across.wait_recv()
        to = self.place(1 - n.zh)
        self.last += [self.wire(to, to, n.along("x", o)) for o in (2, 1, 3)]

    def end(self):
        for copy in self.last:
            copy.wait_recv()
        self.kept.wait()


def sum_shapes(rows, cols, order):
    shape, out = [2, 4, rows, cols], []
    for dim in order:
        if dim == "y":
            shape[1] = 1
        elif dim == "x":
            shape[3] //= 4
        else:
            shape[0], shape[3] = 1, shape[3] // 2
        out.append(tuple(shape))
    return out


PLAN = ((0, 0, 64, "yxz"), (1, 0, 64, "xzy"), (2, 0, 192, "zyx"), (3, 0, 64, "yzx"), (3, 64, 64, "yxz"))


def first_shapes(plan, shapes_in):
    return [sum_shapes(rows, shapes_in[which][-1], order)[0] for which, _, rows, order in plan]


def sum_scratch(plan, shapes_in):
    held = []
    for which, first, rows, order in plan:
        cols = shapes_in[which][-1]
        a, b, c = sum_shapes(rows, cols, order)
        half = (a[0], a[1], a[2] // 2, a[3])
        held += [pltpu.VMEM(s, BF16) for s in ((2, 4, rows, cols), (2, *half), (2, *a), (3, *b), (3, *c), a, b, c)]
    return held


def make_flows(net, wire, here, plan, srcs, outs, held, slots):
    flows = []
    for n, (which, first, rows, order) in enumerate(plan):
        other, relay, g0, g1, g2, p0, p1, fin = held[8 * n:8 * n + 8]
        flows.append(SumFlow(net, wire, here, srcs[which], first, order, slots[n], other, relay, (g0, g1, g2), (p0, p1), fin, outs[which]))
    return flows


class Ends:
    def __init__(self, net, wire, here, dwx, dn, rows_out, dn_out, other, got, fin, got_xa, part_a, got_za, got_zb, part_b, got_xb):
        self.net, self.wire, self.here, self.dwx, self.dn, self.rows_out, self.dn_out = net, wire, here, dwx, dn, rows_out, dn_out
        self.other, self.got, self.fin = other, got, fin
        self.got_xa, self.part_a, self.got_za, self.got_zb, self.part_b, self.got_xb = got_xa, part_a, got_za, got_zb, part_b, got_xb
        self.half = part_a.shape[-1]
        self.rows = part_a.shape[1]

    def begin(self):
        n, h = self.net, self.half
        self.over_b = self.wire(self.dn.at[1 - n.zh, :, :, pl.ds(h, h)], self.got_zb, n.peer)
        self.moved_a = [self.wire(self.dn.at[:, (n.x + o) % 4, :, pl.ds(0, h)], self.got_xa.at[o - 1], n.along("x", o)) for o in (2, 1, 3)]
        self.near = self.wire(self.dwx.at[:, :, 1 - n.k], self.other, n.sib)

    def chip(self):
        n = self.net
        self.near.wait_recv()
        for a in range(2):
            for b in range(4):
                self.other[a, b] = self.other[a, b] + self.dwx[a, b, n.k]
        self.far = []
        for dz in (1, 0):
            for dy in (2, 1, 3, 0):
                if dz or dy:
                    there = ((n.zl + dz) % 2, (n.y + dy) % 4)
                    self.far.append(self.wire(self.other.at[there[0], there[1]], self.got.at[dz * 4 + dy - 1], (fid(there[0], there[1], n.k), n.c)))

    def along_z(self):
        n, h = self.net, self.half
        self.over_b.wait_recv()
        for x in range(4):
            def put(here, value):
                self.part_b[x, here, :] = value
            add_rows(put, [lambda here: self.dn[n.zh, x, here, h:], lambda here: self.got_zb[x, here, :]], self.rows, 16)
        self.moved_b = [self.wire(self.part_b.at[(n.x + o) % 4], self.got_xb.at[o - 1], n.along("x", o)) for o in (2, 1, 3)]

    def along_x(self):
        n, h = self.net, self.half
        for copy in self.moved_a:
            copy.wait_recv()
        for zh in range(2):
            def take(o):
                return (lambda here: self.dn[zh, n.x, here, :h]) if o == 0 else (lambda here: self.got_xa[o - 1, zh, here, :])

            def put(here, value):
                self.part_a[zh, here, :] = value
            add_rows(put, [take(o) for o in range(4)], self.rows, 16)
        self.over_a = self.wire(self.part_a.at[1 - n.zh], self.got_za, n.peer)

    def share(self):
        n = self.net
        for copy in self.far:
            copy.wait_recv()
        total = self.other[n.zl, n.y].astype(F32)
        for i in range(7):
            total = total + self.got[i].astype(F32)
        self.fin[...] = total.astype(BF16)
        self.copies = [self.wire(self.fin, self.rows_out.at[n.c], (n.f, n.ctx(o))) for o in (6, 2, 4, 5, 7, 1, 3)]
        self.kept = self.here(self.fin, self.rows_out.at[n.c])

    def end(self):
        n, h = self.net, self.half
        self.over_a.wait_recv()
        for copy in self.moved_b:
            copy.wait_recv()

        def some(r, carry):
            at = pl.ds(pl.multiple_of(r * 16, 16), 16)
            self.dn_out[at, :h] = self.part_a[n.zh, at, :].astype(F32) + self.got_za[at, :].astype(F32)
            total = self.part_b[n.x, at, :].astype(F32)
            for o in range(3):
                total = total + self.got_xb[o, at, :].astype(F32)
            self.dn_out[at, h:] = total
            return carry

        lax.fori_loop(0, self.rows // 16, some, 0)
        for copy in self.copies:
            copy.wait_recv()
        self.kept.wait()


def backward_kernel(ng, *refs):
    srcs, x_in, d_heads, mlp_rows, kept_in = refs[:ng], refs[ng], refs[ng + 1], refs[ng + 2], refs[ng + 3:ng + 3 + KEPT]
    refs = refs[ng + 3 + KEPT:]
    outs, rows_out, dn_out = refs[:ng], refs[ng], refs[ng + 1]
    refs = refs[ng + 2:]
    kept, refs = refs[:KEPT], refs[KEPT:]
    w, gains, q, k, v, lin, cs, sn, start, hf, inv = kept
    dh, dq, dk, dv, delta, mlp_at, dwx, dn = refs[:8]
    end_held, refs = refs[8:17], refs[17:]
    held, (send, recv, local) = refs[:-3], refs[-3:]
    net = Net()
    length, width = x_in.shape[0], x_in.shape[1] - HEAD
    depth = w.shape[0] // 16

    def opening(wire, here, slots):
        spread = Spread(net, wire, here, False, d_heads, dh)
        flows = make_flows(net, wire, here, PLAN, srcs, outs, held, slots)
        for fl in flows:
            fl.begin()
        loads = [here(a, b) for a, b in zip(kept_in, kept)] + [here(mlp_rows, mlp_at)]

        def chips(o):
            def go():
                for fl in flows:
                    fl.chip(o)
            return go

        chips(2)()
        return spread, loads, Later([chips(1), chips(3), chips(0)]), flows

    def slotted(*slots):
        barrier(neighbours(net))
        spread, loads, tick, _ = opening(Wire(send, recv), Local(local), slots)
        for c in loads:
            c.wait()
        spread.end()
        attn_backward(tick, gains, q, k, v, start, hf, inv, dh, dq, dk, dv, delta)
        tick.rest()

    pl.run_scoped(slotted, *[pltpu.VMEM((2, *a), BF16) for a in first_shapes(PLAN, [s.shape for s in srcs])])
    wire, here = Wire(send, recv, True), Local(local, True)
    _, _, tick, flows = opening(wire, here, held[2::8])
    tick.rest()
    wire.again = here.again = False
    ends = Ends(net, wire, here, dwx, dn, rows_out, dn_out, *end_held)

    def ending(x, dlin, dw):
        fetch = pltpu.make_async_copy(x_in, x, local.at[local.shape[0] - 1])
        fetch.start()
        fetch.wait()
        d_attn, d_query, d_key = attn_backward_end(x, w, gains, lin, cs, sn, dq, dk, dv, dlin, dw, dn)
        cols = dw.shape[1]
        lanes = jnp.concatenate([d_query, d_key, jnp.zeros((1, cols - 2 * HEAD), F32)], axis=1)
        small = jnp.concatenate([d_attn[:, :cols], d_attn[:, cols:], jnp.zeros((2, cols), F32), lanes, jnp.zeros((11, cols), F32)], axis=0)
        small = (small + mlp_at[...]).astype(BF16)
        for f in range(16):
            at = (f // 8, (f // 2) % 4, f % 2)
            dwx[at[0], at[1], at[2], :depth, :] = dw[f * depth:(f + 1) * depth, :].astype(BF16)
            dwx[at[0], at[1], at[2], depth:, :] = small

    def phase(p):
        for fl in flows:
            fl.phase(p)

    def share():
        for fl in flows:
            fl.share()

    pl.run_scoped(ending, pltpu.VMEM((length, width + HEAD), BF16), pltpu.VMEM((length, 4 * HEAD), BF16), pltpu.VMEM((16 * depth, 4 * HEAD), F32))
    ends.begin()
    phase(0)
    phase(1)
    ends.chip()
    ends.along_z()
    ends.along_x()
    phase(2)
    ends.share()
    share()
    ends.end()
    for fl in flows:
        fl.end()
    wire.finish()


def backward(grads, x, d_heads, mlp_rows, kept):
    srcs = [g.reshape(2, 4, 2, g.shape[0] // 16, g.shape[1]) for g in grads]
    length, width = x.shape[0], x.shape[1] - HEAD
    rows, cols = length // 8, 4 * HEAD
    depth, half = width // 16, width // 2
    out = [jax.ShapeDtypeStruct((g.shape[0] // 16, g.shape[1]), BF16) for g in grads]
    out += shapes(((8, depth + 16, cols), BF16), ((rows, width), F32))
    scratch = [(a.shape, a.dtype) for a in kept]
    scratch += [((length, 2 * HEAD), BF16), ((2, length, HEAD), F32), ((length, HEAD), F32), ((length, HEAD), F32),
                ((2, length, HEAD), F32), (mlp_rows.shape, F32), ((2, 4, 2, depth + 16, cols), BF16), ((2, 4, rows, width), BF16)]
    scratch += [((2, 4, depth + 16, cols), BF16), ((7, depth + 16, cols), BF16), ((depth + 16, cols), BF16),
                ((3, 2, rows, half), BF16), ((2, rows, half), BF16), ((rows, half), BF16),
                ((4, rows, half), BF16), ((4, rows, half), BF16), ((3, rows, half), BF16)]
    ng = len(grads)
    wires = 21 * len(PLAN) + 7 + 3 + 1 + 3 + 1 + 7 + 1 + 7
    local = 5 * len(PLAN) + 1 + KEPT + 1 + 1 + 1
    res = pl.pallas_call(
        functools.partial(backward_kernel, ng), out_shape=out,
        in_specs=[ANY] * (ng + 3 + KEPT), out_specs=[ANY] * (ng + 1) + [VM],
        scratch_shapes=[pltpu.VMEM(s, d) for s, d in scratch] + sum_scratch(PLAN, [s.shape for s in srcs]) + sems(wires, local),
        **talking(1, "layer_backward"))(*srcs, x, d_heads, mlp_rows, *kept)
    return res[:ng], res[ng], res[ng + 1]
CHUNK = 384


def mlp_kernel(steps, x, heads, g, gains, wo, wg, wu, wd, out, d_hidden, d_heads, rows_out, dg, du, dd, do, hidden, mixed, mixed_t, acc, d_mixed):
    step = pl.program_id(0)
    width = x.shape[1]
    gain = jnp.concatenate([gains[2:3], gains[3:4]], axis=1)

    @pl.when(step == 0)
    def _():
        h = x[...].astype(F32) + plain_dot(heads[...], wo[...])
        hidden[...] = h
        m = unit(h)[0] * gain
        mixed[...] = m.astype(BF16)
        mixed_t[...] = m.T.astype(BF16)
        acc[...] = h
        d_mixed[...] = jnp.zeros_like(d_mixed)

    m, grad = mixed[...], g[...]
    gate, upward = plain_dot(m, wg[...]), plain_dot(m, wu[...])
    s = jax.nn.sigmoid(gate)
    act = gate * s
    active = (act * upward).astype(BF16)
    acc[...] += plain_dot(active, wd[...])
    d_active = dot_t(grad, wd[...])
    dd[...] = t_dot(active, grad).astype(BF16)
    d_up = (d_active * act).astype(BF16)
    d_gate = (d_active * upward * (s + act * (1.0 - s))).astype(BF16)
    dg[...] = plain_dot(mixed_t[...], d_gate).astype(BF16)
    du[...] = plain_dot(mixed_t[...], d_up).astype(BF16)
    d_mixed[...] += dot_t(d_gate, wg[...]) + dot_t(d_up, wu[...])

    @pl.when(step == steps - 1)
    def _():
        out[...] = acc[...].astype(BF16)
        e, r = unit(hidden[...])
        d = d_mixed[...]
        d_gain = jnp.sum(d * e, axis=0, keepdims=True)
        d = d * gain
        d = g[...].astype(F32) + r * (d - e * jnp.mean(d * e, axis=-1, keepdims=True))
        d_hidden[...] = d
        low = d.astype(BF16)
        d_heads[...] = dot_t(low, wo[...]).astype(BF16)
        do[...] = t_dot(heads[...], low).astype(BF16)
        half = width // 2
        rows_out[...] = jnp.concatenate([jnp.zeros((2, half), F32), d_gain[:, :half], d_gain[:, half:], jnp.zeros((12, half), F32)], axis=0)


def mlp(x, heads, g, gains, wo, wg, wu, wd):
    rows, width = x.shape
    steps = wg.shape[1] // CHUNK
    whole = lambda a: pl.BlockSpec(a.shape, lambda i: (0,) * len(a.shape), pipeline_mode=pl.Buffered(1))
    fixed = lambda *s: pl.BlockSpec(s, lambda i: (0, 0))
    by_col = pl.BlockSpec((width, CHUNK), lambda i: (0, i))
    by_row = pl.BlockSpec((CHUNK, width), lambda i: (i, 0))
    out = shapes(((rows, width), BF16), ((rows, width), F32), (heads.shape, BF16), ((16, width // 2), F32),
                 (wg.shape, BF16), (wu.shape, BF16), (wd.shape, BF16), (wo.shape, BF16))
    return pl.pallas_call(
        functools.partial(mlp_kernel, steps), out_shape=out, grid=(steps,),
        in_specs=[whole(x), whole(heads), whole(g), whole(gains), whole(wo), by_col, by_col, by_row],
        out_specs=[fixed(rows, width), fixed(rows, width), fixed(*heads.shape), fixed(16, width // 2), by_col, by_col, by_row, fixed(*wo.shape)],
        scratch_shapes=[pltpu.VMEM((rows, width), F32), pltpu.VMEM((rows, width), BF16), pltpu.VMEM((width, rows), BF16),
                        pltpu.VMEM((rows, width), F32), pltpu.VMEM((rows, width), F32)],
        compiler_params=pltpu.CompilerParams(vmem_limit_bytes=56 << 20), name="mlp")(x, heads, g, gains, wo, wg, wu, wd)
def root_mean_norm(rows, scaling):
    return rows * lax.rsqrt(jnp.mean(rows * rows, axis=-1, keepdims=True) + EPSILON) * scaling


def tables(length):
    freqs = THETA ** (-np.arange(HEAD // 2, dtype=np.float64) * 2.0 / HEAD)
    angles = np.arange(length, dtype=np.float64)[:, None] * np.concatenate([freqs, freqs])[None, :]
    return jnp.asarray(np.cos(angles), F32), jnp.asarray(np.sin(angles), F32)


def placed(values, f):
    return jnp.where(jnp.arange(16)[:, None] == f, values[None, :], jnp.zeros((), BF16)).reshape(-1)


def body(inputs, doc_ids, query_proj, key_projection, value_projection, output_proj, gate_proj, up_proj, down_proj,
         attn_gain, mlp_gain, query_norm_gain, key_gain, out_grad):
    f, c = lax.axis_index("fsdp"), lax.axis_index("ctx")
    rows, width = inputs.shape[1:]
    depth = query_proj.shape[0]
    cols = 4 * HEAD
    own = jnp.concatenate([
        lax.dynamic_slice_in_dim(query_proj, c * 2 * HEAD, 2 * HEAD, 1),
        lax.dynamic_slice_in_dim(key_projection, c * HEAD, HEAD, 1),
        lax.dynamic_slice_in_dim(value_projection, c * HEAD, HEAD, 1)], axis=1)
    small = jnp.concatenate([
        placed(attn_gain, f), placed(mlp_gain, f), placed(query_norm_gain, f), placed(key_gain, f),
        jnp.zeros((16 * cols - 2 * width - 2 * HEAD,), BF16)]).reshape(16, cols)
    pack = jnp.concatenate([own, small], axis=0)
    sequence = jnp.concatenate([inputs[0], jnp.broadcast_to(doc_ids[0].astype(BF16)[:, None], (rows, HEAD))], axis=1)
    (full_output, full_gate, full_up, full_down), x, own_heads, kept = forward(
        [pack, output_proj, gate_proj, up_proj, down_proj], sequence, *tables(8 * rows))
    gains = kept[1]
    residual = inputs[0].astype(F32)
    outputs, d_hidden, d_heads, mlp_rows, *grads = mlp(
        inputs[0], own_heads, out_grad[0], gains, full_output, full_gate, full_up, full_down)
    (gate_g, up_g, down_g, output_g), back, d_normed = backward(grads, x, d_heads, mlp_rows, kept)
    _, norm_pull = jax.vjp(lambda r: root_mean_norm(r, gains[0:2].reshape(width)), residual)
    input_grad = d_hidden + norm_pull(d_normed)[0]
    back = back.astype(F32)
    query_g = jnp.moveaxis(back[:, :depth, :2 * HEAD], 0, 1).reshape(depth, -1)
    key_g = jnp.moveaxis(back[:, :depth, 2 * HEAD:3 * HEAD], 0, 1).reshape(depth, -1)
    value_g = jnp.moveaxis(back[:, :depth, 3 * HEAD:], 0, 1).reshape(depth, -1)
    small_g = jnp.sum(back[:, depth:, :], axis=0)

    def mine(values, size):
        return lax.dynamic_slice_in_dim(values, f * size, size)

    return (outputs[None], input_grad[None], query_g, key_g, value_g, output_g.astype(F32), gate_g.astype(F32),
            up_g.astype(F32), down_g.astype(F32), mine(small_g[0:2].reshape(width), depth), mine(small_g[2:4].reshape(width), depth),
            mine(small_g[4, :HEAD], HEAD // 16), mine(small_g[4, HEAD:2 * HEAD], HEAD // 16))


def solution(mesh):
    seq, weight, gain = P("fsdp", "ctx", None), P("fsdp", None), P("fsdp")
    in_specs = (seq, P("fsdp", "ctx")) + (weight,) * 7 + (gain,) * 4 + (seq,)
    out_specs = (seq, seq) + (weight,) * 7 + (gain,) * 4
    return jax.shard_map(body, mesh=mesh, in_specs=in_specs, out_specs=out_specs, check_vma=False)
```

```python
import functools
import math

import jax
import jax.numpy as jnp
import numpy as np
from jax import lax
from jax.experimental import pallas as pl
from jax.experimental.pallas import tpu as pltpu
from jax.sharding import PartitionSpec as P

MESH = pl.DeviceIdType.MESH
HEAD = 128
EPSILON = 1e-06
THETA = 1000000.0
BF16, F32 = jnp.bfloat16, jnp.float32
FACTOR = 1.0 / math.sqrt(HEAD)
ANY = pl.BlockSpec(memory_space=pl.ANY)
VM = pl.BlockSpec(memory_space=pltpu.VMEM)
DMA = pltpu.SemaphoreType.DMA


def fid(zl, y, k):
    return zl * 8 + y * 2 + k


class Net:
    def __init__(self):
        f, c = lax.axis_index("fsdp"), lax.axis_index("ctx")
        zl, y, k, zh, x = f // 8, (f // 2) % 4, f % 2, c // 4, c % 4
        self.zl, self.y, self.k, self.zh, self.x = zl, y, k, zh, x
        self.z = zh * 2 + zl
        self.f, self.c = f, c
        self.yp, self.ym = self.along("y", 1), self.along("y", 3)
        self.zp, self.zm = self.along("z", 1), self.along("z", 3)
        self.xp, self.xm = self.along("x", 1), self.along("x", 3)
        self.pair = (fid(1 - zl, y, k), c)
        self.sib = (fid(zl, y, 1 - k), c)
        self.peer_c = (1 - zh) * 4 + x
        self.peer = (f, self.peer_c)

    def at(self, dim):
        return {"y": self.y, "x": self.x, "z": self.z}[dim]

    def along(self, dim, off):
        there = (self.at(dim) + off) % 4
        if dim == "y":
            return (fid(self.zl, there, self.k), self.c)
        if dim == "x":
            return (self.f, self.zh * 4 + there)
        return (fid(there % 2, self.y, self.k), (there // 2) * 4 + self.x)

    def ctx(self, off):
        return (self.c + off) % 8


def barrier(devices):
    sem = pltpu.get_barrier_semaphore()
    for d in devices:
        pl.semaphore_signal(sem, inc=1, device_id=d, device_id_type=MESH)
    pl.semaphore_wait(sem, len(devices))


class Copy:
    def __init__(self, copy, made_by):
        self.copy, self.made_by = copy, made_by
        if not made_by.again:
            copy.start()

    def wait_recv(self):
        if not self.made_by.again:
            self.copy.wait_recv()

    def wait(self):
        if not self.made_by.again:
            self.copy.wait()


class Wire:
    def __init__(self, send, recv, again=False):
        self.send, self.recv, self.n, self.all, self.again = send, recv, 0, [], again

    def __call__(self, src, dst, device):
        i = self.n
        self.n += 1
        copy = pltpu.make_async_remote_copy(
            src_ref=src, dst_ref=dst, send_sem=self.send.at[i], recv_sem=self.recv.at[i],
            device_id=device, device_id_type=MESH)
        self.all.append(copy)
        return Copy(copy, self)

    def finish(self):
        for copy in self.all:
            copy.wait_send()


class Local:
    def __init__(self, sems, again=False):
        self.sems, self.n, self.again = sems, 0, again

    def __call__(self, src, dst):
        i = self.n
        self.n += 1
        return Copy(None if self.again else pltpu.make_async_copy(src, dst, self.sems.at[i]), self)


def sems(wires, local):
    return [DMA((wires,)), DMA((wires,)), DMA((local,))]


def talking(number, name, **more):
    return dict(
        compiler_params=pltpu.CompilerParams(
            collective_id=number, has_side_effects=True, vmem_limit_bytes=63 << 20),
        name=name, **more)
def quarters(rows):
    if rows % 64 == 0:
        q = rows // 4
        return (0, q, 2 * q, 3 * q, rows)
    return (0, 16, 32, 48, rows)


class WeightFlow:
    def __init__(self, net, wire, src, out, paired=False):
        self.net, self.wire, self.src, self.out = net, wire, src, out
        self.zp, self.zm = (net.pair, net.pair) if paired else (net.zp, net.zm)
        self.rows = src.shape[0]
        self.q = quarters(self.rows)
        self.c = {}

    def place(self, dz, dy, a=0, b=4):
        n = self.net
        zl = n.zl if dz == 0 else 1 - n.zl
        at = fid(zl, (n.y + dy + 4) % 4, n.k) * self.rows + self.q[a]
        return self.out.at[pl.ds(pl.multiple_of(at, 16), self.q[b] - self.q[a])]

    def own(self, a=0, b=4):
        return self.src.at[pl.ds(self.q[a], self.q[b] - self.q[a])]

    def pass_on(self, name, device, dz, dy, a=0, b=4):
        ref = self.place(dz, dy, a, b)
        self.c[name] = self.wire(ref, ref, device)

    def got(self, name):
        self.c[name].wait_recv()

    def stage(self, s):
        n, w, c = self.net, self.wire, self.c
        if s == 0:
            c["yp"] = w(self.own(), self.place(0, 0), n.yp)
            c["ym"] = w(self.own(), self.place(0, 0), n.ym)
            c["zp"] = w(self.own(0, 2), self.place(0, 0, 0, 2), self.zp)
            c["zm"] = w(self.own(2, 4), self.place(0, 0, 2, 4), self.zm)
            c["d"] = w(self.own(), self.place(0, 0), n.sib)
        elif s == 1:
            self.got("yp")
            self.pass_on("yp2", n.yp, 0, -1, 0, 2)
            self.pass_on("zp_m", self.zp, 0, -1, 0, 2)
            self.pass_on("zm_m", self.zm, 0, -1, 2, 4)
            self.pass_on("d_m", n.sib, 0, -1)
            self.got("ym")
            self.pass_on("ym2", n.ym, 0, 1, 2, 4)
            self.pass_on("zp_p", self.zp, 0, 1, 0, 2)
            self.pass_on("zm_p", self.zm, 0, 1, 2, 4)
            self.pass_on("d_p", n.sib, 0, 1)
            self.got("zp")
            self.pass_on("dz0", n.sib, 1, 0, 0, 2)
            self.got("zm")
            self.pass_on("dz1", n.sib, 1, 0, 2, 4)
        elif s == 2:
            self.got("yp2")
            self.pass_on("zp_2", self.zp, 0, 2, 0, 1)
            self.pass_on("d2a", n.sib, 0, 2, 0, 2)
            self.got("ym2")
            self.pass_on("zm_2", self.zm, 0, 2, 2, 3)
            self.pass_on("d2b", n.sib, 0, 2, 2, 4)
            self.got("zp_m")
            self.pass_on("yq", n.yp, 1, -1, 1, 2)
            self.pass_on("dzm0", n.sib, 1, -1, 0, 2)
            self.got("zm_p")
            self.pass_on("yr", n.ym, 1, 1, 3, 4)
            self.pass_on("dzp1", n.sib, 1, 1, 2, 4)
            self.got("zm_m")
            self.pass_on("dzm1", n.sib, 1, -1, 2, 4)
            self.got("zp_p")
            self.pass_on("dzp0", n.sib, 1, 1, 0, 2)
        elif s == 3:
            self.got("zp_2")
            self.got("yq")
            self.pass_on("dz20", n.sib, 1, 2, 0, 2)
            self.got("zm_2")
            self.got("yr")
            self.pass_on("dz21", n.sib, 1, 2, 2, 4)
        elif s == 4:
            for name in ("d", "d_m", "d_p", "dz0", "dz1", "d2a", "d2b", "dzm0", "dzp1", "dzm1", "dzp0", "dz20", "dz21"):
                self.got(name)


class SharedFlow(WeightFlow):
    def quarter(self, dz, dy, hi, own=False):
        n, q = self.net, self.rows // 4
        zl = n.zl if dz == 0 else 1 - n.zl
        at = (2 * hi + n.x % 2) * q
        if own:
            return self.src.at[pl.ds(pl.multiple_of(at, 16), q)]
        return self.out.at[pl.ds(pl.multiple_of(fid(zl, (n.y + dy + 4) % 4, n.k) * self.rows + at, 16), q)]

    def hand(self, name, device, dz, dy, hi):
        ref = self.quarter(dz, dy, hi)
        self.c[name] = self.wire(ref, ref, device)

    def along_z(self, tag, dy):
        self.hand("zp" + tag, self.zp, 0, dy, 0)
        self.hand("zm" + tag, self.zm, 0, dy, 1)

    def along_x(self, tag, dy):
        self.got("zp" + tag)
        self.hand("xp" + tag, self.net.xp, 1, dy, 0)
        self.got("zm" + tag)
        self.hand("xm" + tag, self.net.xm, 1, dy, 1)

    def to_sibling(self, tag, dy):
        self.got("xp" + tag)
        self.got("xm" + tag)
        self.pass_on("dz" + tag, self.net.sib, 1, dy)

    def stage(self, s):
        n, w, c = self.net, self.wire, self.c
        if s == 0:
            c["yp"] = w(self.own(), self.place(0, 0), n.yp)
            c["ym"] = w(self.own(), self.place(0, 0), n.ym)
            c["zp0"] = w(self.quarter(0, 0, 0, True), self.quarter(0, 0, 0), self.zp)
            c["zm0"] = w(self.quarter(0, 0, 1, True), self.quarter(0, 0, 1), self.zm)
            c["d"] = w(self.own(), self.place(0, 0), n.sib)
        elif s == 1:
            self.got("yp")
            self.pass_on("yp2", n.yp, 0, -1, 0, 2)
            self.along_z("m", -1)
            self.pass_on("d_m", n.sib, 0, -1)
            self.got("ym")
            self.pass_on("ym2", n.ym, 0, 1, 2, 4)
            self.along_z("p", 1)
            self.pass_on("d_p", n.sib, 0, 1)
            self.along_x("0", 0)
        elif s == 2:
            self.got("yp2")
            self.hand("zp2", self.zp, 0, 2, 0)
            self.pass_on("d2a", n.sib, 0, 2, 0, 2)
            self.got("ym2")
            self.hand("zm2", self.zm, 0, 2, 1)
            self.pass_on("d2b", n.sib, 0, 2, 2, 4)
            self.along_x("m", -1)
            self.along_x("p", 1)
            self.to_sibling("0", 0)
        elif s == 3:
            self.along_x("2", 2)
            self.to_sibling("m", -1)
            self.to_sibling("p", 1)
        elif s == 4:
            self.to_sibling("2", 2)
            for name in ("d", "d_m", "d_p", "d2a", "d2b", "dz0", "dzm", "dzp", "dz2"):
                self.got(name)


class RowFlow:
    def __init__(self, net, wire, src, out):
        self.net, self.wire, self.src, self.out = net, wire, src, out
        self.rows = src.shape[0]
        self.c = {}

    def place(self, ctx, a=0, b=2):
        lo, hi = a * self.rows // 2, b * self.rows // 2
        return self.out.at[pl.ds(pl.multiple_of(ctx * self.rows + lo, 16), hi - lo)]

    def pass_on(self, name, device, ctx, a=0, b=2):
        ref = self.place(ctx, a, b)
        self.c[name] = self.wire(ref, ref, device)

    def got(self, name):
        self.c[name].wait_recv()

    def stage(self, s):
        n, w, c = self.net, self.wire, self.c
        left, right = n.zh * 4 + (n.x + 3) % 4, n.zh * 4 + (n.x + 1) % 4
        left2, right2 = (1 - n.zh) * 4 + (n.x + 3) % 4, (1 - n.zh) * 4 + (n.x + 1) % 4
        if s == 0:
            c["pz"] = w(self.src, self.place(n.c), n.peer)
            c["xp"] = w(self.src, self.place(n.c), n.xp)
            c["xm"] = w(self.src, self.place(n.c), n.xm)
        elif s == 1:
            self.got("pz")
            self.pass_on("px", n.xp, n.peer_c)
            self.pass_on("pxm", n.xm, n.peer_c)
            self.got("xp")
            self.pass_on("xp2", n.xp, left, 0, 1)
            self.got("xm")
            self.pass_on("xm2", n.xm, right, 1, 2)
        elif s == 2:
            self.got("px")
            self.pass_on("px2", n.xp, left2, 0, 1)
            self.got("pxm")
            self.pass_on("pxm2", n.xm, right2, 1, 2)
        elif s == 3:
            for name in ("xp2", "xm2", "px2", "pxm2"):
                self.got(name)


class Later:
    def __init__(self, steps):
        self.steps = list(steps)

    def __call__(self):
        if self.steps:
            self.steps.pop(0)()

    def rest(self):
        while self.steps:
            self()


def stage(flow, *numbers):
    def go():
        for s in numbers:
            flow.stage(s)
    return go


def together(*steps):
    def go():
        for s in steps:
            s()
    return go


class Spread:
    def __init__(self, net, wire, here, forward, src, dst):
        rows, cols = (dst.shape[0], src.shape[1]) if forward else (src.shape[0], dst.shape[1])

        def by_row(ref, c):
            return ref.at[pl.ds(pl.multiple_of(c * rows, 16), rows)]

        def by_col(ref, c):
            return ref.at[:, pl.ds(pl.multiple_of(c * cols, 128), cols)]

        pick, put = (by_row, by_col) if forward else (by_col, by_row)
        self.copies = []
        for o in (6, 2, 4, 5, 7, 1, 3):
            there = net.ctx(o)
            self.copies.append(wire(pick(src, there), put(dst, net.c), (net.f, there)))
        self.own = here(pick(src, net.c), put(dst, net.c))

    def end(self):
        for copy in self.copies:
            copy.wait_recv()
        self.own.wait()


def neighbours(net):
    return ([net.sib] + [net.along(d, o) for d in "yz" for o in (1, 2, 3)] + [(net.f, net.ctx(o)) for o in (1, 2, 3, 5, 6, 7)])


KEPT = 11


def forward_kernel(nw, *refs):
    srcs, rows, cos_in, sin_in = refs[:nw], refs[nw], refs[nw + 1], refs[nw + 2]
    refs = refs[nw + 3:]
    outs, rows_out, own_heads, kept_out = refs[:nw - 1], refs[nw - 1], refs[nw], refs[nw + 1:nw + 1 + KEPT]
    refs = refs[nw + 1 + KEPT:]
    x, t, cos_at, sin_at, heads = refs[:5]
    kept = refs[5:5 + KEPT]
    send, recv, local = refs[5 + KEPT:]
    w, gains, q, k, v, lin, cs, sn, start, hf, inv = kept
    net, wire, here = Net(), Wire(send, recv), Local(local)
    barrier(neighbours(net))
    first, out_f, gate_f, up_f, down_f = [
        kind(net, wire, s, o, i == 0)
        for i, (kind, s, o) in enumerate(zip((WeightFlow, WeightFlow, WeightFlow, SharedFlow, SharedFlow), srcs, (t, *outs)))]
    flows = (first, out_f, gate_f, up_f, down_f)
    seq = RowFlow(net, wire, rows, x)
    first.stage(0)
    seq.stage(0)
    out_f.stage(0)
    gate_f.stage(0)
    tables_in = [here(cos_in, cos_at), here(sin_in, sin_at)]
    placed_here = [here(fl.src, fl.place(0, 0)) for fl in flows]
    placed_here.append(here(rows, seq.place(net.c)))
    first.stage(1)
    out_f.stage(1)
    up_f.stage(0)
    first.stage(2)
    seq.stage(1)
    gate_f.stage(1)
    down_f.stage(0)
    first.stage(3)
    out_f.stage(2)
    seq.stage(2)
    up_f.stage(1)
    first.stage(4)
    gate_f.stage(2)
    seq.stage(3)
    for c in tables_in + placed_here:
        c.wait()
    saved = [here(x, rows_out)]
    tick = Later([
        together(stage(down_f, 1), stage(out_f, 3)),
        stage(up_f, 2),
        stage(gate_f, 3),
        stage(down_f, 2),
        stage(up_f, 3),
        stage(down_f, 3),
    ])
    attn_forward(tick, x, t, cos_at, sin_at, w, gains, q, k, v, lin, cs, sn, start, hf, heads, inv)
    spread = Spread(net, wire, here, True, heads, own_heads)
    saved += [here(a, b) for a, b in zip(kept, kept_out)]
    tick.rest()
    for fl in flows[1:]:
        fl.stage(4)
    spread.end()
    for c in saved:
        c.wait()
    wire.finish()


def shapes(*items):
    return [jax.ShapeDtypeStruct(s, d) for s, d in items]


def forward(weights, rows, cos_in, sin_in):
    nw = len(weights)
    per, cols = weights[0].shape
    length = 8 * rows.shape[0]
    kept = shapes(
        ((16 * (per - 16), cols), BF16), ((16, cols), F32), ((2, length, HEAD), BF16), ((length, HEAD), BF16),
        ((length, HEAD), BF16), ((length, 3 * HEAD), F32), ((length, HEAD), F32), ((length, HEAD), F32),
        ((length, HEAD), F32), ((length, 2 * HEAD), F32), ((2, length, HEAD), F32))
    outs = [jax.ShapeDtypeStruct((16 * w.shape[0], w.shape[1]), w.dtype) for w in weights[1:]]
    outs += shapes(((length, rows.shape[1]), BF16), ((rows.shape[0], 16 * HEAD), BF16)) + kept
    scratch = [((length, rows.shape[1]), BF16), ((16 * per, cols), BF16), ((length, HEAD), F32), ((length, HEAD), F32), ((length, 2 * HEAD), BF16)]
    res = pl.pallas_call(
        functools.partial(forward_kernel, nw),
        out_shape=outs, in_specs=[ANY] * (nw + 3), out_specs=[ANY] * len(outs),
        scratch_shapes=[pltpu.VMEM(s, d) for s, d in scratch] + [pltpu.VMEM(a.shape, a.dtype) for a in kept]
        + sems(29 * nw + 9 + 7, nw + 3 + 1 + 1 + KEPT), **talking(0, "layer_forward"),
    )(*weights, rows, cos_in, sin_in)
    return res[:nw - 1], res[nw - 1], res[nw], res[nw + 1:]
def block(i, size):
    return pl.ds(pl.multiple_of(i * size, size), size)


def dot_t(left, right):
    return lax.dot_general(left, right, (((1,), (1,)), ((), ())), preferred_element_type=F32)


def t_dot(left, right):
    return lax.dot_general(left, right, (((0,), (0,)), ((), ())), preferred_element_type=F32)


def plain_dot(left, right):
    return jnp.dot(left, right, preferred_element_type=F32)


def unit(v):
    r = lax.rsqrt(jnp.mean(v * v, axis=-1, keepdims=True) + EPSILON)
    return v * r, r


ROWS = 256


def attn_forward(tick, x, t, cos_in, sin_in, w, gains, q, k, v, lin, cs, sn, start, hf, heads, inv):
    length, width = x.shape[0], x.shape[1] - HEAD
    per = t.shape[0] // 16
    depth = per - 16
    total = jnp.zeros((16, t.shape[1]), F32)
    for f in range(16):
        w[f * depth:(f + 1) * depth, :] = t[f * per:f * per + depth, :]
        total = total + t[f * per + depth:(f + 1) * per, :].astype(F32)
    gains[...] = total
    attn_gain = jnp.concatenate([total[0:1], total[1:2]], axis=1)
    query_gain, key_gain = total[4:5, 0:HEAD], total[4:5, HEAD:2 * HEAD]

    def count(i, carry):
        doc = x[block(i, ROWS), width:].astype(F32)
        return (carry[0] + jnp.sum((doc < 0.5).astype(F32), axis=0, keepdims=True),
                carry[1] + jnp.sum((doc < 1.5).astype(F32), axis=0, keepdims=True))

    zero = jnp.zeros((1, HEAD), F32)
    first, second = lax.fori_loop(0, length // ROWS, count, (zero, zero))
    lanes = lax.broadcasted_iota(jnp.int32, (1, HEAD), 1) % (HEAD // 2)
    freqs = jnp.exp(lanes.astype(F32) * (-2.0 * math.log(THETA) / HEAD))
    c1, s1 = jnp.cos(first * freqs), jnp.sin(first * freqs)
    c2, s2 = jnp.cos(second * freqs), jnp.sin(second * freqs)
    sign = jnp.where(lax.broadcasted_iota(jnp.int32, (1, HEAD), 1) < HEAD // 2, -1.0, 1.0)

    def prepare(i, carry):
        rows = block(i, ROWS)
        doc = x[rows, width:].astype(F32)
        start[rows, :] = jnp.where(doc < 0.5, 0.0, jnp.where(doc < 1.5, first, second))
        cd = jnp.where(doc < 0.5, 1.0, jnp.where(doc < 1.5, c1, c2))
        sd = jnp.where(doc < 0.5, 0.0, jnp.where(doc < 1.5, s1, s2))
        ci, si = cos_in[rows, :], sin_in[rows, :]
        cosine = ci * cd + si * sd
        sine = (si * cd - ci * sd) * sign
        cs[rows, :] = cosine
        sn[rows, :] = sine
        normed = (unit(x[rows, :width].astype(F32))[0] * attn_gain).astype(BF16)
        out = plain_dot(normed, w[...])
        lin[rows, :] = out[:, :3 * HEAD]
        v[rows, :] = out[:, 3 * HEAD:].astype(BF16)
        for h in range(3):
            e = unit(out[:, h * HEAD:(h + 1) * HEAD])[0] * (query_gain if h < 2 else key_gain)
            e = (e * cosine + pltpu.roll(e, HEAD // 2, 1) * sine).astype(BF16)
            if h < 2:
                q[h, rows, :] = e
            else:
                k[rows, :] = e
        return carry

    for i in range(0, length // ROWS, 2):
        lax.fori_loop(i, i + 2, prepare, 0)
        tick()

    def queries(i, carry):
        rows = block(i, ROWS)
        here = q[:, rows, :].reshape(2 * ROWS, HEAD)
        begin = start[rows, :]

        def keys(j, state):
            acc, norm = state
            these = block(j, ROWS)
            p = jnp.exp(dot_t(here, k[these, :]) * FACTOR)
            p = jnp.where(allowed_at(i, j, begin), p.reshape(2, ROWS, ROWS), 0.0).reshape(2 * ROWS, ROWS)
            norm = norm + p[:, :HEAD] + p[:, HEAD:]
            return acc + plain_dot(p.astype(BF16), v[these, :]), norm

        zeros = jnp.zeros((2 * ROWS, HEAD), F32)
        acc, norm = lax.fori_loop(0, i + 1, keys, (zeros, zeros))
        over = jnp.broadcast_to(1.0 / jnp.sum(norm, axis=1, keepdims=True), (2 * ROWS, HEAD))
        acc = acc * over
        inv[:, rows, :] = over.reshape(2, ROWS, HEAD)
        for h in range(2):
            part = acc[h * ROWS:(h + 1) * ROWS]
            hf[rows, h * HEAD:(h + 1) * HEAD] = part
            heads[rows, h * HEAD:(h + 1) * HEAD] = part.astype(BF16)
        return carry

    for i, j in ((0, 3), (3, 4), (4, 5), (5, 6)):
        lax.fori_loop(i, j, queries, 0)
        tick()


def allowed_at(i, j, begin):
    own = lax.broadcasted_iota(jnp.int32, (ROWS, ROWS), 0) + i * ROWS
    other = lax.broadcasted_iota(jnp.int32, (ROWS, ROWS), 1) + j * ROWS
    begin = jnp.concatenate([begin, begin], axis=1)
    return ((other.astype(F32) >= begin) & (other <= own))[None]


def attn_backward(tick, gains, q, k, v, start, hf, inv, dh, dq, dk, dv, delta):
    length = dh.shape[0]
    blocks = length // ROWS

    def before(i, carry):
        rows = block(i, ROWS)
        for h in range(2):
            cols = slice(h * HEAD, (h + 1) * HEAD)
            s = jnp.sum(dh[rows, cols].astype(F32) * hf[rows, cols], axis=1, keepdims=True)
            delta[h, rows, :] = jnp.broadcast_to(s, (ROWS, HEAD))
            dq[h, rows, :] = jnp.zeros((ROWS, HEAD), F32)
        return carry

    lax.fori_loop(0, blocks, before, 0)

    def keys(j, carry):
        these = block(j, ROWS)
        kt, vt = k[these, :], v[these, :]

        def queries(i, state):
            d_key, d_value = state
            rows = block(i, ROWS)
            here = q[:, rows, :].reshape(2 * ROWS, HEAD)
            grad = jnp.concatenate([dh[rows, :HEAD], dh[rows, HEAD:]], axis=0)
            over = inv[:, rows, :].reshape(2 * ROWS, HEAD)
            off = delta[:, rows, :].reshape(2 * ROWS, HEAD)
            over = jnp.concatenate([over, over], axis=1)
            off = jnp.concatenate([off, off], axis=1)
            p = jnp.exp(dot_t(here, kt) * FACTOR) * over
            p = jnp.where(allowed_at(i, j, start[rows, :]), p.reshape(2, ROWS, ROWS), 0.0).reshape(2 * ROWS, ROWS)
            ds = (p * (dot_t(grad, vt) - off)).astype(BF16)
            dq[:, rows, :] = dq[:, rows, :] + plain_dot(ds, kt).reshape(2, ROWS, HEAD)
            return d_key + t_dot(ds, here), d_value + t_dot(p.astype(BF16), grad)

        zeros = jnp.zeros((ROWS, HEAD), F32)
        d_key, d_value = lax.fori_loop(j, blocks, queries, (zeros, zeros))
        dk[these, :] = d_key
        dv[these, :] = d_value
        return carry

    for i, j in ((0, 1), (1, 2), (2, 4), (4, 6)):
        lax.fori_loop(i, j, keys, 0)
        tick()


WIDE = 384


def attn_backward_end(x, w, gains, lin, cs, sn, dq, dk, dv, dlin, dw, dn):
    length, width = x.shape[0], x.shape[1] - HEAD
    g = gains[...]
    attn_gain = jnp.concatenate([g[0:1], g[1:2]], axis=1)
    query_gain, key_gain = g[4:5, 0:HEAD], g[4:5, HEAD:2 * HEAD]

    def after(i, carry):
        d_attn, d_query, d_key = carry
        rows = block(i, WIDE)
        cosine, sine = cs[rows, :], sn[rows, :]
        for h in range(3):
            cols = slice(h * HEAD, (h + 1) * HEAD)
            d = (dq[h, rows, :] if h < 2 else dk[rows, :]) * FACTOR
            d = d * cosine - pltpu.roll(d, HEAD // 2, 1) * sine
            e, r = unit(lin[rows, cols])
            s = jnp.sum(d * e, axis=0, keepdims=True)
            d_query, d_key = (d_query + s, d_key) if h < 2 else (d_query, d_key + s)
            d = d * (query_gain if h < 2 else key_gain)
            d = r * (d - e * jnp.mean(d * e, axis=-1, keepdims=True))
            dlin[rows, cols] = d.astype(BF16)
        dlin[rows, 3 * HEAD:] = dv[rows, :].astype(BF16)
        part = dot_t(dlin[rows, :], w[...])
        e = unit(x[rows, :width].astype(F32))[0]
        d_attn = d_attn + jnp.sum(part * e, axis=0, keepdims=True)
        dn[i // 2, pl.ds((i % 2) * 2, 2)] = part.astype(BF16).reshape(2, WIDE // 2, width)
        normed = (e * attn_gain).astype(BF16)

        part = t_dot(normed, dlin[rows, :])
        dw[...] = jnp.where(i == 0, part, dw[...] + part)
        return d_attn, d_query, d_key

    zero = jnp.zeros((1, HEAD), F32)
    dw[...] = jnp.zeros_like(dw)
    return lax.fori_loop(0, length // WIDE, after, (jnp.zeros((1, width), F32), zero, zero))


def shapes(*items):
    return [jax.ShapeDtypeStruct(s, d) for s, d in items]


def add_rows(out, parts, rows, step):
    def some(r, carry):
        here = pl.ds(pl.multiple_of(r * step, 16), step)
        if len(parts) == 2:
            out(here, parts[0](here) + parts[1](here))
            return carry
        total = parts[0](here).astype(F32)
        for part in parts[1:]:
            total = total + part(here).astype(F32)
        out(here, total.astype(BF16))
        return carry

    lax.fori_loop(0, rows // step, some, 0)


FIRST = (2, 1, 3, 0)


class SumFlow:
    def __init__(self, net, wire, here, src, first, order, slots, other, relay, got, part, fin, out):
        self.net, self.wire, self.here, self.src, self.first, self.order = net, wire, here, src, first, order
        self.slots, self.other, self.relay, self.got, self.part, self.fin, self.out = slots, other, relay, got, part, fin, out
        self.rows, self.cols = other.shape[2], other.shape[3]
        self.w = self.cols // 8
        self.far, self.via = {}, {}

    def cut(self, ref, dim, d, k=None):
        tail = ref.shape[-1]
        a = (slice(None), slice(None))
        cols = pl.ds(0, tail)
        if dim == "y":
            a = (slice(None), pl.ds(d, 1))
        elif dim == "x":
            cols = pl.ds(pl.multiple_of(d * (tail // 4), 128), tail // 4)
        else:
            a = (pl.ds(d % 2, 1), slice(None))
            cols = pl.ds(pl.multiple_of((d // 2) * (tail // 2), 128), tail // 2)
        if k is None:
            return ref.at[a[0], a[1], :, cols]
        return ref.at[a[0], a[1], k, pl.ds(self.first, self.rows), cols]

    def begin(self):
        self.near, self.own = {}, {}
        self.bring(0)
        self.bring(1)

    def bring(self, i):
        n, dim = self.net, self.order[0]
        o = FIRST[i]
        d = (n.at(dim) + o) % 4
        self.near[o] = self.wire(self.cut(self.src, dim, d, 1 - n.k), self.cut(self.other, dim, d), n.sib)
        self.own[o] = self.here(self.cut(self.src, dim, d, n.k), self.slots.at[i % 2])

    def add(self, out, parts):
        if self.wire.again:
            return
        a, b = out.shape[0], out.shape[1]
        step = 16
        for i in range(a):
            for j in range(b):
                def take(ref):
                    return lambda here: ref[i, j, here, :]

                def put(here, value):
                    out[i, j, here, :] = value
                add_rows(put, [take(p) for p in parts], out.shape[2], step)

    def chip(self, o):
        n, dim = self.net, self.order[0]
        d = (n.at(dim) + o) % 4
        self.near[o].wait_recv()
        self.own[o].wait()
        i = FIRST.index(o)
        piece = self.cut(self.other, dim, d)
        self.add(piece, [piece, self.slots.at[i % 2]])
        if i + 2 < 4:
            self.bring(i + 2)
        half = self.rows // 2
        if o == 2:
            for which, to in ((0, 1), (1, 3)):
                self.via[to] = self.wire(piece.at[:, :, pl.ds(which * half, half)], self.relay.at[which], n.along(dim, to))
        elif o:
            which = 0 if o == 1 else 1
            self.via[o].wait_recv()
            part = piece.at[:, :, pl.ds(which * half, half)]
            self.add(part, [part, self.relay.at[which]])
            self.far[o] = self.wire(piece, self.got[0].at[which], n.along(dim, o))

    def phase(self, p):
        n, dim = self.net, self.order[p]
        held = self.other if p == 0 else self.part[p - 1]
        for o in (1, 3, 2) if p else (1, 3):
            self.far[o].wait_recv()
        result = self.part[p] if p < 2 else self.fin
        self.add(result, [self.cut(held, dim, n.at(dim))] + [self.got[p].at[i] for i in range(3 if p else 2)])
        if p < 2:
            after = self.order[p + 1]
            for o in (2, 1, 3):
                d = (n.at(after) + o) % 4
                self.far[o] = self.wire(self.cut(result, after, d), self.got[p + 1].at[o - 1], n.along(after, o))
        else:
            fin, to = self.fin.at[0, 0], self.place(n.zh)
            self.across = self.wire(fin, to, n.peer)
            self.last = [self.wire(fin, to, n.along("x", o)) for o in (2, 1, 3)]
            self.kept = self.here(fin, to)

    def place(self, zh):
        n = self.net
        s = zh * 4 + n.x if self.order.index("z") < self.order.index("x") else n.x * 2 + zh
        return self.out.at[pl.ds(self.first, self.rows), pl.ds(pl.multiple_of(s * self.w, 128), self.w)]

    def share(self):
        n = self.net
        self.across.wait_recv()
        to = self.place(1 - n.zh)
        self.last += [self.wire(to, to, n.along("x", o)) for o in (2, 1, 3)]

    def end(self):
        for copy in self.last:
            copy.wait_recv()
        self.kept.wait()


def sum_shapes(rows, cols, order):
    shape, out = [2, 4, rows, cols], []
    for dim in order:
        if dim == "y":
            shape[1] = 1
        elif dim == "x":
            shape[3] //= 4
        else:
            shape[0], shape[3] = 1, shape[3] // 2
        out.append(tuple(shape))
    return out


PLAN = ((0, 0, 64, "yxz"), (1, 0, 64, "xzy"), (2, 0, 192, "zyx"), (3, 0, 64, "yzx"), (3, 64, 64, "yxz"))


def first_shapes(plan, shapes_in):
    return [sum_shapes(rows, shapes_in[which][-1], order)[0] for which, _, rows, order in plan]


def sum_scratch(plan, shapes_in):
    held = []
    for which, first, rows, order in plan:
        cols = shapes_in[which][-1]
        a, b, c = sum_shapes(rows, cols, order)
        half = (a[0], a[1], a[2] // 2, a[3])
        held += [pltpu.VMEM(s, BF16) for s in ((2, 4, rows, cols), (2, *half), (2, *a), (3, *b), (3, *c), a, b, c)]
    return held


def make_flows(net, wire, here, plan, srcs, outs, held, slots):
    flows = []
    for n, (which, first, rows, order) in enumerate(plan):
        other, relay, g0, g1, g2, p0, p1, fin = held[8 * n:8 * n + 8]
        flows.append(SumFlow(net, wire, here, srcs[which], first, order, slots[n], other, relay, (g0, g1, g2), (p0, p1), fin, outs[which]))
    return flows


class Ends:
    def __init__(self, net, wire, here, dwx, dn, rows_out, dn_out, other, got, fin, got_xa, part_a, got_za, got_zb, part_b, got_xb):
        self.net, self.wire, self.here, self.dwx, self.dn, self.rows_out, self.dn_out = net, wire, here, dwx, dn, rows_out, dn_out
        self.other, self.got, self.fin = other, got, fin
        self.got_xa, self.part_a, self.got_za, self.got_zb, self.part_b, self.got_xb = got_xa, part_a, got_za, got_zb, part_b, got_xb
        self.half = part_a.shape[-1]
        self.rows = part_a.shape[1]

    def begin(self):
        n, h = self.net, self.half
        self.over_b = self.wire(self.dn.at[1 - n.zh, :, :, pl.ds(h, h)], self.got_zb, n.peer)
        self.moved_a = [self.wire(self.dn.at[:, (n.x + o) % 4, :, pl.ds(0, h)], self.got_xa.at[o - 1], n.along("x", o)) for o in (2, 1, 3)]
        self.near = self.wire(self.dwx.at[:, :, 1 - n.k], self.other, n.sib)

    def chip(self):
        n = self.net
        self.near.wait_recv()
        for a in range(2):
            for b in range(4):
                self.other[a, b] = self.other[a, b] + self.dwx[a, b, n.k]
        self.far = []
        for dz in (1, 0):
            for dy in (2, 1, 3, 0):
                if dz or dy:
                    there = ((n.zl + dz) % 2, (n.y + dy) % 4)
                    self.far.append(self.wire(self.other.at[there[0], there[1]], self.got.at[dz * 4 + dy - 1], (fid(there[0], there[1], n.k), n.c)))

    def along_z(self):
        n, h = self.net, self.half
        self.over_b.wait_recv()
        for x in range(4):
            def put(here, value):
                self.part_b[x, here, :] = value
            add_rows(put, [lambda here: self.dn[n.zh, x, here, h:], lambda here: self.got_zb[x, here, :]], self.rows, 16)
        self.moved_b = [self.wire(self.part_b.at[(n.x + o) % 4], self.got_xb.at[o - 1], n.along("x", o)) for o in (2, 1, 3)]

    def along_x(self):
        n, h = self.net, self.half
        for copy in self.moved_a:
            copy.wait_recv()
        for zh in range(2):
            def take(o):
                return (lambda here: self.dn[zh, n.x, here, :h]) if o == 0 else (lambda here: self.got_xa[o - 1, zh, here, :])

            def put(here, value):
                self.part_a[zh, here, :] = value
            add_rows(put, [take(o) for o in range(4)], self.rows, 16)
        self.over_a = self.wire(self.part_a.at[1 - n.zh], self.got_za, n.peer)

    def share(self):
        n = self.net
        for copy in self.far:
            copy.wait_recv()
        total = self.other[n.zl, n.y].astype(F32)
        for i in range(7):
            total = total + self.got[i].astype(F32)
        self.fin[...] = total.astype(BF16)
        self.copies = [self.wire(self.fin, self.rows_out.at[n.c], (n.f, n.ctx(o))) for o in (6, 2, 4, 5, 7, 1, 3)]
        self.kept = self.here(self.fin, self.rows_out.at[n.c])

    def end(self):
        n, h = self.net, self.half
        self.over_a.wait_recv()
        for copy in self.moved_b:
            copy.wait_recv()

        def some(r, carry):
            at = pl.ds(pl.multiple_of(r * 16, 16), 16)
            self.dn_out[at, :h] = self.part_a[n.zh, at, :].astype(F32) + self.got_za[at, :].astype(F32)
            total = self.part_b[n.x, at, :].astype(F32)
            for o in range(3):
                total = total + self.got_xb[o, at, :].astype(F32)
            self.dn_out[at, h:] = total
            return carry

        lax.fori_loop(0, self.rows // 16, some, 0)
        for copy in self.copies:
            copy.wait_recv()
        self.kept.wait()


def backward_kernel(ng, *refs):
    srcs, x_in, d_heads, mlp_rows, kept_in = refs[:ng], refs[ng], refs[ng + 1], refs[ng + 2], refs[ng + 3:ng + 3 + KEPT]
    refs = refs[ng + 3 + KEPT:]
    outs, rows_out, dn_out = refs[:ng], refs[ng], refs[ng + 1]
    refs = refs[ng + 2:]
    kept, refs = refs[:KEPT], refs[KEPT:]
    w, gains, q, k, v, lin, cs, sn, start, hf, inv = kept
    dh, dq, dk, dv, delta, mlp_at, dwx, dn = refs[:8]
    end_held, refs = refs[8:17], refs[17:]
    held, (send, recv, local) = refs[:-3], refs[-3:]
    net = Net()
    length, width = x_in.shape[0], x_in.shape[1] - HEAD
    depth = w.shape[0] // 16

    def opening(wire, here, slots):
        spread = Spread(net, wire, here, False, d_heads, dh)
        flows = make_flows(net, wire, here, PLAN, srcs, outs, held, slots)
        for fl in flows:
            fl.begin()
        loads = [here(a, b) for a, b in zip(kept_in, kept)] + [here(mlp_rows, mlp_at)]

        def chips(o):
            def go():
                for fl in flows:
                    fl.chip(o)
            return go

        chips(2)()
        return spread, loads, Later([chips(1), chips(3), chips(0)]), flows

    def slotted(*slots):
        barrier(neighbours(net))
        spread, loads, tick, _ = opening(Wire(send, recv), Local(local), slots)
        for c in loads:
            c.wait()
        spread.end()
        attn_backward(tick, gains, q, k, v, start, hf, inv, dh, dq, dk, dv, delta)
        tick.rest()

    pl.run_scoped(slotted, *[pltpu.VMEM((2, *a), BF16) for a in first_shapes(PLAN, [s.shape for s in srcs])])
    wire, here = Wire(send, recv, True), Local(local, True)
    _, _, tick, flows = opening(wire, here, held[2::8])
    tick.rest()
    wire.again = here.again = False
    ends = Ends(net, wire, here, dwx, dn, rows_out, dn_out, *end_held)

    def ending(x, dlin, dw):
        fetch = pltpu.make_async_copy(x_in, x, local.at[local.shape[0] - 1])
        fetch.start()
        fetch.wait()
        d_attn, d_query, d_key = attn_backward_end(x, w, gains, lin, cs, sn, dq, dk, dv, dlin, dw, dn)
        cols = dw.shape[1]
        lanes = jnp.concatenate([d_query, d_key, jnp.zeros((1, cols - 2 * HEAD), F32)], axis=1)
        small = jnp.concatenate([d_attn[:, :cols], d_attn[:, cols:], jnp.zeros((2, cols), F32), lanes, jnp.zeros((11, cols), F32)], axis=0)
        small = (small + mlp_at[...]).astype(BF16)
        for f in range(16):
            at = (f // 8, (f // 2) % 4, f % 2)
            dwx[at[0], at[1], at[2], :depth, :] = dw[f * depth:(f + 1) * depth, :].astype(BF16)
            dwx[at[0], at[1], at[2], depth:, :] = small

    def phase(p):
        for fl in flows:
            fl.phase(p)

    def share():
        for fl in flows:
            fl.share()

    pl.run_scoped(ending, pltpu.VMEM((length, width + HEAD), BF16), pltpu.VMEM((length, 4 * HEAD), BF16), pltpu.VMEM((16 * depth, 4 * HEAD), F32))
    ends.begin()
    phase(0)
    phase(1)
    ends.chip()
    ends.along_z()
    ends.along_x()
    phase(2)
    ends.share()
    share()
    ends.end()
    for fl in flows:
        fl.end()
    wire.finish()


def backward(grads, x, d_heads, mlp_rows, kept):
    srcs = [g.reshape(2, 4, 2, g.shape[0] // 16, g.shape[1]) for g in grads]
    length, width = x.shape[0], x.shape[1] - HEAD
    rows, cols = length // 8, 4 * HEAD
    depth, half = width // 16, width // 2
    out = [jax.ShapeDtypeStruct((g.shape[0] // 16, g.shape[1]), BF16) for g in grads]
    out += shapes(((8, depth + 16, cols), BF16), ((rows, width), F32))
    scratch = [(a.shape, a.dtype) for a in kept]
    scratch += [((length, 2 * HEAD), BF16), ((2, length, HEAD), F32), ((length, HEAD), F32), ((length, HEAD), F32),
                ((2, length, HEAD), F32), (mlp_rows.shape, F32), ((2, 4, 2, depth + 16, cols), BF16), ((2, 4, rows, width), BF16)]
    scratch += [((2, 4, depth + 16, cols), BF16), ((7, depth + 16, cols), BF16), ((depth + 16, cols), BF16),
                ((3, 2, rows, half), BF16), ((2, rows, half), BF16), ((rows, half), BF16),
                ((4, rows, half), BF16), ((4, rows, half), BF16), ((3, rows, half), BF16)]
    ng = len(grads)
    wires = 21 * len(PLAN) + 7 + 3 + 1 + 3 + 1 + 7 + 1 + 7
    local = 5 * len(PLAN) + 1 + KEPT + 1 + 1 + 1
    res = pl.pallas_call(
        functools.partial(backward_kernel, ng), out_shape=out,
        in_specs=[ANY] * (ng + 3 + KEPT), out_specs=[ANY] * (ng + 1) + [VM],
        scratch_shapes=[pltpu.VMEM(s, d) for s, d in scratch] + sum_scratch(PLAN, [s.shape for s in srcs]) + sems(wires, local),
        **talking(1, "layer_backward"))(*srcs, x, d_heads, mlp_rows, *kept)
    return res[:ng], res[ng], res[ng + 1]
CHUNK = 512


def mlp_kernel(steps, x, heads, g, gains, wo, wg, wu, wd, out, d_hidden, d_heads, rows_out, dg, du, dd, do, hidden, mixed, mixed_t, acc, d_mixed):
    step = pl.program_id(0)
    width = x.shape[1]
    gain = jnp.concatenate([gains[2:3], gains[3:4]], axis=1)

    @pl.when(step == 0)
    def _():
        h = x[...].astype(F32) + plain_dot(heads[...], wo[...])
        hidden[...] = h
        m = unit(h)[0] * gain
        mixed[...] = m.astype(BF16)
        mixed_t[...] = m.T.astype(BF16)
        acc[...] = h
        d_mixed[...] = jnp.zeros_like(d_mixed)

    m, grad = mixed[...], g[...]
    gate, upward = plain_dot(m, wg[...]), plain_dot(m, wu[...])
    s = jax.nn.sigmoid(gate)
    act = gate * s
    active = (act * upward).astype(BF16)
    acc[...] += plain_dot(active, wd[...])
    d_active = dot_t(grad, wd[...])
    dd[...] = t_dot(active, grad).astype(BF16)
    d_up = (d_active * act).astype(BF16)
    d_gate = (d_active * upward * (s + act * (1.0 - s))).astype(BF16)
    dg[...] = plain_dot(mixed_t[...], d_gate).astype(BF16)
    du[...] = plain_dot(mixed_t[...], d_up).astype(BF16)
    d_mixed[...] += dot_t(d_gate, wg[...]) + dot_t(d_up, wu[...])

    @pl.when(step == steps - 1)
    def _():
        out[...] = acc[...].astype(BF16)
        e, r = unit(hidden[...])
        d = d_mixed[...]
        d_gain = jnp.sum(d * e, axis=0, keepdims=True)
        d = d * gain
        d = g[...].astype(F32) + r * (d - e * jnp.mean(d * e, axis=-1, keepdims=True))
        d_hidden[...] = d
        low = d.astype(BF16)
        d_heads[...] = dot_t(low, wo[...]).astype(BF16)
        do[...] = t_dot(heads[...], low).astype(BF16)
        half = width // 2
        rows_out[...] = jnp.concatenate([jnp.zeros((2, half), F32), d_gain[:, :half], d_gain[:, half:], jnp.zeros((12, half), F32)], axis=0)


def mlp(x, heads, g, gains, wo, wg, wu, wd):
    rows, width = x.shape
    steps = wg.shape[1] // CHUNK
    whole = lambda a: pl.BlockSpec(a.shape, lambda i: (0,) * len(a.shape), pipeline_mode=pl.Buffered(1))
    fixed = lambda *s: pl.BlockSpec(s, lambda i: (0, 0))
    by_col = pl.BlockSpec((width, CHUNK), lambda i: (0, i))
    by_row = pl.BlockSpec((CHUNK, width), lambda i: (i, 0))
    out = shapes(((rows, width), BF16), ((rows, width), F32), (heads.shape, BF16), ((16, width // 2), F32),
                 (wg.shape, BF16), (wu.shape, BF16), (wd.shape, BF16), (wo.shape, BF16))
    return pl.pallas_call(
        functools.partial(mlp_kernel, steps), out_shape=out, grid=(steps,),
        in_specs=[whole(x), whole(heads), whole(g), whole(gains), whole(wo), by_col, by_col, by_row],
        out_specs=[fixed(rows, width), fixed(rows, width), fixed(*heads.shape), fixed(16, width // 2), by_col, by_col, by_row, fixed(*wo.shape)],
        scratch_shapes=[pltpu.VMEM((rows, width), F32), pltpu.VMEM((rows, width), BF16), pltpu.VMEM((width, rows), BF16),
                        pltpu.VMEM((rows, width), F32), pltpu.VMEM((rows, width), F32)],
        compiler_params=pltpu.CompilerParams(vmem_limit_bytes=56 << 20), name="mlp")(x, heads, g, gains, wo, wg, wu, wd)
def root_mean_norm(rows, scaling):
    return rows * lax.rsqrt(jnp.mean(rows * rows, axis=-1, keepdims=True) + EPSILON) * scaling


def tables(length):
    freqs = THETA ** (-np.arange(HEAD // 2, dtype=np.float64) * 2.0 / HEAD)
    angles = np.arange(length, dtype=np.float64)[:, None] * np.concatenate([freqs, freqs])[None, :]
    return jnp.asarray(np.cos(angles), F32), jnp.asarray(np.sin(angles), F32)


def placed(values, f):
    return jnp.where(jnp.arange(16)[:, None] == f, values[None, :], jnp.zeros((), BF16)).reshape(-1)


def body(inputs, doc_ids, query_proj, key_projection, value_projection, output_proj, gate_proj, up_proj, down_proj,
         attn_gain, mlp_gain, query_norm_gain, key_gain, out_grad):
    f, c = lax.axis_index("fsdp"), lax.axis_index("ctx")
    rows, width = inputs.shape[1:]
    depth = query_proj.shape[0]
    cols = 4 * HEAD
    own = jnp.concatenate([
        lax.dynamic_slice_in_dim(query_proj, c * 2 * HEAD, 2 * HEAD, 1),
        lax.dynamic_slice_in_dim(key_projection, c * HEAD, HEAD, 1),
        lax.dynamic_slice_in_dim(value_projection, c * HEAD, HEAD, 1)], axis=1)
    small = jnp.concatenate([
        placed(attn_gain, f), placed(mlp_gain, f), placed(query_norm_gain, f), placed(key_gain, f),
        jnp.zeros((16 * cols - 2 * width - 2 * HEAD,), BF16)]).reshape(16, cols)
    pack = jnp.concatenate([own, small], axis=0)
    sequence = jnp.concatenate([inputs[0], jnp.broadcast_to(doc_ids[0].astype(BF16)[:, None], (rows, HEAD))], axis=1)
    (full_output, full_gate, full_up, full_down), x, own_heads, kept = forward(
        [pack, output_proj, gate_proj, up_proj, down_proj], sequence, *tables(8 * rows))
    gains = kept[1]
    residual = inputs[0].astype(F32)
    outputs, d_hidden, d_heads, mlp_rows, *grads = mlp(
        inputs[0], own_heads, out_grad[0], gains, full_output, full_gate, full_up, full_down)
    (gate_g, up_g, down_g, output_g), back, d_normed = backward(grads, x, d_heads, mlp_rows, kept)
    _, norm_pull = jax.vjp(lambda r: root_mean_norm(r, gains[0:2].reshape(width)), residual)
    input_grad = d_hidden + norm_pull(d_normed)[0]

    def side_by_side(lo, hi):
        return jnp.concatenate([back[i, :depth, lo:hi] for i in range(8)], axis=1).astype(F32)

    query_g, key_g, value_g = side_by_side(0, 2 * HEAD), side_by_side(2 * HEAD, 3 * HEAD), side_by_side(3 * HEAD, 4 * HEAD)
    small_g = jnp.sum(back[:, depth:, :].astype(F32), axis=0)

    def mine(values, size):
        return lax.dynamic_slice_in_dim(values, f * size, size)

    return (outputs[None], input_grad[None], query_g, key_g, value_g, output_g.astype(F32), gate_g.astype(F32),
            up_g.astype(F32), down_g.astype(F32), mine(small_g[0:2].reshape(width), depth), mine(small_g[2:4].reshape(width), depth),
            mine(small_g[4, :HEAD], HEAD // 16), mine(small_g[4, HEAD:2 * HEAD], HEAD // 16))


def solution(mesh):
    seq, weight, gain = P("fsdp", "ctx", None), P("fsdp", None), P("fsdp")
    in_specs = (seq, P("fsdp", "ctx")) + (weight,) * 7 + (gain,) * 4 + (seq,)
    out_specs = (seq, seq) + (weight,) * 7 + (gain,) * 4
    return jax.shard_map(body, mesh=mesh, in_specs=in_specs, out_specs=out_specs, check_vma=False)
```

```python
import functools
import math

import jax
import jax.numpy as jnp
import numpy as np
from jax import lax
from jax.experimental import pallas as pl
from jax.experimental.pallas import tpu as pltpu
from jax.sharding import PartitionSpec as P

MESH = pl.DeviceIdType.MESH
HEAD = 128
EPSILON = 1e-06
THETA = 1000000.0
BF16, F32 = jnp.bfloat16, jnp.float32
FACTOR = 1.0 / math.sqrt(HEAD)
ANY = pl.BlockSpec(memory_space=pl.ANY)
VM = pl.BlockSpec(memory_space=pltpu.VMEM)
DMA = pltpu.SemaphoreType.DMA


def fid(zl, y, k):
    return zl * 8 + y * 2 + k


class Net:
    def __init__(self):
        f, c = lax.axis_index("fsdp"), lax.axis_index("ctx")
        zl, y, k, zh, x = f // 8, (f // 2) % 4, f % 2, c // 4, c % 4
        self.zl, self.y, self.k, self.zh, self.x = zl, y, k, zh, x
        self.z = zh * 2 + zl
        self.f, self.c = f, c
        self.yp, self.ym = self.along("y", 1), self.along("y", 3)
        self.zp, self.zm = self.along("z", 1), self.along("z", 3)
        self.xp, self.xm = self.along("x", 1), self.along("x", 3)
        self.pair = (fid(1 - zl, y, k), c)
        self.sib = (fid(zl, y, 1 - k), c)
        self.peer_c = (1 - zh) * 4 + x
        self.peer = (f, self.peer_c)

    def at(self, dim):
        return {"y": self.y, "x": self.x, "z": self.z}[dim]

    def along(self, dim, off):
        there = (self.at(dim) + off) % 4
        if dim == "y":
            return (fid(self.zl, there, self.k), self.c)
        if dim == "x":
            return (self.f, self.zh * 4 + there)
        return (fid(there % 2, self.y, self.k), (there // 2) * 4 + self.x)

    def ctx(self, off):
        return (self.c + off) % 8


def barrier(devices):
    sem = pltpu.get_barrier_semaphore()
    for d in devices:
        pl.semaphore_signal(sem, inc=1, device_id=d, device_id_type=MESH)
    pl.semaphore_wait(sem, len(devices))


class Copy:
    def __init__(self, copy, made_by):
        self.copy, self.made_by = copy, made_by
        if not made_by.again:
            copy.start()

    def wait_recv(self):
        if not self.made_by.again:
            self.copy.wait_recv()

    def wait(self):
        if not self.made_by.again:
            self.copy.wait()


class Wire:
    def __init__(self, send, recv, again=False):
        self.send, self.recv, self.n, self.all, self.again = send, recv, 0, [], again

    def __call__(self, src, dst, device):
        i = self.n
        self.n += 1
        copy = pltpu.make_async_remote_copy(
            src_ref=src, dst_ref=dst, send_sem=self.send.at[i], recv_sem=self.recv.at[i],
            device_id=device, device_id_type=MESH)
        self.all.append(copy)
        return Copy(copy, self)

    def finish(self):
        for copy in self.all:
            copy.wait_send()


class Local:
    def __init__(self, sems, again=False):
        self.sems, self.n, self.again = sems, 0, again

    def __call__(self, src, dst):
        i = self.n
        self.n += 1
        return Copy(None if self.again else pltpu.make_async_copy(src, dst, self.sems.at[i]), self)


def sems(wires, local):
    return [DMA((wires,)), DMA((wires,)), DMA((local,))]


def talking(number, name, **more):
    return dict(
        compiler_params=pltpu.CompilerParams(
            collective_id=number, has_side_effects=True, vmem_limit_bytes=63 << 20),
        name=name, **more)
def quarters(rows):
    if rows % 64 == 0:
        q = rows // 4
        return (0, q, 2 * q, 3 * q, rows)
    return (0, 16, 32, 48, rows)


class WeightFlow:
    def __init__(self, net, wire, src, out, paired=False):
        self.net, self.wire, self.src, self.out = net, wire, src, out
        self.zp, self.zm = (net.pair, net.pair) if paired else (net.zp, net.zm)
        self.rows = src.shape[0]
        self.q = quarters(self.rows)
        self.c = {}

    def place(self, dz, dy, a=0, b=4):
        n = self.net
        zl = n.zl if dz == 0 else 1 - n.zl
        at = fid(zl, (n.y + dy + 4) % 4, n.k) * self.rows + self.q[a]
        return self.out.at[pl.ds(pl.multiple_of(at, 16), self.q[b] - self.q[a])]

    def own(self, a=0, b=4):
        return self.src.at[pl.ds(self.q[a], self.q[b] - self.q[a])]

    def pass_on(self, name, device, dz, dy, a=0, b=4):
        ref = self.place(dz, dy, a, b)
        self.c[name] = self.wire(ref, ref, device)

    def got(self, name):
        self.c[name].wait_recv()

    def stage(self, s):
        n, w, c = self.net, self.wire, self.c
        if s == 0:
            c["yp"] = w(self.own(), self.place(0, 0), n.yp)
            c["ym"] = w(self.own(), self.place(0, 0), n.ym)
            c["zp"] = w(self.own(0, 2), self.place(0, 0, 0, 2), self.zp)
            c["zm"] = w(self.own(2, 4), self.place(0, 0, 2, 4), self.zm)
            c["d"] = w(self.own(), self.place(0, 0), n.sib)
        elif s == 1:
            self.got("yp")
            self.pass_on("yp2", n.yp, 0, -1, 0, 2)
            self.pass_on("zp_m", self.zp, 0, -1, 0, 2)
            self.pass_on("zm_m", self.zm, 0, -1, 2, 4)
            self.pass_on("d_m", n.sib, 0, -1)
            self.got("ym")
            self.pass_on("ym2", n.ym, 0, 1, 2, 4)
            self.pass_on("zp_p", self.zp, 0, 1, 0, 2)
            self.pass_on("zm_p", self.zm, 0, 1, 2, 4)
            self.pass_on("d_p", n.sib, 0, 1)
            self.got("zp")
            self.pass_on("dz0", n.sib, 1, 0, 0, 2)
            self.got("zm")
            self.pass_on("dz1", n.sib, 1, 0, 2, 4)
        elif s == 2:
            self.got("yp2")
            self.pass_on("zp_2", self.zp, 0, 2, 0, 1)
            self.pass_on("d2a", n.sib, 0, 2, 0, 2)
            self.got("ym2")
            self.pass_on("zm_2", self.zm, 0, 2, 2, 3)
            self.pass_on("d2b", n.sib, 0, 2, 2, 4)
            self.got("zp_m")
            self.pass_on("yq", n.yp, 1, -1, 1, 2)
            self.pass_on("dzm0", n.sib, 1, -1, 0, 2)
            self.got("zm_p")
            self.pass_on("yr", n.ym, 1, 1, 3, 4)
            self.pass_on("dzp1", n.sib, 1, 1, 2, 4)
            self.got("zm_m")
            self.pass_on("dzm1", n.sib, 1, -1, 2, 4)
            self.got("zp_p")
            self.pass_on("dzp0", n.sib, 1, 1, 0, 2)
        elif s == 3:
            self.got("zp_2")
            self.got("yq")
            self.pass_on("dz20", n.sib, 1, 2, 0, 2)
            self.got("zm_2")
            self.got("yr")
            self.pass_on("dz21", n.sib, 1, 2, 2, 4)
        elif s == 4:
            for name in ("d", "d_m", "d_p", "dz0", "dz1", "d2a", "d2b", "dzm0", "dzp1", "dzm1", "dzp0", "dz20", "dz21"):
                self.got(name)


class SharedFlow(WeightFlow):
    def quarter(self, dz, dy, hi, own=False):
        n, q = self.net, self.rows // 4
        zl = n.zl if dz == 0 else 1 - n.zl
        at = (2 * hi + n.x % 2) * q
        if own:
            return self.src.at[pl.ds(pl.multiple_of(at, 16), q)]
        return self.out.at[pl.ds(pl.multiple_of(fid(zl, (n.y + dy + 4) % 4, n.k) * self.rows + at, 16), q)]

    def hand(self, name, device, dz, dy, hi):
        ref = self.quarter(dz, dy, hi)
        self.c[name] = self.wire(ref, ref, device)

    def along_z(self, tag, dy):
        self.hand("zp" + tag, self.zp, 0, dy, 0)
        self.hand("zm" + tag, self.zm, 0, dy, 1)

    def along_x(self, tag, dy):
        self.got("zp" + tag)
        self.hand("xp" + tag, self.net.xp, 1, dy, 0)
        self.got("zm" + tag)
        self.hand("xm" + tag, self.net.xm, 1, dy, 1)

    def to_sibling(self, tag, dy):
        self.got("xp" + tag)
        self.got("xm" + tag)
        self.pass_on("dz" + tag, self.net.sib, 1, dy)

    def stage(self, s):
        n, w, c = self.net, self.wire, self.c
        if s == 0:
            c["yp"] = w(self.own(), self.place(0, 0), n.yp)
            c["ym"] = w(self.own(), self.place(0, 0), n.ym)
            c["zp0"] = w(self.quarter(0, 0, 0, True), self.quarter(0, 0, 0), self.zp)
            c["zm0"] = w(self.quarter(0, 0, 1, True), self.quarter(0, 0, 1), self.zm)
            c["d"] = w(self.own(), self.place(0, 0), n.sib)
        elif s == 1:
            self.got("yp")
            self.pass_on("yp2", n.yp, 0, -1, 0, 2)
            self.along_z("m", -1)
            self.pass_on("d_m", n.sib, 0, -1)
            self.got("ym")
            self.pass_on("ym2", n.ym, 0, 1, 2, 4)
            self.along_z("p", 1)
            self.pass_on("d_p", n.sib, 0, 1)
            self.along_x("0", 0)
        elif s == 2:
            self.got("yp2")
            self.hand("zp2", self.zp, 0, 2, 0)
            self.pass_on("d2a", n.sib, 0, 2, 0, 2)
            self.got("ym2")
            self.hand("zm2", self.zm, 0, 2, 1)
            self.pass_on("d2b", n.sib, 0, 2, 2, 4)
            self.along_x("m", -1)
            self.along_x("p", 1)
            self.to_sibling("0", 0)
        elif s == 3:
            self.along_x("2", 2)
            self.to_sibling("m", -1)
            self.to_sibling("p", 1)
        elif s == 4:
            self.to_sibling("2", 2)
            for name in ("d", "d_m", "d_p", "d2a", "d2b", "dz0", "dzm", "dzp", "dz2"):
                self.got(name)


class RowFlow:
    def __init__(self, net, wire, src, out):
        self.net, self.wire, self.src, self.out = net, wire, src, out
        self.rows = src.shape[0]
        self.c = {}

    def place(self, ctx, a=0, b=2):
        lo, hi = a * self.rows // 2, b * self.rows // 2
        return self.out.at[pl.ds(pl.multiple_of(ctx * self.rows + lo, 16), hi - lo)]

    def pass_on(self, name, device, ctx, a=0, b=2):
        ref = self.place(ctx, a, b)
        self.c[name] = self.wire(ref, ref, device)

    def got(self, name):
        self.c[name].wait_recv()

    def stage(self, s):
        n, w, c = self.net, self.wire, self.c
        left, right = n.zh * 4 + (n.x + 3) % 4, n.zh * 4 + (n.x + 1) % 4
        left2, right2 = (1 - n.zh) * 4 + (n.x + 3) % 4, (1 - n.zh) * 4 + (n.x + 1) % 4
        if s == 0:
            c["pz"] = w(self.src, self.place(n.c), n.peer)
            c["xp"] = w(self.src, self.place(n.c), n.xp)
            c["xm"] = w(self.src, self.place(n.c), n.xm)
        elif s == 1:
            self.got("pz")
            self.pass_on("px", n.xp, n.peer_c)
            self.pass_on("pxm", n.xm, n.peer_c)
            self.got("xp")
            self.pass_on("xp2", n.xp, left, 0, 1)
            self.got("xm")
            self.pass_on("xm2", n.xm, right, 1, 2)
        elif s == 2:
            self.got("px")
            self.pass_on("px2", n.xp, left2, 0, 1)
            self.got("pxm")
            self.pass_on("pxm2", n.xm, right2, 1, 2)
        elif s == 3:
            for name in ("xp2", "xm2", "px2", "pxm2"):
                self.got(name)


class Later:
    def __init__(self, steps):
        self.steps = list(steps)

    def __call__(self):
        if self.steps:
            self.steps.pop(0)()

    def rest(self):
        while self.steps:
            self()


def stage(flow, *numbers):
    def go():
        for s in numbers:
            flow.stage(s)
    return go


def together(*steps):
    def go():
        for s in steps:
            s()
    return go


class Spread:
    def __init__(self, net, wire, here, forward, src, dst):
        rows, cols = (dst.shape[0], src.shape[1]) if forward else (src.shape[0], dst.shape[1])

        def by_row(ref, c):
            return ref.at[pl.ds(pl.multiple_of(c * rows, 16), rows)]

        def by_col(ref, c):
            return ref.at[:, pl.ds(pl.multiple_of(c * cols, 128), cols)]

        pick, put = (by_row, by_col) if forward else (by_col, by_row)
        self.copies = []
        for o in (6, 2, 4, 5, 7, 1, 3):
            there = net.ctx(o)
            self.copies.append(wire(pick(src, there), put(dst, net.c), (net.f, there)))
        self.own = here(pick(src, net.c), put(dst, net.c))

    def end(self):
        for copy in self.copies:
            copy.wait_recv()
        self.own.wait()


def neighbours(net):
    return ([net.sib] + [net.along(d, o) for d in "yz" for o in (1, 2, 3)] + [(net.f, net.ctx(o)) for o in (1, 2, 3, 5, 6, 7)])


KEPT = 11


def forward_kernel(nw, *refs):
    srcs, rows, cos_in, sin_in = refs[:nw], refs[nw], refs[nw + 1], refs[nw + 2]
    refs = refs[nw + 3:]
    outs, rows_out, own_heads, kept_out = refs[:nw - 1], refs[nw - 1], refs[nw], refs[nw + 1:nw + 1 + KEPT]
    refs = refs[nw + 1 + KEPT:]
    x, t, cos_at, sin_at, heads = refs[:5]
    kept = refs[5:5 + KEPT]
    send, recv, local = refs[5 + KEPT:]
    w, gains, q, k, v, lin, cs, sn, start, hf, inv = kept
    net, wire, here = Net(), Wire(send, recv), Local(local)
    barrier(neighbours(net))
    first, out_f, gate_f, up_f, down_f = [
        kind(net, wire, s, o, i == 0)
        for i, (kind, s, o) in enumerate(zip((WeightFlow, WeightFlow, WeightFlow, SharedFlow, SharedFlow), srcs, (t, *outs)))]
    flows = (first, out_f, gate_f, up_f, down_f)
    seq = RowFlow(net, wire, rows, x)
    first.stage(0)
    seq.stage(0)
    out_f.stage(0)
    gate_f.stage(0)
    tables_in = [here(cos_in, cos_at), here(sin_in, sin_at)]
    placed_here = [here(fl.src, fl.place(0, 0)) for fl in flows]
    placed_here.append(here(rows, seq.place(net.c)))
    first.stage(1)
    out_f.stage(1)
    up_f.stage(0)
    first.stage(2)
    seq.stage(1)
    gate_f.stage(1)
    down_f.stage(0)
    first.stage(3)
    out_f.stage(2)
    seq.stage(2)
    up_f.stage(1)
    first.stage(4)
    gate_f.stage(2)
    seq.stage(3)
    for c in tables_in + placed_here:
        c.wait()
    saved = [here(x, rows_out)]
    tick = Later([
        together(stage(down_f, 1), stage(out_f, 3)),
        stage(up_f, 2),
        stage(gate_f, 3),
        stage(down_f, 2),
        stage(up_f, 3),
        stage(down_f, 3),
    ])
    attn_forward(tick, x, t, cos_at, sin_at, w, gains, q, k, v, lin, cs, sn, start, hf, heads, inv)
    spread = Spread(net, wire, here, True, heads, own_heads)
    saved += [here(a, b) for a, b in zip(kept, kept_out)]
    tick.rest()
    for fl in flows[1:]:
        fl.stage(4)
    spread.end()
    for c in saved:
        c.wait()
    wire.finish()


def shapes(*items):
    return [jax.ShapeDtypeStruct(s, d) for s, d in items]


def forward(weights, rows, cos_in, sin_in):
    nw = len(weights)
    per, cols = weights[0].shape
    length = 8 * rows.shape[0]
    kept = shapes(
        ((16 * (per - 16), cols), BF16), ((16, cols), F32), ((2, length, HEAD), BF16), ((length, HEAD), BF16),
        ((length, HEAD), BF16), ((length, 3 * HEAD), F32), ((length, HEAD), F32), ((length, HEAD), F32),
        ((length, HEAD), F32), ((length, 2 * HEAD), F32), ((2, length, HEAD), F32))
    outs = [jax.ShapeDtypeStruct((16 * w.shape[0], w.shape[1]), w.dtype) for w in weights[1:]]
    outs += shapes(((length, rows.shape[1]), BF16), ((rows.shape[0], 16 * HEAD), BF16)) + kept
    scratch = [((length, rows.shape[1]), BF16), ((16 * per, cols), BF16), ((length, HEAD), F32), ((length, HEAD), F32), ((length, 2 * HEAD), BF16)]
    res = pl.pallas_call(
        functools.partial(forward_kernel, nw),
        out_shape=outs, in_specs=[ANY] * (nw + 3), out_specs=[ANY] * len(outs),
        scratch_shapes=[pltpu.VMEM(s, d) for s, d in scratch] + [pltpu.VMEM(a.shape, a.dtype) for a in kept]
        + sems(29 * nw + 9 + 7, nw + 3 + 1 + 1 + KEPT), **talking(0, "layer_forward"),
    )(*weights, rows, cos_in, sin_in)
    return res[:nw - 1], res[nw - 1], res[nw], res[nw + 1:]
def block(i, size):
    return pl.ds(pl.multiple_of(i * size, size), size)


def dot_t(left, right):
    return lax.dot_general(left, right, (((1,), (1,)), ((), ())), preferred_element_type=F32)


def t_dot(left, right):
    return lax.dot_general(left, right, (((0,), (0,)), ((), ())), preferred_element_type=F32)


def plain_dot(left, right):
    return jnp.dot(left, right, preferred_element_type=F32)


def unit(v):
    r = lax.rsqrt(jnp.mean(v * v, axis=-1, keepdims=True) + EPSILON)
    return v * r, r


ROWS = 256


def attn_forward(tick, x, t, cos_in, sin_in, w, gains, q, k, v, lin, cs, sn, start, hf, heads, inv):
    length, width = x.shape[0], x.shape[1] - HEAD
    per = t.shape[0] // 16
    depth = per - 16
    total = jnp.zeros((16, t.shape[1]), F32)
    for f in range(16):
        w[f * depth:(f + 1) * depth, :] = t[f * per:f * per + depth, :]
        total = total + t[f * per + depth:(f + 1) * per, :].astype(F32)
    gains[...] = total
    attn_gain = jnp.concatenate([total[0:1], total[1:2]], axis=1)
    query_gain, key_gain = total[4:5, 0:HEAD], total[4:5, HEAD:2 * HEAD]

    def count(i, carry):
        doc = x[block(i, ROWS), width:].astype(F32)
        return (carry[0] + jnp.sum((doc < 0.5).astype(F32), axis=0, keepdims=True),
                carry[1] + jnp.sum((doc < 1.5).astype(F32), axis=0, keepdims=True))

    zero = jnp.zeros((1, HEAD), F32)
    first, second = lax.fori_loop(0, length // ROWS, count, (zero, zero))
    lanes = lax.broadcasted_iota(jnp.int32, (1, HEAD), 1) % (HEAD // 2)
    freqs = jnp.exp(lanes.astype(F32) * (-2.0 * math.log(THETA) / HEAD))
    c1, s1 = jnp.cos(first * freqs), jnp.sin(first * freqs)
    c2, s2 = jnp.cos(second * freqs), jnp.sin(second * freqs)
    sign = jnp.where(lax.broadcasted_iota(jnp.int32, (1, HEAD), 1) < HEAD // 2, -1.0, 1.0)

    def prepare(i, carry):
        rows = block(i, ROWS)
        doc = x[rows, width:].astype(F32)
        start[rows, :] = jnp.where(doc < 0.5, 0.0, jnp.where(doc < 1.5, first, second))
        cd = jnp.where(doc < 0.5, 1.0, jnp.where(doc < 1.5, c1, c2))
        sd = jnp.where(doc < 0.5, 0.0, jnp.where(doc < 1.5, s1, s2))
        ci, si = cos_in[rows, :], sin_in[rows, :]
        cosine = ci * cd + si * sd
        sine = (si * cd - ci * sd) * sign
        cs[rows, :] = cosine
        sn[rows, :] = sine
        normed = (unit(x[rows, :width].astype(F32))[0] * attn_gain).astype(BF16)
        out = plain_dot(normed, w[...])
        lin[rows, :] = out[:, :3 * HEAD]
        v[rows, :] = out[:, 3 * HEAD:].astype(BF16)
        for h in range(3):
            e = unit(out[:, h * HEAD:(h + 1) * HEAD])[0] * (query_gain if h < 2 else key_gain)
            e = (e * cosine + pltpu.roll(e, HEAD // 2, 1) * sine).astype(BF16)
            if h < 2:
                q[h, rows, :] = e
            else:
                k[rows, :] = e
        return carry

    for i in range(0, length // ROWS, 2):
        lax.fori_loop(i, i + 2, prepare, 0)
        tick()

    def queries(i, carry):
        rows = block(i, ROWS)
        here = q[:, rows, :].reshape(2 * ROWS, HEAD)
        begin = start[rows, :]

        def keys(j, state):
            acc, norm = state
            these = block(j, ROWS)
            p = jnp.exp(dot_t(here, k[these, :]) * FACTOR)
            p = jnp.where(allowed_at(i, j, begin), p.reshape(2, ROWS, ROWS), 0.0).reshape(2 * ROWS, ROWS)
            norm = norm + p[:, :HEAD] + p[:, HEAD:]
            return acc + plain_dot(p.astype(BF16), v[these, :]), norm

        zeros = jnp.zeros((2 * ROWS, HEAD), F32)
        acc, norm = lax.fori_loop(0, i + 1, keys, (zeros, zeros))
        over = jnp.broadcast_to(1.0 / jnp.sum(norm, axis=1, keepdims=True), (2 * ROWS, HEAD))
        acc = acc * over
        inv[:, rows, :] = over.reshape(2, ROWS, HEAD)
        for h in range(2):
            part = acc[h * ROWS:(h + 1) * ROWS]
            hf[rows, h * HEAD:(h + 1) * HEAD] = part
            heads[rows, h * HEAD:(h + 1) * HEAD] = part.astype(BF16)
        return carry

    for i, j in ((0, 3), (3, 4), (4, 5), (5, 6)):
        lax.fori_loop(i, j, queries, 0)
        tick()


def allowed_at(i, j, begin):
    own = lax.broadcasted_iota(jnp.int32, (ROWS, ROWS), 0) + i * ROWS
    other = lax.broadcasted_iota(jnp.int32, (ROWS, ROWS), 1) + j * ROWS
    begin = jnp.concatenate([begin, begin], axis=1)
    return ((other.astype(F32) >= begin) & (other <= own))[None]


def attn_backward(tick, gains, q, k, v, start, hf, inv, dh, dq, dk, dv, delta):
    length = dh.shape[0]
    blocks = length // ROWS

    def before(i, carry):
        rows = block(i, ROWS)
        for h in range(2):
            cols = slice(h * HEAD, (h + 1) * HEAD)
            s = jnp.sum(dh[rows, cols].astype(F32) * hf[rows, cols], axis=1, keepdims=True)
            delta[h, rows, :] = jnp.broadcast_to(s, (ROWS, HEAD))
            dq[h, rows, :] = jnp.zeros((ROWS, HEAD), F32)
        return carry

    lax.fori_loop(0, blocks, before, 0)

    def keys(j, carry):
        these = block(j, ROWS)
        kt, vt = k[these, :], v[these, :]

        def queries(i, state):
            d_key, d_value = state
            rows = block(i, ROWS)
            here = q[:, rows, :].reshape(2 * ROWS, HEAD)
            grad = jnp.concatenate([dh[rows, :HEAD], dh[rows, HEAD:]], axis=0)
            over = inv[:, rows, :].reshape(2 * ROWS, HEAD)
            off = delta[:, rows, :].reshape(2 * ROWS, HEAD)
            over = jnp.concatenate([over, over], axis=1)
            off = jnp.concatenate([off, off], axis=1)
            p = jnp.exp(dot_t(here, kt) * FACTOR) * over
            p = jnp.where(allowed_at(i, j, start[rows, :]), p.reshape(2, ROWS, ROWS), 0.0).reshape(2 * ROWS, ROWS)
            ds = (p * (dot_t(grad, vt) - off)).astype(BF16)
            dq[:, rows, :] = dq[:, rows, :] + plain_dot(ds, kt).reshape(2, ROWS, HEAD)
            return d_key + t_dot(ds, here), d_value + t_dot(p.astype(BF16), grad)

        zeros = jnp.zeros((ROWS, HEAD), F32)
        d_key, d_value = lax.fori_loop(j, blocks, queries, (zeros, zeros))
        dk[these, :] = d_key
        dv[these, :] = d_value
        return carry

    for i, j in ((0, 1), (1, 2), (2, 4), (4, 6)):
        lax.fori_loop(i, j, keys, 0)
        tick()


WIDE = 384


def attn_backward_end(x, w, gains, lin, cs, sn, dq, dk, dv, dlin, dw, dn):
    length, width = x.shape[0], x.shape[1] - HEAD
    g = gains[...]
    attn_gain = jnp.concatenate([g[0:1], g[1:2]], axis=1)
    query_gain, key_gain = g[4:5, 0:HEAD], g[4:5, HEAD:2 * HEAD]

    def after(i, carry):
        d_attn, d_query, d_key = carry
        rows = block(i, WIDE)
        cosine, sine = cs[rows, :], sn[rows, :]
        for h in range(3):
            cols = slice(h * HEAD, (h + 1) * HEAD)
            d = (dq[h, rows, :] if h < 2 else dk[rows, :]) * FACTOR
            d = d * cosine - pltpu.roll(d, HEAD // 2, 1) * sine
            e, r = unit(lin[rows, cols])
            s = jnp.sum(d * e, axis=0, keepdims=True)
            d_query, d_key = (d_query + s, d_key) if h < 2 else (d_query, d_key + s)
            d = d * (query_gain if h < 2 else key_gain)
            d = r * (d - e * jnp.mean(d * e, axis=-1, keepdims=True))
            dlin[rows, cols] = d.astype(BF16)
        dlin[rows, 3 * HEAD:] = dv[rows, :].astype(BF16)
        part = dot_t(dlin[rows, :], w[...])
        e = unit(x[rows, :width].astype(F32))[0]
        d_attn = d_attn + jnp.sum(part * e, axis=0, keepdims=True)
        dn[i // 2, pl.ds((i % 2) * 2, 2)] = part.astype(BF16).reshape(2, WIDE // 2, width)
        normed = (e * attn_gain).astype(BF16)

        part = t_dot(normed, dlin[rows, :])
        dw[...] = jnp.where(i == 0, part, dw[...] + part)
        return d_attn, d_query, d_key

    zero = jnp.zeros((1, HEAD), F32)
    dw[...] = jnp.zeros_like(dw)
    return lax.fori_loop(0, length // WIDE, after, (jnp.zeros((1, width), F32), zero, zero))


def shapes(*items):
    return [jax.ShapeDtypeStruct(s, d) for s, d in items]


def add_rows(out, parts, rows, step):
    def some(r, carry):
        here = pl.ds(pl.multiple_of(r * step, 16), step)
        if len(parts) == 2:
            out(here, parts[0](here) + parts[1](here))
            return carry
        total = parts[0](here).astype(F32)
        for part in parts[1:]:
            total = total + part(here).astype(F32)
        out(here, total.astype(BF16))
        return carry

    lax.fori_loop(0, rows // step, some, 0)


FIRST = (2, 1, 3, 0)


class SumFlow:
    def __init__(self, net, wire, here, src, first, order, slots, other, relay, got, part, fin, out):
        self.net, self.wire, self.here, self.src, self.first, self.order = net, wire, here, src, first, order
        self.slots, self.other, self.relay, self.got, self.part, self.fin, self.out = slots, other, relay, got, part, fin, out
        self.rows, self.cols = other.shape[2], other.shape[3]
        self.w = self.cols // 8
        self.far, self.via = {}, {}

    def cut(self, ref, dim, d, k=None):
        tail = ref.shape[-1]
        a = (slice(None), slice(None))
        cols = pl.ds(0, tail)
        if dim == "y":
            a = (slice(None), pl.ds(d, 1))
        elif dim == "x":
            cols = pl.ds(pl.multiple_of(d * (tail // 4), 128), tail // 4)
        else:
            a = (pl.ds(d % 2, 1), slice(None))
            cols = pl.ds(pl.multiple_of((d // 2) * (tail // 2), 128), tail // 2)
        if k is None:
            return ref.at[a[0], a[1], :, cols]
        return ref.at[a[0], a[1], k, pl.ds(self.first, self.rows), cols]

    def begin(self):
        self.near, self.own = {}, {}
        self.bring(0)
        self.bring(1)

    def bring(self, i):
        n, dim = self.net, self.order[0]
        o = FIRST[i]
        d = (n.at(dim) + o) % 4
        self.near[o] = self.wire(self.cut(self.src, dim, d, 1 - n.k), self.cut(self.other, dim, d), n.sib)
        self.own[o] = self.here(self.cut(self.src, dim, d, n.k), self.slots.at[i % 2])

    def add(self, out, parts):
        if self.wire.again:
            return
        a, b = out.shape[0], out.shape[1]
        step = 16
        for i in range(a):
            for j in range(b):
                def take(ref):
                    return lambda here: ref[i, j, here, :]

                def put(here, value):
                    out[i, j, here, :] = value
                add_rows(put, [take(p) for p in parts], out.shape[2], step)

    def chip(self, o):
        n, dim = self.net, self.order[0]
        d = (n.at(dim) + o) % 4
        self.near[o].wait_recv()
        self.own[o].wait()
        i = FIRST.index(o)
        piece = self.cut(self.other, dim, d)
        self.add(piece, [piece, self.slots.at[i % 2]])
        if i + 2 < 4:
            self.bring(i + 2)
        half = self.rows // 2
        if o == 2:
            for which, to in ((0, 1), (1, 3)):
                self.via[to] = self.wire(piece.at[:, :, pl.ds(which * half, half)], self.relay.at[which], n.along(dim, to))
        elif o:
            which = 0 if o == 1 else 1
            self.via[o].wait_recv()
            part = piece.at[:, :, pl.ds(which * half, half)]
            self.add(part, [part, self.relay.at[which]])
            self.far[o] = self.wire(piece, self.got[0].at[which], n.along(dim, o))

    def phase(self, p):
        n, dim = self.net, self.order[p]
        held = self.other if p == 0 else self.part[p - 1]
        for o in (1, 3, 2) if p else (1, 3):
            self.far[o].wait_recv()
        result = self.part[p] if p < 2 else self.fin
        self.add(result, [self.cut(held, dim, n.at(dim))] + [self.got[p].at[i] for i in range(3 if p else 2)])
        if p < 2:
            after = self.order[p + 1]
            for o in (2, 1, 3):
                d = (n.at(after) + o) % 4
                self.far[o] = self.wire(self.cut(result, after, d), self.got[p + 1].at[o - 1], n.along(after, o))
        else:
            fin, to = self.fin.at[0, 0], self.place(n.zh)
            self.across = self.wire(fin, to, n.peer)
            self.last = [self.wire(fin, to, n.along("x", o)) for o in (2, 1, 3)]
            self.kept = self.here(fin, to)

    def place(self, zh):
        n = self.net
        s = zh * 4 + n.x if self.order.index("z") < self.order.index("x") else n.x * 2 + zh
        return self.out.at[pl.ds(self.first, self.rows), pl.ds(pl.multiple_of(s * self.w, 128), self.w)]

    def share(self):
        n = self.net
        self.across.wait_recv()
        to = self.place(1 - n.zh)
        self.last += [self.wire(to, to, n.along("x", o)) for o in (2, 1, 3)]

    def end(self):
        for copy in self.last:
            copy.wait_recv()
        self.kept.wait()


def sum_shapes(rows, cols, order):
    shape, out = [2, 4, rows, cols], []
    for dim in order:
        if dim == "y":
            shape[1] = 1
        elif dim == "x":
            shape[3] //= 4
        else:
            shape[0], shape[3] = 1, shape[3] // 2
        out.append(tuple(shape))
    return out


PLAN = ((0, 0, 64, "yxz"), (1, 0, 64, "xzy"), (2, 0, 192, "zyx"), (3, 0, 64, "yzx"), (3, 64, 64, "yxz"))


def first_shapes(plan, shapes_in):
    return [sum_shapes(rows, shapes_in[which][-1], order)[0] for which, _, rows, order in plan]


def sum_scratch(plan, shapes_in):
    held = []
    for which, first, rows, order in plan:
        cols = shapes_in[which][-1]
        a, b, c = sum_shapes(rows, cols, order)
        half = (a[0], a[1], a[2] // 2, a[3])
        held += [pltpu.VMEM(s, BF16) for s in ((2, 4, rows, cols), (2, *half), (2, *a), (3, *b), (3, *c), a, b, c)]
    return held


def make_flows(net, wire, here, plan, srcs, outs, held, slots):
    flows = []
    for n, (which, first, rows, order) in enumerate(plan):
        other, relay, g0, g1, g2, p0, p1, fin = held[8 * n:8 * n + 8]
        flows.append(SumFlow(net, wire, here, srcs[which], first, order, slots[n], other, relay, (g0, g1, g2), (p0, p1), fin, outs[which]))
    return flows


class Ends:
    def __init__(self, net, wire, here, dwx, dn, rows_out, dn_out, other, got, fin, got_xa, part_a, got_za, got_zb, part_b, got_xb):
        self.net, self.wire, self.here, self.dwx, self.dn, self.rows_out, self.dn_out = net, wire, here, dwx, dn, rows_out, dn_out
        self.other, self.got, self.fin = other, got, fin
        self.got_xa, self.part_a, self.got_za, self.got_zb, self.part_b, self.got_xb = got_xa, part_a, got_za, got_zb, part_b, got_xb
        self.half = part_a.shape[-1]
        self.rows = part_a.shape[1]

    def begin(self):
        n, h = self.net, self.half
        self.over_b = self.wire(self.dn.at[1 - n.zh, :, :, pl.ds(h, h)], self.got_zb, n.peer)
        self.moved_a = [self.wire(self.dn.at[:, (n.x + o) % 4, :, pl.ds(0, h)], self.got_xa.at[o - 1], n.along("x", o)) for o in (2, 1, 3)]
        self.near = self.wire(self.dwx.at[:, :, 1 - n.k], self.other, n.sib)

    def chip(self):
        n = self.net
        self.near.wait_recv()
        for a in range(2):
            for b in range(4):
                self.other[a, b] = self.other[a, b] + self.dwx[a, b, n.k]
        self.far = []
        for dz in (1, 0):
            for dy in (2, 1, 3, 0):
                if dz or dy:
                    there = ((n.zl + dz) % 2, (n.y + dy) % 4)
                    self.far.append(self.wire(self.other.at[there[0], there[1]], self.got.at[dz * 4 + dy - 1], (fid(there[0], there[1], n.k), n.c)))

    def along_z(self):
        n, h = self.net, self.half
        self.over_b.wait_recv()
        for x in range(4):
            def put(here, value):
                self.part_b[x, here, :] = value
            add_rows(put, [lambda here: self.dn[n.zh, x, here, h:], lambda here: self.got_zb[x, here, :]], self.rows, 16)
        self.moved_b = [self.wire(self.part_b.at[(n.x + o) % 4], self.got_xb.at[o - 1], n.along("x", o)) for o in (2, 1, 3)]

    def along_x(self):
        n, h = self.net, self.half
        for copy in self.moved_a:
            copy.wait_recv()
        for zh in range(2):
            def take(o):
                return (lambda here: self.dn[zh, n.x, here, :h]) if o == 0 else (lambda here: self.got_xa[o - 1, zh, here, :])

            def put(here, value):
                self.part_a[zh, here, :] = value
            add_rows(put, [take(o) for o in range(4)], self.rows, 16)
        self.over_a = self.wire(self.part_a.at[1 - n.zh], self.got_za, n.peer)

    def share(self):
        n = self.net
        for copy in self.far:
            copy.wait_recv()
        total = self.other[n.zl, n.y].astype(F32)
        for i in range(7):
            total = total + self.got[i].astype(F32)
        self.fin[...] = total.astype(BF16)
        self.copies = [self.wire(self.fin, self.rows_out.at[n.c], (n.f, n.ctx(o))) for o in (6, 2, 4, 5, 7, 1, 3)]
        self.kept = self.here(self.fin, self.rows_out.at[n.c])

    def end(self):
        n, h = self.net, self.half
        self.over_a.wait_recv()
        for copy in self.moved_b:
            copy.wait_recv()

        def some(r, carry):
            at = pl.ds(pl.multiple_of(r * 16, 16), 16)
            self.dn_out[at, :h] = self.part_a[n.zh, at, :].astype(F32) + self.got_za[at, :].astype(F32)
            total = self.part_b[n.x, at, :].astype(F32)
            for o in range(3):
                total = total + self.got_xb[o, at, :].astype(F32)
            self.dn_out[at, h:] = total
            return carry

        lax.fori_loop(0, self.rows // 16, some, 0)
        for copy in self.copies:
            copy.wait_recv()
        self.kept.wait()


def backward_kernel(ng, *refs):
    srcs, x_in, d_heads, mlp_rows, kept_in = refs[:ng], refs[ng], refs[ng + 1], refs[ng + 2], refs[ng + 3:ng + 3 + KEPT]
    refs = refs[ng + 3 + KEPT:]
    outs, rows_out, dn_out = refs[:ng], refs[ng], refs[ng + 1]
    refs = refs[ng + 2:]
    kept, refs = refs[:KEPT], refs[KEPT:]
    w, gains, q, k, v, lin, cs, sn, start, hf, inv = kept
    dh, dq, dk, dv, delta, mlp_at, dwx, dn = refs[:8]
    end_held, refs = refs[8:17], refs[17:]
    held, (send, recv, local) = refs[:-3], refs[-3:]
    net = Net()
    length, width = x_in.shape[0], x_in.shape[1] - HEAD
    depth = w.shape[0] // 16

    def opening(wire, here, slots):
        spread = Spread(net, wire, here, False, d_heads, dh)
        flows = make_flows(net, wire, here, PLAN, srcs, outs, held, slots)
        for fl in flows:
            fl.begin()
        loads = [here(a, b) for a, b in zip(kept_in, kept)] + [here(mlp_rows, mlp_at)]

        def chips(o):
            def go():
                for fl in flows:
                    fl.chip(o)
            return go

        chips(2)()
        return spread, loads, Later([chips(1), chips(3), chips(0)]), flows

    def slotted(*slots):
        barrier(neighbours(net))
        spread, loads, tick, _ = opening(Wire(send, recv), Local(local), slots)
        for c in loads:
            c.wait()
        spread.end()
        attn_backward(tick, gains, q, k, v, start, hf, inv, dh, dq, dk, dv, delta)
        tick.rest()

    pl.run_scoped(slotted, *[pltpu.VMEM((2, *a), BF16) for a in first_shapes(PLAN, [s.shape for s in srcs])])
    wire, here = Wire(send, recv, True), Local(local, True)
    _, _, tick, flows = opening(wire, here, held[2::8])
    tick.rest()
    wire.again = here.again = False
    ends = Ends(net, wire, here, dwx, dn, rows_out, dn_out, *end_held)

    def ending(x, dlin, dw):
        fetch = pltpu.make_async_copy(x_in, x, local.at[local.shape[0] - 1])
        fetch.start()
        fetch.wait()
        d_attn, d_query, d_key = attn_backward_end(x, w, gains, lin, cs, sn, dq, dk, dv, dlin, dw, dn)
        cols = dw.shape[1]
        lanes = jnp.concatenate([d_query, d_key, jnp.zeros((1, cols - 2 * HEAD), F32)], axis=1)
        small = jnp.concatenate([d_attn[:, :cols], d_attn[:, cols:], jnp.zeros((2, cols), F32), lanes, jnp.zeros((11, cols), F32)], axis=0)
        small = (small + mlp_at[...]).astype(BF16)
        for f in range(16):
            at = (f // 8, (f // 2) % 4, f % 2)
            dwx[at[0], at[1], at[2], :depth, :] = dw[f * depth:(f + 1) * depth, :].astype(BF16)
            dwx[at[0], at[1], at[2], depth:, :] = small

    def phase(p):
        for fl in flows:
            fl.phase(p)

    def share():
        for fl in flows:
            fl.share()

    pl.run_scoped(ending, pltpu.VMEM((length, width + HEAD), BF16), pltpu.VMEM((length, 4 * HEAD), BF16), pltpu.VMEM((16 * depth, 4 * HEAD), F32))
    ends.begin()
    phase(0)
    phase(1)
    ends.chip()
    ends.along_z()
    ends.along_x()
    phase(2)
    ends.share()
    share()
    ends.end()
    for fl in flows:
        fl.end()
    wire.finish()


def backward(grads, x, d_heads, mlp_rows, kept):
    srcs = [g.reshape(2, 4, 2, g.shape[0] // 16, g.shape[1]) for g in grads]
    length, width = x.shape[0], x.shape[1] - HEAD
    rows, cols = length // 8, 4 * HEAD
    depth, half = width // 16, width // 2
    out = [jax.ShapeDtypeStruct((g.shape[0] // 16, g.shape[1]), BF16) for g in grads]
    out += shapes(((8, depth + 16, cols), BF16), ((rows, width), F32))
    scratch = [(a.shape, a.dtype) for a in kept]
    scratch += [((length, 2 * HEAD), BF16), ((2, length, HEAD), F32), ((length, HEAD), F32), ((length, HEAD), F32),
                ((2, length, HEAD), F32), (mlp_rows.shape, F32), ((2, 4, 2, depth + 16, cols), BF16), ((2, 4, rows, width), BF16)]
    scratch += [((2, 4, depth + 16, cols), BF16), ((7, depth + 16, cols), BF16), ((depth + 16, cols), BF16),
                ((3, 2, rows, half), BF16), ((2, rows, half), BF16), ((rows, half), BF16),
                ((4, rows, half), BF16), ((4, rows, half), BF16), ((3, rows, half), BF16)]
    ng = len(grads)
    wires = 21 * len(PLAN) + 7 + 3 + 1 + 3 + 1 + 7 + 1 + 7
    local = 5 * len(PLAN) + 1 + KEPT + 1 + 1 + 1
    res = pl.pallas_call(
        functools.partial(backward_kernel, ng), out_shape=out,
        in_specs=[ANY] * (ng + 3 + KEPT), out_specs=[ANY] * (ng + 1) + [VM],
        scratch_shapes=[pltpu.VMEM(s, d) for s, d in scratch] + sum_scratch(PLAN, [s.shape for s in srcs]) + sems(wires, local),
        **talking(1, "layer_backward"))(*srcs, x, d_heads, mlp_rows, *kept)
    return res[:ng], res[ng], res[ng + 1]
CHUNK = 512


def mlp_kernel(steps, x, heads, g, gains, wo, wg, wu, wd, out, d_hidden, d_heads, rows_out, dg, du, dd, do, hidden, mixed, mixed_t, acc, d_mixed):
    step = pl.program_id(0)
    width = x.shape[1]
    gain = jnp.concatenate([gains[2:3], gains[3:4]], axis=1)

    @pl.when(step == 0)
    def _():
        h = x[...].astype(F32) + plain_dot(heads[...], wo[...])
        hidden[...] = h
        m = unit(h)[0] * gain
        mixed[...] = m.astype(BF16)
        mixed_t[...] = m.T.astype(BF16)
        acc[...] = h
        d_mixed[...] = jnp.zeros_like(d_mixed)

    m, grad = mixed[...], g[...]
    gate, upward = plain_dot(m, wg[...]), plain_dot(m, wu[...])
    s = jax.nn.sigmoid(gate)
    act = gate * s
    active = (act * upward).astype(BF16)
    acc[...] += plain_dot(active, wd[...])
    d_active = dot_t(grad, wd[...])
    dd[...] = t_dot(active, grad).astype(BF16)
    d_up = (d_active * act).astype(BF16)
    d_gate = (d_active * upward * (s + act * (1.0 - s))).astype(BF16)
    dg[...] = plain_dot(mixed_t[...], d_gate).astype(BF16)
    du[...] = plain_dot(mixed_t[...], d_up).astype(BF16)
    d_mixed[...] += dot_t(d_gate, wg[...]) + dot_t(d_up, wu[...])

    @pl.when(step == steps - 1)
    def _():
        out[...] = acc[...].astype(BF16)
        e, r = unit(hidden[...])
        d = d_mixed[...]
        d_gain = jnp.sum(d * e, axis=0, keepdims=True)
        d = d * gain
        d = g[...].astype(F32) + r * (d - e * jnp.mean(d * e, axis=-1, keepdims=True))
        d_hidden[...] = d
        low = d.astype(BF16)
        d_heads[...] = dot_t(low, wo[...]).astype(BF16)
        do[...] = t_dot(heads[...], low).astype(BF16)
        half = width // 2
        rows_out[...] = jnp.concatenate([jnp.zeros((2, half), F32), d_gain[:, :half], d_gain[:, half:], jnp.zeros((12, half), F32)], axis=0)


def mlp(x, heads, g, gains, wo, wg, wu, wd):
    rows, width = x.shape
    steps = wg.shape[1] // CHUNK
    whole = lambda a: pl.BlockSpec(a.shape, lambda i: (0,) * len(a.shape), pipeline_mode=pl.Buffered(1))
    fixed = lambda *s: pl.BlockSpec(s, lambda i: (0, 0))
    by_col = pl.BlockSpec((width, CHUNK), lambda i: (0, i))
    by_row = pl.BlockSpec((CHUNK, width), lambda i: (i, 0))
    out = shapes(((rows, width), BF16), ((rows, width), F32), (heads.shape, BF16), ((16, width // 2), F32),
                 (wg.shape, BF16), (wu.shape, BF16), (wd.shape, BF16), (wo.shape, BF16))
    return pl.pallas_call(
        functools.partial(mlp_kernel, steps), out_shape=out, grid=(steps,),
        in_specs=[whole(x), whole(heads), whole(g), whole(gains), whole(wo), by_col, by_col, by_row],
        out_specs=[fixed(rows, width), fixed(rows, width), fixed(*heads.shape), fixed(16, width // 2), by_col, by_col, by_row, fixed(*wo.shape)],
        scratch_shapes=[pltpu.VMEM((rows, width), F32), pltpu.VMEM((rows, width), BF16), pltpu.VMEM((width, rows), BF16),
                        pltpu.VMEM((rows, width), F32), pltpu.VMEM((rows, width), F32)],
        compiler_params=pltpu.CompilerParams(vmem_limit_bytes=56 << 20), name="mlp")(x, heads, g, gains, wo, wg, wu, wd)
def root_mean_norm(rows, scaling):
    return rows * lax.rsqrt(jnp.mean(rows * rows, axis=-1, keepdims=True) + EPSILON) * scaling


def tables(length):
    freqs = THETA ** (-np.arange(HEAD // 2, dtype=np.float64) * 2.0 / HEAD)
    angles = np.arange(length, dtype=np.float64)[:, None] * np.concatenate([freqs, freqs])[None, :]
    return jnp.asarray(np.cos(angles), F32), jnp.asarray(np.sin(angles), F32)


def placed(values, f):
    return jnp.where(jnp.arange(16)[:, None] == f, values[None, :], jnp.zeros((), BF16)).reshape(-1)


def body(inputs, doc_ids, query_proj, key_projection, value_projection, output_proj, gate_proj, up_proj, down_proj,
         attn_gain, mlp_gain, query_norm_gain, key_gain, out_grad):
    f, c = lax.axis_index("fsdp"), lax.axis_index("ctx")
    rows, width = inputs.shape[1:]
    depth = query_proj.shape[0]
    cols = 4 * HEAD
    own = jnp.concatenate([
        lax.dynamic_slice_in_dim(query_proj, c * 2 * HEAD, 2 * HEAD, 1),
        lax.dynamic_slice_in_dim(key_projection, c * HEAD, HEAD, 1),
        lax.dynamic_slice_in_dim(value_projection, c * HEAD, HEAD, 1)], axis=1)
    small = jnp.concatenate([
        placed(attn_gain, f), placed(mlp_gain, f), placed(query_norm_gain, f), placed(key_gain, f),
        jnp.zeros((16 * cols - 2 * width - 2 * HEAD,), BF16)]).reshape(16, cols)
    pack = jnp.concatenate([own, small], axis=0)
    sequence = jnp.concatenate([inputs[0], jnp.broadcast_to(doc_ids[0].astype(BF16)[:, None], (rows, HEAD))], axis=1)
    (full_output, full_gate, full_up, full_down), x, own_heads, kept = forward(
        [pack, output_proj, gate_proj, up_proj, down_proj], sequence, *tables(8 * rows))
    gains = kept[1]
    residual = inputs[0].astype(F32)
    outputs, d_hidden, d_heads, mlp_rows, *grads = mlp(
        inputs[0], own_heads, out_grad[0], gains, full_output, full_gate, full_up, full_down)
    (gate_g, up_g, down_g, output_g), back, d_normed = backward(grads, x, d_heads, mlp_rows, kept)
    _, norm_pull = jax.vjp(lambda r: root_mean_norm(r, gains[0:2].reshape(width)), residual)
    input_grad = d_hidden + norm_pull(d_normed)[0]
    back = back.astype(F32)
    query_g = jnp.moveaxis(back[:, :depth, :2 * HEAD], 0, 1).reshape(depth, -1)
    key_g = jnp.moveaxis(back[:, :depth, 2 * HEAD:3 * HEAD], 0, 1).reshape(depth, -1)
    value_g = jnp.moveaxis(back[:, :depth, 3 * HEAD:], 0, 1).reshape(depth, -1)
    small_g = jnp.sum(back[:, depth:, :], axis=0)

    def mine(values, size):
        return lax.dynamic_slice_in_dim(values, f * size, size)

    return (outputs[None], input_grad[None], query_g, key_g, value_g, output_g.astype(F32), gate_g.astype(F32),
            up_g.astype(F32), down_g.astype(F32), mine(small_g[0:2].reshape(width), depth), mine(small_g[2:4].reshape(width), depth),
            mine(small_g[4, :HEAD], HEAD // 16), mine(small_g[4, HEAD:2 * HEAD], HEAD // 16))


def solution(mesh):
    seq, weight, gain = P("fsdp", "ctx", None), P("fsdp", None), P("fsdp")
    in_specs = (seq, P("fsdp", "ctx")) + (weight,) * 7 + (gain,) * 4 + (seq,)
    out_specs = (seq, seq) + (weight,) * 7 + (gain,) * 4
    return jax.shard_map(body, mesh=mesh, in_specs=in_specs, out_specs=out_specs, check_vma=False)
```
